32 devices in a mesh: fsdp: 8 (over y, x, core), rep: 4 (over z).
Axes of the slice: x: 2, y: 2, z: 4, core: 2. Of those that a mesh axis runs over, the one named last changes fastest.
Arguments:
- tokens: bfloat16 [8192, 2048], P(('fsdp', 'rep')), may hold values from -6 to 6
- block_lengths: int32 [64], P(('fsdp', 'rep')), may hold values from 0 to 256, as said below
- w_query: bfloat16 [2048, 2048], P(('fsdp', 'rep')), may hold values from -0.125 to 0.125
- w_key: bfloat16 [2048, 2048], P(('fsdp', 'rep')), may hold values from -0.125 to 0.125
- w_value: bfloat16 [2048, 2048], P(('fsdp', 'rep')), may hold values from -0.125 to 0.125
- w_out: bfloat16 [2048, 2048], P(('fsdp', 'rep')), may hold values from -0.125 to 0.125
- w_gate: bfloat16 [2048, 8192], P(('fsdp', 'rep')), may hold values from -0.125 to 0.125
- w_up: bfloat16 [2048, 8192], P(('fsdp', 'rep')), may hold values from -0.125 to 0.125
- w_down: bfloat16 [8192, 2048], P(('fsdp', 'rep')), may hold values from -0.0625 to 0.0625
- query_gain: bfloat16 [2048], P(('fsdp', 'rep')), may hold values from 0.099609375 to 1.8984375
- key_gain: bfloat16 [2048], P(('fsdp', 'rep')), may hold values from 0.099609375 to 1.8984375
- attn_gain: bfloat16 [2048], P(('fsdp', 'rep')), may hold values from 0.099609375 to 1.8984375
- mlp_gain: bfloat16 [2048], P(('fsdp', 'rep')), may hold values from 0.099609375 to 1.8984375
- cotangent: bfloat16 [8192, 2048], P(('fsdp', 'rep')), may hold values from -6 to 6
Outputs:
- block_out: bfloat16 [8192, 2048], P(('fsdp', 'rep'))
- grad_tokens: bfloat16 [8192, 2048], P(('fsdp', 'rep'))
- grad_w_query: float32 [2048, 2048], P(('fsdp', 'rep'))
- grad_w_key: float32 [2048, 2048], P(('fsdp', 'rep'))
- grad_w_value: float32 [2048, 2048], P(('fsdp', 'rep'))
- grad_w_out: float32 [2048, 2048], P(('fsdp', 'rep'))
- grad_w_gate: float32 [2048, 8192], P(('fsdp', 'rep'))
- grad_w_up: float32 [2048, 8192], P(('fsdp', 'rep'))
- grad_w_down: float32 [8192, 2048], P(('fsdp', 'rep'))
- grad_query_gain: float32 [2048], P(('fsdp', 'rep'))
- grad_key_gain: float32 [2048], P(('fsdp', 'rep'))
- grad_attn_gain: float32 [2048], P(('fsdp', 'rep'))
- grad_mlp_gain: float32 [2048], P(('fsdp', 'rep'))
The draws below stay inside these ranges and needn't reach their ends.
Inputs may be any that keep to these rules, and one draw needn't show every extreme that they name: `block_lengths`: entry b is the length of the sequence whose first token is the first row of block b, 0 where none starts there. A device's sequences lie in its own 2 blocks and never run into a block where another starts; every device holds one or more, and in every draw some device holds one of 256 tokens.
All inputs are finite; a program needn't handle non-finite values.
Results may differ from the reference program's by a relative error of at most 0.015.
Values may be sent and summed in bfloat16 or wider, within the bound.
No kernel may reach another device: no remote copies, remote signals or barrier semaphores. Data moves between devices by JAX's collectives and lax.ppermute only.
A program may use at most 768 MiB of HBM per device.

```python
import jax
import jax.numpy as jnp
from jax import lax

HEADS = 16
HEAD_DIM = 128
FF = 8192
BLOCK = 128
BLOCKS_DEV = 2
D = 2048
ROWS_DEV = 256
NBLOCKS = 64
TOKENS = 8192


def draw_block_lengths(key, part):
    key = jax.random.fold_in(key, 11)
    devs = NBLOCKS // 2
    keys = jax.random.split(key, 5)
    pattern = jax.random.randint(keys[0], (devs,), 0, 3)
    long_len = jax.random.randint(keys[1], (devs,), BLOCK + 1, 2 * BLOCK + 1)
    first = jax.random.randint(keys[2], (devs,), BLOCK // 4, BLOCK + 1)
    second = jax.random.randint(keys[3], (devs,), BLOCK // 4, BLOCK + 1)
    chosen = jax.random.randint(keys[4], (), 0, devs)
    index = jnp.arange(devs)
    pattern = jnp.where(index == chosen, 0, pattern)
    long_len = jnp.where(index == chosen, 2 * BLOCK, long_len)
    slot_first = jnp.where(pattern == 0, long_len, first)
    slot_second = jnp.where(pattern == 2, second, 0)
    return jnp.stack([slot_first, slot_second], axis=1).reshape(-1).astype(jnp.int32)


def block_levels(stream_key, extent, cuts, smallest, high):
    loudness = 1.0
    for dim, blocks in cuts:
        steps = jax.random.uniform(jax.random.fold_in(jax.random.fold_in(stream_key, 6), dim), (blocks,), jnp.float32, smallest / len(cuts), high / len(cuts))
        loudness = loudness * jnp.repeat(jnp.exp(steps), extent[dim] // blocks).reshape((-1,) + (1,) * (len(extent) - 1 - dim))
    return loudness


def gaussian(stream_key, dims, deviation, limit, pieces=(), kind=jnp.bfloat16):
    array = jax.random.normal(stream_key, dims, jnp.float32) * deviation
    if len(pieces) > 0:
        array = block_levels(stream_key, dims, pieces, -0.22, 0.18) * array
    return jnp.clip(array, min=-limit, max=limit).astype(kind)


def setup_inputs(seed: int = 0) -> dict:
    key_of = jax.random.split(jax.random.key(seed), 15)
    return {
        "tokens": gaussian(key_of[0], (TOKENS, D), 1.0, 6.0, ((0, 32),)),
        "block_lengths": draw_block_lengths(jax.random.fold_in(key_of[14], 71), 0),
        "w_query": gaussian(key_of[2], (D, D), D ** -0.5, 0.125, ((0, 32),)),
        "w_key": gaussian(key_of[3], (D, D), D ** -0.5, 0.125, ((0, 32),)),
        "w_value": gaussian(key_of[4], (D, D), D ** -0.5, 0.125, ((0, 32),)),
        "w_out": gaussian(key_of[5], (D, D), D ** -0.5, 0.125, ((0, 32),)),
        "w_gate": gaussian(key_of[6], (D, FF), D ** -0.5, 0.125, ((0, 32),)),
        "w_up": gaussian(key_of[7], (D, FF), D ** -0.5, 0.125, ((0, 32),)),
        "w_down": gaussian(key_of[8], (FF, D), FF ** -0.5, 0.0625, ((0, 32),)),
        "query_gain": jnp.clip(1.0 + 0.18 * jax.random.normal(key_of[9], (D,), jnp.float32), 0.099609375, 1.8984375).astype(jnp.bfloat16),
        "key_gain": jnp.clip(1.0 + 0.18 * jax.random.normal(key_of[10], (D,), jnp.float32), 0.099609375, 1.8984375).astype(jnp.bfloat16),
        "attn_gain": jnp.clip(1.0 + 0.18 * jax.random.normal(key_of[11], (D,), jnp.float32), 0.099609375, 1.8984375).astype(jnp.bfloat16),
        "mlp_gain": jnp.clip(1.0 + 0.18 * jax.random.normal(key_of[12], (D,), jnp.float32), 0.099609375, 1.8984375).astype(jnp.bfloat16),
        "cotangent": gaussian(key_of[13], (TOKENS, D), 1.0, 6.0, ((0, 32),)),
    }


@jax.custom_vjp
def low(v):
    return lax.optimization_barrier(v.astype(jnp.bfloat16)).astype(jnp.float32)

@jax.custom_vjp
def low_back(v):
    return v

def low_keep(v):
    return (low(v), None)

def low_pass(kept, grad):
    return (grad,)

def back_keep(v):
    return (v, None)

def back_low(kept, grad):
    return (low(grad),)
low.defvjp(low_keep, low_pass)
low_back.defvjp(back_keep, back_low)
epsilon = 1e-06
rope_base = 500000.0
highest = lax.Precision.HIGHEST

def product(left, right):
    return jnp.dot(left, right, precision=highest, preferred_element_type=jnp.float32)

def rms_scale(values, gain):
    return values * lax.rsqrt(lax.optimization_barrier(jnp.mean(values * values, axis=-1, keepdims=True)) + epsilon) * gain

def rotate(values, position, sign):
    half = HEAD_DIM // 2
    freq = rope_base ** (-jnp.arange(half, dtype=jnp.float32) / half)
    angle = sign * position.astype(jnp.float32)[:, None] * freq[None, :]
    cosine = jnp.cos(angle)[:, None, :]
    sine = jnp.sin(angle)[:, None, :]
    shaped = values.reshape(values.shape[0], HEADS, HEAD_DIM)
    first = shaped[..., :half]
    second = shaped[..., half:]
    turned = jnp.concatenate([first * cosine - second * sine, second * cosine + first * sine], axis=-1)
    return turned.reshape(values.shape)

def row_layout(lengths):
    nblock = lengths.shape[0]
    row_ids = jnp.arange(nblock * BLOCK, dtype=jnp.int32)
    begin = jnp.arange(nblock, dtype=jnp.int32) * BLOCK
    cover = (lengths[None, :] > 0) & (row_ids[:, None] >= begin[None, :]) & (row_ids[:, None] < begin[None, :] + lengths[None, :])
    live = jnp.any(cover, axis=1)
    owner = lax.optimization_barrier(jnp.sum(jnp.where(cover, begin[None, :], 0), axis=1)).astype(jnp.int32)
    position = row_ids - owner
    same = live[:, None] & live[None, :] & (owner[:, None] == owner[None, :]) & (row_ids[None, :] <= row_ids[:, None])
    allowed = same | (row_ids[:, None] == row_ids[None, :])
    return (live, position, allowed)

def attend(inputs):
    query_rot, key_rot, value_low, allowed = inputs
    scores = jnp.einsum('qhd,khd->hqk', query_rot, key_rot, precision=highest) * HEAD_DIM ** (-0.5)
    scores = low_back(scores)
    scores = jnp.where(allowed[None], scores, -1e+30)
    weights = low(jax.nn.softmax(scores, axis=-1))
    return jnp.einsum('hqk,khd->qhd', weights, value_low, precision=highest)

def layer(tokens, w_query, w_key, w_value, w_out, w_gate, w_up, w_down, query_gain, key_gain, attn_gain, mlp_gain, live, position, allowed):
    query_raw = low_back(product(tokens, w_query))
    key_raw = low_back(product(tokens, w_key))
    value_raw = low(low_back(product(tokens, w_value)))
    query_rot = low(rotate(rms_scale(query_raw, query_gain), position, 1.0))
    key_rot = low(rotate(rms_scale(key_raw, key_gain), position, 1.0))
    groups = TOKENS // ROWS_DEV
    grouped = (groups, ROWS_DEV, HEADS, HEAD_DIM)
    mixed = lax.map(jax.checkpoint(attend), (query_rot.reshape(grouped), key_rot.reshape(grouped), value_raw.reshape(grouped), allowed))
    mixed = low(low_back(mixed.reshape(TOKENS, HEADS * HEAD_DIM)))
    attn_proj = low_back(product(mixed, w_out))
    hidden = tokens + rms_scale(attn_proj, attn_gain)
    hidden_low = low(hidden)
    gate = low_back(product(hidden_low, w_gate))
    upward = low_back(product(hidden_low, w_up))
    inner = low(jax.nn.silu(gate) * upward)
    down = low_back(product(inner, w_down))
    return live[:, None] * (hidden + rms_scale(down, mlp_gain))

def reference(tokens, block_lengths, w_query, w_key, w_value, w_out, w_gate, w_up, w_down, query_gain, key_gain, attn_gain, mlp_gain, cotangent):
    live, position, allowed = jax.vmap(row_layout)(block_lengths.reshape(-1, BLOCKS_DEV))
    live = live.reshape(-1).astype(jnp.float32)
    position = position.reshape(-1)

    def forward(tokens_in, wq_in, wk_in, wv_in, wo_in, wg_in, wu_in, wd_in, gq_in, gk_in, ga_in, gm_in):
        return layer(tokens_in, wq_in, wk_in, wv_in, wo_in, wg_in, wu_in, wd_in, gq_in, gk_in, ga_in, gm_in, live, position, allowed)
    block_out, pullback = jax.vjp(forward, tokens.astype(jnp.float32), w_query.astype(jnp.float32), w_key.astype(jnp.float32), w_value.astype(jnp.float32), w_out.astype(jnp.float32), w_gate.astype(jnp.float32), w_up.astype(jnp.float32), w_down.astype(jnp.float32), query_gain.astype(jnp.float32), key_gain.astype(jnp.float32), attn_gain.astype(jnp.float32), mlp_gain.astype(jnp.float32))
    grads = pullback(cotangent.astype(jnp.float32))
    return (block_out.astype(jnp.bfloat16), grads[0].astype(jnp.bfloat16), grads[1], grads[2], grads[3], grads[4], grads[5], grads[6], grads[7], grads[8], grads[9], grads[10], grads[11])
```

```python
import jax
import jax.numpy as jnp
from jax import lax
from jax.sharding import Mesh, PartitionSpec as P

HEAD_DIM = 128
BLOCK = 128

epsilon = 1e-06
rope_base = 500000.0
f32 = jnp.float32
bf16 = jnp.bfloat16


def product(left, right):
    return jnp.dot(left, right, preferred_element_type=f32)


def product_tt(left, right):
    return lax.dot_general(left, right, (((1,), (1,)), ((), ())), preferred_element_type=f32)


def inner_rows(left, right):
    return lax.dot_general(left, right, (((0,), (0,)), ((), ())), preferred_element_type=f32)


def norm_forward(values, gain):
    inverse = lax.rsqrt(jnp.mean(values * values, axis=-1, keepdims=True) + epsilon)
    return (values * inverse * gain, inverse)


def norm_back(values, inverse, gain, incoming):
    normed = values * inverse
    scaled = incoming * gain
    gain_term = jnp.sum(incoming * normed, axis=0)
    back = inverse * (scaled - normed * jnp.mean(scaled * normed, axis=-1, keepdims=True))
    return (back, gain_term)


def angles(position):
    half = HEAD_DIM // 2
    freq = rope_base ** (-jnp.arange(half, dtype=f32) / half)
    angle = position.astype(f32)[..., None] * freq
    return jnp.cos(angle)[..., None, :], jnp.sin(angle)[..., None, :]


def rotate(values, cosine, sine):
    half = HEAD_DIM // 2
    first = values[..., :half]
    second = values[..., half:]
    return jnp.concatenate(
        [first * cosine - second * sine, second * cosine + first * sine], axis=-1
    )


def row_layout(lengths):
    nblock = lengths.shape[0]
    row_ids = jnp.arange(nblock * BLOCK, dtype=jnp.int32)
    begin = jnp.arange(nblock, dtype=jnp.int32) * BLOCK
    cover = (
        (lengths[None, :] > 0)
        & (row_ids[:, None] >= begin[None, :])
        & (row_ids[:, None] < begin[None, :] + lengths[None, :])
    )
    live = jnp.any(cover, axis=1)
    owner = jnp.sum(jnp.where(cover, begin[None, :], 0), axis=1)
    position = row_ids - owner
    same = (
        live[:, None]
        & live[None, :]
        & (owner[:, None] == owner[None, :])
        & (row_ids[None, :] <= row_ids[:, None])
    )
    allowed = same | (row_ids[:, None] == row_ids[None, :])
    return (live, position, allowed)


def swap(value, axis):
    return lax.ppermute(value, axis, ((0, 1), (1, 0)))


def pick(value, index, axis):
    return lax.dynamic_index_in_dim(value, index, axis, keepdims=False)


class Cube:
    every = ("y", "x", "c", "zh", "zl")
    team = ("zl", "x", "c")

    def __init__(self):
        self.y = lax.axis_index("y")
        self.zh = lax.axis_index("zh")
        self.size = 8
        self.index = lax.axis_index(self.team)

    def gather_lengths(self, lengths):
        for axis in ("x", "zl", "c"):
            lengths = jnp.stack([lengths, swap(lengths, axis)])
        return lengths.reshape(8, -1)

    def gather_rows(self, rows):
        half = rows.shape[0] // 2
        top, low = rows[:half], rows[half:]
        top_x, low_z = swap(top, "x"), swap(low, "zl")
        top_z, low_x = swap(top, "zl"), swap(low, "x")
        top_zx, low_zx = swap(top_x, "zl"), swap(low_z, "x")
        near = swap(rows, "c")
        middle = swap(jnp.concatenate([top_x, low_z]), "c")
        far = swap(jnp.concatenate([low_x, top_z, top_zx, low_zx]), "c")
        return jnp.concatenate(
            [
                rows, top_x, low_x, top_z, low_z, top_zx, low_zx,
                near, middle[:half], far[:half], far[half : 2 * half], middle[half:], far[2 * half :],
            ]
        )

    def scatter_rows(self, make):
        away = make(1).astype(bf16)
        mine = make(0)
        total = mine.astype(f32) + swap(away, "c").astype(f32)
        width = total.shape[1]
        total = total.reshape(2, 2, 2, -1, width)
        top, low = total[:, :, 0], total[:, :, 1]
        top = top[0] + swap(top[1].astype(bf16), "zl").astype(f32)
        low = low[:, 0] + swap(low[:, 1].astype(bf16), "x").astype(f32)
        top = top[0] + swap(top[1].astype(bf16), "x").astype(f32)
        low = low[0] + swap(low[1].astype(bf16), "zl").astype(f32)
        return jnp.concatenate([top, low])

    def split_rows(self, rows):
        half = rows.shape[0] // 2
        return rows[:half], rows[half:]

    def sum_rows(self, rows):
        shape = rows.shape
        rows = rows.reshape((2, 2, 2, -1) + shape[1:])
        for dim, axis in enumerate(("c", "zl", "x")):
            rows = rows + jnp.flip(swap(rows, axis), dim)
        return rows.reshape(shape)

    def order(self, mine, other, index, axis):
        first = index == 0
        return jnp.stack([jnp.where(first, mine, other), jnp.where(first, other, mine)], axis)

    def gather_group(self, block, axis_zh, axis_y):
        zh_block = swap(block, "zh")
        y_block, both_block = swap(block, "y"), swap(zh_block, "y")
        mine = self.order(block, zh_block, self.zh, axis_zh)
        other = self.order(y_block, both_block, self.zh, axis_zh)
        return self.order(mine, other, self.y, axis_y)

    def scatter_group(self, terms, axis_y, axis_zh):
        away = pick(terms, 1 - self.y, axis_y)
        mine = pick(terms, self.y, axis_y)
        total = mine.astype(f32) + swap(away, "y").astype(f32)
        away = pick(total, 1 - self.zh, axis_zh).astype(bf16)
        mine = pick(total, self.zh, axis_zh)
        return mine + swap(away, "zh").astype(f32)

    def team_columns(self, weight):
        rows = weight.shape[0]
        return weight.reshape(rows, 8, -1).transpose(1, 0, 2)

    def team_hidden(self, weight):
        rows = weight.shape[0]
        parts = weight.reshape(rows, 2, 2, 2, 2, 2, -1)
        return parts.transpose(5, 2, 3, 0, 4, 1, 6).reshape(8, rows, -1)

    def whole_columns(self, parts):
        return parts.transpose(1, 0, 2).reshape(parts.shape[1], -1)

    def whole_hidden(self, parts):
        rows = parts.shape[1]
        parts = parts.reshape(2, 2, 2, rows, 2, 2, -1)
        return parts.transpose(3, 5, 1, 2, 4, 0, 6).reshape(rows, -1)

    def gather_columns(self, parts):
        rows, width = parts.shape[1:]
        block = lax.all_to_all(parts, self.team, 0, 0)
        block = block.reshape(2, 2, 2, rows, width).transpose(1, 2, 0, 3, 4)
        return self.gather_group(block, 2, 0).reshape(-1, width)

    def scatter_columns(self, terms):
        width = terms.shape[1]
        terms = terms.reshape(2, 2, 2, 2, 2, -1, width)
        block = self.scatter_group(terms, 0, 2).astype(bf16)
        block = block.transpose(2, 0, 1, 3, 4).reshape(8, -1, width)
        return lax.all_to_all(block, self.team, 0, 0)

    def gather_down(self, weight):
        return self.gather_group(weight, 0, 1).reshape(-1, weight.shape[1])

    def scatter_down(self, terms):
        width = terms.shape[1]
        return self.scatter_group(terms.reshape(2, 2, -1, width), 1, 0)

    def turn(self, value):
        return lax.ppermute(value, ("y", "zl"), ((0, 0), (1, 2), (2, 1), (3, 3)))

    def gather_out(self, weight):
        return self.gather_down(self.turn(weight))

    def scatter_out(self, terms):
        return self.turn(self.scatter_down(terms).astype(bf16)).astype(f32)


class Plain:
    def __init__(self, team, group):
        self.team, self.group = team, group
        self.every = (team, group)
        self.size = lax.axis_size(team)
        self.groups = lax.axis_size(group)
        self.index = lax.axis_index(team)

    def gather_lengths(self, lengths):
        return lax.all_gather(lengths, self.team)

    def gather_rows(self, rows):
        return lax.all_gather(rows, self.team, axis=0, tiled=True)

    def scatter_rows(self, make):
        terms = jnp.concatenate([make(0), make(1)]).astype(bf16)
        return lax.psum_scatter(terms, self.team, scatter_dimension=0, tiled=True).astype(f32)

    def split_rows(self, rows):
        half = rows.shape[0] // 2
        return rows[:half], rows[half:]

    def sum_rows(self, rows):
        return lax.psum(rows, self.team)

    def team_columns(self, weight):
        rows = weight.shape[0]
        return weight.reshape(rows, self.size, -1).transpose(1, 0, 2)

    team_hidden = team_columns

    def whole_columns(self, parts):
        return parts.transpose(1, 0, 2).reshape(parts.shape[1], -1)

    whole_hidden = whole_columns

    def gather_columns(self, parts):
        width = parts.shape[2]
        block = lax.all_to_all(parts, self.team, 0, 0)
        return lax.all_gather(block, self.group, axis=1, tiled=True).reshape(-1, width)

    def scatter_columns(self, terms):
        width = terms.shape[1]
        terms = terms.reshape(self.size, -1, width)
        block = lax.psum_scatter(terms, self.group, scatter_dimension=1, tiled=True)
        return lax.all_to_all(block, self.team, 0, 0)

    def gather_down(self, weight):
        return lax.all_gather(weight, self.group, axis=0, tiled=True)

    def scatter_down(self, terms):
        return lax.psum_scatter(terms, self.group, scatter_dimension=0, tiled=True).astype(f32)

    gather_out = gather_down
    scatter_out = scatter_down


def local(
    make_plan,
    tokens,
    block_lengths,
    w_query,
    w_key,
    w_value,
    w_out,
    w_gate,
    w_up,
    w_down,
    query_gain,
    key_gain,
    attn_gain,
    mlp_gain,
    cotangent,
):
    plan = make_plan()
    nrows, width = tokens.shape
    size = plan.size
    columns = width // size
    heads = columns // HEAD_DIM
    score_scale = HEAD_DIM ** (-0.5)

    live = row_layout(block_lengths)[0]
    live_col = live.astype(f32)[:, None]
    lengths = plan.gather_lengths(block_lengths)
    _, position, allowed = jax.vmap(row_layout)(lengths)
    cosine, sine = angles(position)
    gains = lax.all_gather(
        jnp.stack([query_gain, key_gain, attn_gain, mlp_gain]), plan.every, axis=1, tiled=True
    ).astype(f32)
    query_gain_part = lax.dynamic_slice_in_dim(gains[0], plan.index * columns, columns)
    key_gain_part = lax.dynamic_slice_in_dim(gains[1], plan.index * columns, columns)
    attn_gain_wide, mlp_gain_wide = gains[2], gains[3]

    attn_parts = jnp.concatenate([plan.team_columns(w) for w in (w_query, w_key, w_value)], axis=2)
    attn_whole = plan.gather_columns(attn_parts)
    out_whole = plan.gather_out(w_out)
    mlp_parts = jnp.concatenate([plan.team_hidden(w) for w in (w_gate, w_up)], axis=2)
    mlp_whole = plan.gather_columns(mlp_parts)
    down_whole = plan.gather_down(w_down)
    hidden_columns = mlp_whole.shape[1] // 2

    team_tokens = plan.gather_rows(tokens)
    raw = product(team_tokens, attn_whole)
    query_raw, key_raw = raw[:, :columns], raw[:, columns : 2 * columns]
    value_low = raw[:, 2 * columns :].astype(bf16)
    squares = jnp.stack(
        [jnp.sum(query_raw * query_raw, axis=-1), jnp.sum(key_raw * key_raw, axis=-1)], axis=-1
    )
    inverse = lax.rsqrt(plan.sum_rows(squares) / width + epsilon)
    query_inverse, key_inverse = inverse[:, :1], inverse[:, 1:]
    head_shape = (size, nrows, heads, HEAD_DIM)
    query_normed = query_raw * query_inverse
    key_normed = key_raw * key_inverse
    query_rot = rotate((query_normed * query_gain_part).reshape(head_shape), cosine, sine)
    key_rot = rotate((key_normed * key_gain_part).reshape(head_shape), cosine, sine)
    query_rot, key_rot = query_rot.astype(bf16), key_rot.astype(bf16)
    value_low = value_low.reshape(head_shape)

    def dots(spec, left, right):
        return jnp.einsum(spec, left, right, preferred_element_type=f32)

    scores = dots("bqhd,bkhd->bhqk", query_rot, key_rot) * score_scale
    scores = jnp.where(allowed[:, None], scores, -1e30)
    probs = jax.nn.softmax(scores, axis=-1)
    probs_low = probs.astype(bf16)
    mixed = dots("bhqk,bkhd->bqhd", probs_low, value_low)
    mixed_low = mixed.reshape(size * nrows, columns).astype(bf16)
    mixed_parts = plan.split_rows(mixed_low)
    attn_proj = plan.scatter_rows(lambda part: product(mixed_parts[part], out_whole))
    attn_normed, attn_inverse = norm_forward(attn_proj, attn_gain_wide)
    hidden = tokens.astype(f32) + attn_normed

    team_hidden = plan.gather_rows(hidden.astype(bf16))
    both = product(team_hidden, mlp_whole)
    gate, upward = both[:, :hidden_columns], both[:, hidden_columns:]
    sigmoid_gate = jax.nn.sigmoid(gate)
    activated = gate * sigmoid_gate
    inner_low = (activated * upward).astype(bf16)
    inner_parts = plan.split_rows(inner_low)
    down = plan.scatter_rows(lambda part: product(inner_parts[part], down_whole))
    down_normed, down_inverse = norm_forward(down, mlp_gain_wide)
    block_out = (live_col * (hidden + down_normed)).astype(bf16)

    grad_out = live_col * cotangent.astype(f32)
    grad_down, term_mlp_gain = norm_back(down, down_inverse, mlp_gain_wide, grad_out)
    team_grad_down = plan.gather_rows(grad_down.astype(bf16))
    grad_inner = product_tt(team_grad_down, down_whole)
    grad_gate = grad_inner * upward * sigmoid_gate * (1.0 + gate * (1.0 - sigmoid_gate))
    grad_up = grad_inner * activated
    grad_both = jnp.concatenate([grad_gate.astype(bf16), grad_up.astype(bf16)], axis=1)
    both_parts = plan.split_rows(grad_both)
    grad_hidden = grad_out + plan.scatter_rows(
        lambda part: product_tt(both_parts[part], mlp_whole)
    )
    grad_w_down = plan.scatter_down(inner_rows(inner_low, team_grad_down).astype(bf16))
    grad_w_mlp = plan.scatter_columns(inner_rows(team_hidden, grad_both).astype(bf16))
    grad_w_gate = plan.whole_hidden(grad_w_mlp[..., :hidden_columns]).astype(f32)
    grad_w_up = plan.whole_hidden(grad_w_mlp[..., hidden_columns:]).astype(f32)

    grad_proj, term_attn_gain = norm_back(attn_proj, attn_inverse, attn_gain_wide, grad_hidden)
    team_grad_proj = plan.gather_rows(grad_proj.astype(bf16))
    grad_mixed = product_tt(team_grad_proj, out_whole).astype(bf16).reshape(head_shape)
    grad_w_out = plan.scatter_out(inner_rows(mixed_low, team_grad_proj).astype(bf16))
    grad_probs = dots("bqhd,bkhd->bhqk", grad_mixed, value_low)
    grad_scores = probs * (grad_probs - jnp.sum(probs * grad_probs, axis=-1, keepdims=True))
    grad_scores = grad_scores.astype(bf16)
    grad_query_rot = dots("bhqk,bkhd->bqhd", grad_scores, key_rot) * score_scale
    grad_key_rot = dots("bhqk,bqhd->bkhd", grad_scores, query_rot) * score_scale
    grad_value = dots("bhqk,bqhd->bkhd", probs_low, grad_mixed).astype(bf16)
    flat = (size * nrows, columns)
    grad_query_turned = rotate(grad_query_rot, cosine, -sine).reshape(flat)
    grad_key_turned = rotate(grad_key_rot, cosine, -sine).reshape(flat)
    term_query_gain = jnp.sum(grad_query_turned * query_normed, axis=0)
    term_key_gain = jnp.sum(grad_key_turned * key_normed, axis=0)
    query_scaled = grad_query_turned * query_gain_part
    key_scaled = grad_key_turned * key_gain_part
    means = jnp.stack(
        [jnp.sum(query_scaled * query_normed, axis=-1), jnp.sum(key_scaled * key_normed, axis=-1)],
        axis=-1,
    )
    means = plan.sum_rows(means) / width
    grad_query = query_inverse * (query_scaled - query_normed * means[:, :1])
    grad_key = key_inverse * (key_scaled - key_normed * means[:, 1:])
    grad_raw = jnp.concatenate(
        [grad_query.astype(bf16), grad_key.astype(bf16), grad_value.reshape(flat)], axis=1
    )
    raw_parts = plan.split_rows(grad_raw)
    grad_w_attn = plan.scatter_columns(inner_rows(team_tokens, grad_raw).astype(bf16))
    grad_tokens = grad_hidden + plan.scatter_rows(
        lambda part: product_tt(raw_parts[part], attn_whole)
    )
    grad_w_query, grad_w_key, grad_w_value = (
        plan.whole_columns(grad_w_attn[..., k * columns : (k + 1) * columns]).astype(f32)
        for k in range(3)
    )

    blank = jnp.zeros((width,), f32)
    place = plan.index * columns
    terms = jnp.stack(
        [
            lax.dynamic_update_slice_in_dim(blank, term_query_gain, place, 0),
            lax.dynamic_update_slice_in_dim(blank, term_key_gain, place, 0),
            term_attn_gain,
            term_mlp_gain,
        ]
    )
    gain_grads = lax.psum_scatter(terms, plan.every, scatter_dimension=1, tiled=True)
    return (
        block_out,
        grad_tokens.astype(bf16),
        grad_w_query,
        grad_w_key,
        grad_w_value,
        grad_w_out,
        grad_w_gate,
        grad_w_up,
        grad_w_down,
        gain_grads[0],
        gain_grads[1],
        gain_grads[2],
        gain_grads[3],
    )


def solution(mesh):
    if tuple(mesh.shape.values()) == (8, 4):
        mesh = Mesh(mesh.devices.reshape(2, 2, 2, 2, 2), Cube.every)
        every, make_plan = Cube.every, Cube
    else:
        every = tuple(mesh.axis_names)

        def make_plan():
            return Plain(*every)

    def step(*arrays):
        return local(make_plan, *arrays)

    rows, line = P(every, None), P(every)
    return jax.shard_map(
        step,
        mesh=mesh,
        in_specs=(rows, line) + (rows,) * 7 + (line,) * 4 + (rows,),
        out_specs=(rows,) * 9 + (line,) * 4,
        check_vma=False,
    )
```

```python
import functools

import jax
import jax.numpy as jnp
from jax import lax
from jax.experimental import pallas as pl
from jax.experimental.pallas import tpu as pltpu
from jax.sharding import Mesh, PartitionSpec as P

HEAD_DIM = 128
BLOCK = 128

epsilon = 1e-06
rope_base = 500000.0
f32 = jnp.float32
bf16 = jnp.bfloat16
NO_COST = pl.CostEstimate(flops=0, bytes_accessed=0, transcendentals=0)


def product(left, right):
    return jnp.dot(left, right, preferred_element_type=f32)


def product_tt(left, right):
    return lax.dot_general(left, right, (((1,), (1,)), ((), ())), preferred_element_type=f32)


def inner_rows(left, right):
    return lax.dot_general(left, right, (((0,), (0,)), ((), ())), preferred_element_type=f32)


def norm_forward(values, gain):
    inverse = lax.rsqrt(jnp.mean(values * values, axis=-1, keepdims=True) + epsilon)
    return (values * inverse * gain, inverse)


def norm_back(values, inverse, gain, incoming):
    normed = values * inverse
    scaled = incoming * gain
    gain_term = jnp.sum(incoming * normed, axis=0)
    back = inverse * (scaled - normed * jnp.mean(scaled * normed, axis=-1, keepdims=True))
    return (back, gain_term)


def angles(position):
    half = HEAD_DIM // 2
    freq = rope_base ** (-jnp.arange(half, dtype=f32) / half)
    angle = position.astype(f32).reshape(-1, 1) * freq
    cosine, sine = jnp.cos(angle), jnp.sin(angle)
    return jnp.concatenate([cosine, cosine], axis=1), jnp.concatenate([-sine, sine], axis=1)


def row_layout(lengths):
    nblock = lengths.shape[0]
    row_ids = jnp.arange(nblock * BLOCK, dtype=jnp.int32)
    begin = jnp.arange(nblock, dtype=jnp.int32) * BLOCK
    cover = (
        (lengths[None, :] > 0)
        & (row_ids[:, None] >= begin[None, :])
        & (row_ids[:, None] < begin[None, :] + lengths[None, :])
    )
    live = jnp.any(cover, axis=1)
    owner = jnp.sum(jnp.where(cover, begin[None, :], 0), axis=1)
    return (live, row_ids - owner)


def allowed_keys(lengths_ref, device, nrows):
    rows = lax.broadcasted_iota(jnp.int32, (nrows, nrows), 0)
    keys = lax.broadcasted_iota(jnp.int32, (nrows, nrows), 1)

    def number(ids):
        found = -1 - ids
        for block in range(nrows // BLOCK):
            begin, length = block * BLOCK, lengths_ref[device, block]
            found = jnp.where((ids >= begin) & (ids < begin + length), begin, found)
        return found

    return (number(rows) == number(keys)) & (keys <= rows)


def turn(values, cosine, sine):
    return values * cosine + pltpu.roll(values, HEAD_DIM // 2, 1) * sine


def probabilities(query, key, allowed):
    scores = product_tt(query, key) * HEAD_DIM ** (-0.5)
    scores = jnp.where(allowed, scores, -1e30)
    powers = jnp.exp(scores - jnp.max(scores, axis=-1, keepdims=True))
    return powers / jnp.sum(powers, axis=-1, keepdims=True)


def attend_kernel(
    lengths_ref, raw_ref, inverse_ref, gains_ref, cosine_ref, sine_ref, turned_ref, mixed_ref
):
    nrows, columns = mixed_ref.shape
    allowed = allowed_keys(lengths_ref, pl.program_id(0), nrows)
    cosine, sine = cosine_ref[...], sine_ref[...]
    for head in range(columns // HEAD_DIM):
        here = slice(head * HEAD_DIM, (head + 1) * HEAD_DIM)
        turned = []
        for which in range(2):
            there = slice(which * columns + here.start, which * columns + here.stop)
            normed = raw_ref[:, there] * inverse_ref[:, which : which + 1]
            rotated = turn(normed * gains_ref[which : which + 1, here], cosine, sine).astype(bf16)
            turned_ref[:, there] = rotated
            turned.append(rotated)
        there = slice(2 * columns + here.start, 2 * columns + here.stop)
        value = raw_ref[:, there].astype(bf16)
        turned_ref[:, there] = value
        probs = probabilities(turned[0], turned[1], allowed)
        mixed_ref[:, here] = product(probs.astype(bf16), value).astype(bf16)


def attend_back_kernel(
    lengths_ref, raw_ref, turned_ref, inverse_ref, gains_ref, cosine_ref, sine_ref, grad_ref,
    scaled_ref, grad_value_ref, means_ref, terms_ref,
):
    nrows, columns = grad_ref.shape
    device = pl.program_id(0)
    allowed = allowed_keys(lengths_ref, device, nrows)
    cosine, sine = cosine_ref[...], sine_ref[...]

    @pl.when(device == 0)
    def _():
        terms_ref[...] = jnp.zeros_like(terms_ref)

    sums = [0.0, 0.0]
    for head in range(columns // HEAD_DIM):
        here = slice(head * HEAD_DIM, (head + 1) * HEAD_DIM)
        spots = [slice(k * columns + here.start, k * columns + here.stop) for k in range(3)]
        query, key, value = (turned_ref[:, spot] for spot in spots)
        incoming = grad_ref[:, here]
        probs = probabilities(query, key, allowed)
        grad_probs = product_tt(incoming, value)
        inner = jnp.sum(probs * grad_probs, axis=-1, keepdims=True)
        grad_scores = (probs * (grad_probs - inner)).astype(bf16)
        grad_value_ref[:, here] = inner_rows(probs.astype(bf16), incoming).astype(bf16)
        back = (product(grad_scores, key), inner_rows(grad_scores, query))
        for which in range(2):
            turned = turn(back[which] * HEAD_DIM ** (-0.5), cosine, -sine)
            normed = raw_ref[:, spots[which]] * inverse_ref[:, which : which + 1]
            terms_ref[which : which + 1, here] += jnp.sum(turned * normed, axis=0, keepdims=True)
            scaled = turned * gains_ref[which : which + 1, here]
            scaled_ref[:, spots[which]] = scaled
            sums[which] = sums[which] + jnp.sum(scaled * normed, axis=-1, keepdims=True)
    means_ref[...] = jnp.concatenate(sums, axis=1)


def attend_specs(nrows, columns):
    def rows(wide):
        return pl.BlockSpec((nrows, wide), lambda b: (b, 0))

    lengths = pl.BlockSpec(memory_space=pltpu.SMEM)
    gains = pl.BlockSpec((2, columns), lambda b: (0, 0))
    return rows, lengths, gains


def attend(lengths, raw, inverse, gains, cosine, sine):
    size, nrows = lengths.shape[0], raw.shape[0] // lengths.shape[0]
    columns = raw.shape[1] // 3
    rows, whole, gain = attend_specs(nrows, columns)
    return pl.pallas_call(
        attend_kernel,
        grid=(size,),
        in_specs=[whole, rows(3 * columns), rows(2), gain, rows(HEAD_DIM), rows(HEAD_DIM)],
        out_specs=[rows(3 * columns), rows(columns)],
        out_shape=[
            jax.ShapeDtypeStruct(raw.shape, bf16),
            jax.ShapeDtypeStruct((raw.shape[0], columns), bf16),
        ],
        cost_estimate=NO_COST,
    )(lengths, raw, inverse, gains, cosine, sine)


def attend_back(lengths, raw, turned, inverse, gains, cosine, sine, grad):
    size, nrows = lengths.shape[0], raw.shape[0] // lengths.shape[0]
    columns = raw.shape[1] // 3
    rows, whole, gain = attend_specs(nrows, columns)
    return pl.pallas_call(
        attend_back_kernel,
        grid=(size,),
        in_specs=[
            whole, rows(3 * columns), rows(3 * columns), rows(2), gain,
            rows(HEAD_DIM), rows(HEAD_DIM), rows(columns),
        ],
        out_specs=[rows(2 * columns), rows(columns), rows(2), gain],
        out_shape=[
            jax.ShapeDtypeStruct((raw.shape[0], 2 * columns), f32),
            jax.ShapeDtypeStruct((raw.shape[0], columns), bf16),
            jax.ShapeDtypeStruct((raw.shape[0], 2), f32),
            jax.ShapeDtypeStruct((2, columns), f32),
        ],
        cost_estimate=NO_COST,
    )(lengths, raw, turned, inverse, gains, cosine, sine, grad)


def swap(value, axis):
    return lax.ppermute(value, axis, ((0, 1), (1, 0)))


def sync(*values):
    return lax.optimization_barrier(values)


def pick(value, index, axis):
    return lax.dynamic_index_in_dim(value, index, axis, keepdims=False)


def join_kernel(table_ref, *refs):
    pieces, out, held, sems = refs[:-3], refs[-3], refs[-2], refs[-1]
    loads, stores = [], []
    for k, piece in enumerate(pieces):
        here = pl.ds(pl.multiple_of(table_ref[k] * 64, 64), piece.shape[0])
        loads.append(pltpu.make_async_copy(piece, held.at[here], sems.at[0, k]))
        stores.append(pltpu.make_async_copy(held.at[here], out.at[here], sems.at[1, k]))
        loads[-1].start()
    for load, store in zip(loads, stores):
        load.wait()
        store.start()
    for store in stores:
        store.wait()


def join(*pieces, table=None):
    if table is None:
        begins = [sum(piece.shape[0] for piece in pieces[:k]) // 64 for k in range(len(pieces))]
        table = jnp.array(begins, jnp.int32)
    shape = (sum(piece.shape[0] for piece in pieces), pieces[0].shape[1])
    return pl.pallas_call(
        join_kernel,
        in_specs=[pl.BlockSpec(memory_space=pltpu.SMEM)]
        + [pl.BlockSpec(memory_space=pl.ANY)] * len(pieces),
        out_specs=pl.BlockSpec(memory_space=pl.ANY),
        out_shape=jax.ShapeDtypeStruct(shape, pieces[0].dtype),
        scratch_shapes=[
            pltpu.VMEM(shape, pieces[0].dtype),
            pltpu.SemaphoreType.DMA((2, len(pieces))),
        ],
        compiler_params=pltpu.CompilerParams(vmem_limit_bytes=32 * 2**20),
        cost_estimate=NO_COST,
    )(table, *pieces)


def regroup_kernel(halves, in_ref, out_ref):
    for tile in range(len(halves) // 2):
        parts = [in_ref[:, half * 64 : (half + 1) * 64] for half in halves[2 * tile : 2 * tile + 2]]
        out_ref[:, tile * 128 : (tile + 1) * 128] = jnp.concatenate(parts, axis=1)


def regroup(value, halves):
    rows, width = value.shape
    block = pl.BlockSpec((rows // 2, width), lambda k: (k, 0))
    return pl.pallas_call(
        functools.partial(regroup_kernel, halves),
        grid=(2,),
        in_specs=[block],
        out_specs=block,
        out_shape=jax.ShapeDtypeStruct(value.shape, value.dtype),
        cost_estimate=NO_COST,
    )(value)


def spread_kernel(order, parts_ref, out_ref):
    wide = out_ref.shape[1] // len(order)
    for block, (part, column) in enumerate(order):
        here = slice(block * wide, (block + 1) * wide)
        out_ref[:, here] = parts_ref[part, :, column * wide : (column + 1) * wide].astype(f32)


def spread(parts, order):
    shape = (parts.shape[1], parts.shape[0] * parts.shape[2])
    return pl.pallas_call(
        functools.partial(spread_kernel, order),
        in_specs=[pl.BlockSpec(memory_space=pltpu.VMEM)],
        out_specs=pl.BlockSpec(memory_space=pltpu.VMEM),
        out_shape=jax.ShapeDtypeStruct(shape, f32),
        cost_estimate=NO_COST,
    )(parts)


class Cube:
    every = ("y", "x", "c", "zh", "zl")
    team = ("y", "x")
    z_axes = ("zh", "zl")
    group = ("c", "zh", "zl")

    def __init__(self):
        self.place = [lax.axis_index(axis) for axis in self.every]
        self.core = self.place[2]
        self.z = lax.axis_index(self.z_axes)
        self.size = 4
        self.index = lax.axis_index(self.team)

    def shift(self, value):
        return lax.ppermute(value, self.z_axes, ((0, 1), (1, 2), (2, 3), (3, 0)))

    def rows_first(self, rows):
        half = rows.shape[0] // 2
        top, low = rows[:half], rows[half:]
        return top, low, swap(top, "x"), swap(low, "y")

    def rows_second(self, top, low, top_x, low_y):
        top_y, low_x = swap(top, "y"), swap(low, "x")
        return top, low, top_x, low_x, top_y, low_y, swap(top_x, "y"), swap(low_y, "x")

    def terms_first(self, terms):
        terms = terms.reshape(2, 2, 2, -1, terms.shape[1])
        top, low = swap(terms[1, :, 0], "y"), swap(terms[:, 1, 1], "x")
        return terms[0, :, 0], terms[:, 0, 1], top, low

    def terms_second(self, top, low, top_y, low_x):
        top = top.astype(f32) + top_y.astype(f32)
        low = low.astype(f32) + low_x.astype(f32)
        return top[0], low[0], swap(top[1].astype(bf16), "x"), swap(low[1].astype(bf16), "y")

    def terms_sum(self, top, low, top_x, low_y):
        return jnp.concatenate([top + top_x.astype(f32), low + low_y.astype(f32)])

    def sum_rows(self, rows):
        shape = rows.shape
        rows = rows.reshape((2, 2, -1) + shape[1:])
        for dim, axis in enumerate(self.team):
            rows = rows + jnp.flip(swap(rows, axis), dim)
        return rows.reshape(shape)

    def order(self, mine, other, index, axis):
        first = index == 0
        return jnp.stack([jnp.where(first, mine, other), jnp.where(first, other, mine)], axis)

    def team_columns(self, weight):
        rows = weight.shape[0]
        return weight.reshape(rows, 4, -1).transpose(1, 0, 2)

    def whole_columns(self, parts):
        return spread(parts, [(part, 0) for part in range(4)])

    def send_columns(self, parts):
        return lax.all_to_all(parts, self.team, 0, 0).reshape(-1, parts.shape[2])

    def return_columns(self, block):
        return lax.all_to_all(block.reshape(4, -1, block.shape[1]), self.team, 0, 0)

    def grouped(self, rows):
        return regroup(rows, [spot * 8 + place for place in range(8) for spot in range(4)])

    def ungrouped(self, rows):
        return regroup(rows, [place * 4 + spot for spot in range(4) for place in range(8)])

    def join_group(self, blocks):
        table, pieces = [], []
        for core in range(2):
            for k in range(4):
                unit = blocks[core][k].shape[0] // 64
                table.append(((self.core ^ core) * 4 + (self.z - k) % 4) * unit)
                pieces.append(blocks[core][k])
        return join(*pieces, table=jnp.stack(table).astype(jnp.int32))

    def core_halves(self, values):
        half = values.shape[1] // 2
        return [
            lax.dynamic_slice_in_dim(values, index * half, half, 1)
            for index in (1 - self.core, self.core)
        ]

    def ring_part(self, terms, k):
        rows = terms.shape[0] // 4
        return lax.dynamic_slice_in_dim(terms, (self.z - k) % 4 * rows, rows, 0)

    def small_rows(self, gains, lengths, width):
        small = [jnp.pad(row.astype(bf16), (0, width - row.shape[0])) for row in (*gains, lengths)]
        return jnp.pad(jnp.stack(small), ((0, 16 - len(small)), (0, 0)))

    def small_step(self, small, axis):
        index = self.place[self.every.index(axis)]
        small = self.order(small, swap(small, axis), index, 1)
        return small.reshape(small.shape[0], -1, small.shape[-1])

    def small_end(self, small, count):
        gains = small[:4].reshape(4, -1).astype(f32)
        y, x, c, _, _ = self.place
        ids = [
            (((y ^ dy) * 2 + (x ^ dx)) * 2 + c) * 4 + self.z for dy in range(2) for dx in range(2)
        ]
        lengths = jnp.stack([pick(small[4], i, 0) for i in ids])[:, :count]
        return gains, lengths.astype(jnp.int32)

    def gain_step(self, terms, axis, dim):
        index = self.place[self.every.index(axis)]
        return pick(terms, index, dim) + swap(pick(terms, 1 - index, dim), axis)

    def own_gains(self, terms):
        terms = terms.reshape(terms.shape[0], 2, 2, 2, -1)
        for index in self.place[2:]:
            terms = pick(terms, index, 1)
        return terms


class Plain:
    def __init__(self, team, group):
        self.team, self.group = team, group
        self.every = (team, group)
        self.size = lax.axis_size(team)
        self.index = lax.axis_index(team)

    def gather_rows(self, rows):
        return lax.all_gather(rows, self.team, axis=0, tiled=True)

    def scatter_rows(self, terms):
        return lax.psum_scatter(terms, self.team, scatter_dimension=0, tiled=True).astype(f32)

    def sum_rows(self, rows):
        return lax.psum(rows, self.team)

    def gather_columns(self, weight):
        rows = weight.shape[0]
        parts = weight.reshape(rows, self.size, -1).transpose(1, 0, 2)
        block = lax.all_to_all(parts, self.team, 0, 0)
        whole = lax.all_gather(block, self.group, axis=1, tiled=True)
        return whole.reshape(-1, block.shape[2])

    def scatter_columns(self, terms):
        terms = terms.reshape(self.size, -1, terms.shape[1])
        block = lax.psum_scatter(terms, self.group, scatter_dimension=1, tiled=True)
        parts = lax.all_to_all(block, self.team, 0, 0)
        return parts.transpose(1, 0, 2).reshape(parts.shape[1], -1).astype(f32)

    def gather_group(self, weight):
        return lax.all_gather(weight, self.group, axis=0, tiled=True)

    def scatter_group(self, terms, axis=0):
        block = lax.psum_scatter(terms, self.group, scatter_dimension=axis, tiled=True)
        return block.astype(f32)


def norm_columns(raw, columns):
    parts = [raw[:, k * columns : (k + 1) * columns] for k in (0, 1)]
    return jnp.stack([jnp.sum(part * part, axis=-1) for part in parts], axis=-1)


def raw_back(raw, scaled, inverse, means, grad_value):
    columns = grad_value.shape[1]
    grads = []
    for which in (0, 1):
        here = slice(which * columns, (which + 1) * columns)
        scale = inverse[:, which : which + 1]
        normed = raw[:, here] * scale
        grad = scale * (scaled[:, here] - normed * means[:, which : which + 1])
        grads.append(grad.astype(bf16))
    return jnp.concatenate(grads + [grad_value], axis=1)


def local_plain(
    plan,
    tokens,
    block_lengths,
    w_query,
    w_key,
    w_value,
    w_out,
    w_gate,
    w_up,
    w_down,
    query_gain,
    key_gain,
    attn_gain,
    mlp_gain,
    cotangent,
):
    width = tokens.shape[1]
    columns = width // plan.size
    live, _ = row_layout(block_lengths)
    live_col = live.astype(f32)[:, None]
    lengths = lax.all_gather(block_lengths, plan.team)
    _, position = jax.vmap(row_layout)(lengths)
    cosine, sine = angles(position)
    gains = jnp.stack([query_gain, key_gain, attn_gain, mlp_gain])
    gains = lax.all_gather(gains, plan.every, axis=1, tiled=True).astype(f32)
    part_gains = lax.dynamic_slice_in_dim(gains[:2], plan.index * columns, columns, axis=1)
    attn_gain_wide, mlp_gain_wide = gains[2], gains[3]
    attn_whole = jnp.concatenate(
        [plan.gather_columns(w) for w in (w_query, w_key, w_value)], axis=1
    )
    out_whole = plan.gather_group(w_out)
    gate_whole = plan.gather_columns(w_gate)
    up_whole = plan.gather_columns(w_up)
    down_whole = plan.gather_group(w_down)

    team_tokens = plan.gather_rows(tokens)
    raw = product(team_tokens, attn_whole)
    inverse = lax.rsqrt(plan.sum_rows(norm_columns(raw, columns)) / width + epsilon)
    turned, mixed_low = attend(lengths, raw, inverse, part_gains, cosine, sine)
    attn_proj = plan.scatter_rows(product(mixed_low, out_whole).astype(bf16))
    attn_normed, attn_inverse = norm_forward(attn_proj, attn_gain_wide)
    hidden = tokens.astype(f32) + attn_normed
    team_hidden = plan.gather_rows(hidden.astype(bf16))
    gate = product(team_hidden, gate_whole)
    upward = product(team_hidden, up_whole)
    sigmoid_gate = jax.nn.sigmoid(gate)
    activated = gate * sigmoid_gate
    inner_low = (activated * upward).astype(bf16)
    down = plan.scatter_rows(product(inner_low, down_whole).astype(bf16))
    down_normed, down_inverse = norm_forward(down, mlp_gain_wide)
    block_out = (live_col * (hidden + down_normed)).astype(bf16)

    grad_out = live_col * cotangent.astype(f32)
    grad_down, term_mlp_gain = norm_back(down, down_inverse, mlp_gain_wide, grad_out)
    team_grad_down = plan.gather_rows(grad_down.astype(bf16))
    grad_w_down = plan.scatter_group(inner_rows(inner_low, team_grad_down).astype(bf16))
    grad_inner = product_tt(team_grad_down, down_whole)
    grad_gate = grad_inner * upward * sigmoid_gate * (1.0 + gate * (1.0 - sigmoid_gate))
    grad_up = grad_inner * activated
    grad_gate, grad_up = grad_gate.astype(bf16), grad_up.astype(bf16)
    grad_w_gate = plan.scatter_columns(inner_rows(team_hidden, grad_gate).astype(bf16))
    grad_w_up = plan.scatter_columns(inner_rows(team_hidden, grad_up).astype(bf16))
    grad_from_mlp = product_tt(grad_gate, gate_whole) + product_tt(grad_up, up_whole)
    grad_hidden = grad_out + plan.scatter_rows(grad_from_mlp.astype(bf16))

    grad_proj, term_attn_gain = norm_back(attn_proj, attn_inverse, attn_gain_wide, grad_hidden)
    team_grad_proj = plan.gather_rows(grad_proj.astype(bf16))
    grad_mixed = product_tt(team_grad_proj, out_whole).astype(bf16)
    grad_w_out = plan.scatter_group(inner_rows(mixed_low, team_grad_proj).astype(bf16))
    scaled, grad_value, means, part_terms = attend_back(
        lengths, raw, turned, inverse, part_gains, cosine, sine, grad_mixed
    )
    means = plan.sum_rows(means) / width
    grad_raw = raw_back(raw, scaled, inverse, means, grad_value)
    grad_w_query, grad_w_key, grad_w_value = (
        plan.scatter_columns(
            inner_rows(team_tokens, grad_raw[:, k * columns : (k + 1) * columns]).astype(bf16)
        )
        for k in range(3)
    )
    grad_from_attn = plan.scatter_rows(product_tt(grad_raw, attn_whole).astype(bf16))
    part_grads = plan.scatter_group(part_terms, 1)
    gain_grads = lax.psum_scatter(
        jnp.stack([term_attn_gain, term_mlp_gain]), plan.every, scatter_dimension=1, tiled=True
    )
    return (
        block_out,
        (grad_hidden + grad_from_attn).astype(bf16),
        grad_w_query,
        grad_w_key,
        grad_w_value,
        grad_w_out,
        grad_w_gate,
        grad_w_up,
        grad_w_down,
        part_grads[0],
        part_grads[1],
        gain_grads[0],
        gain_grads[1],
    )


def local_cube(
    tokens,
    block_lengths,
    w_query,
    w_key,
    w_value,
    w_out,
    w_gate,
    w_up,
    w_down,
    query_gain,
    key_gain,
    attn_gain,
    mlp_gain,
    cotangent,
):
    plan = Cube()
    width = tokens.shape[1]
    columns = width // plan.size
    live, _ = row_layout(block_lengths)
    live_col = live.astype(f32)[:, None]

    def group_whole(block):
        return lax.all_gather(block, plan.group, axis=0, tiled=True)

    shard = query_gain.shape[0]
    small = plan.small_rows((query_gain, key_gain, attn_gain, mlp_gain), block_lengths, width)
    packed = group_whole(jnp.concatenate([w_out, small])).reshape(8, -1, width)
    down1 = plan.shift(w_down)
    rows = plan.rows_first(plan.grouped(tokens))
    attn_parts = jnp.concatenate([plan.team_columns(w) for w in (w_query, w_key, w_value)], axis=2)
    attn0 = plan.send_columns(attn_parts)
    down1, attn0, w_gate, *rows = sync(down1, attn0, w_gate, *rows)
    attn1, attn0c = plan.shift(attn0), swap(attn0, "c")
    rows = plan.rows_second(*rows)
    attn1, attn0c, w_gate, *rows = sync(attn1, attn0c, w_gate, *rows)
    gate = plan.send_columns(plan.team_columns(w_gate))
    attn2, attn1c = plan.shift(attn1), swap(attn1, "c")
    team_tokens = join(*rows)
    attn2, attn1c, gate, w_up, team_tokens, packed = sync(
        attn2, attn1c, gate, w_up, team_tokens, packed
    )
    gate_whole = group_whole(gate)
    up = plan.send_columns(plan.team_columns(w_up))
    attn3, attn2c = plan.shift(attn2), swap(attn2, "c")
    out_whole = packed[:, : w_out.shape[0]].reshape(-1, width)
    small = packed[:, w_out.shape[0] : w_out.shape[0] + 5, :shard].transpose(1, 0, 2)
    small = plan.small_step(plan.small_step(small, "x"), "y")
    attn3, attn2c, small, out_whole, up = sync(attn3, attn2c, small, out_whole, up)
    up_whole = group_whole(up)
    gains, lengths = plan.small_end(small, block_lengths.shape[0])
    _, position = jax.vmap(row_layout)(lengths)
    cosine, sine = angles(position)
    part_gains = lax.dynamic_slice_in_dim(gains[:2], plan.index * columns, columns, axis=1)
    attn_gain_wide, mlp_gain_wide = gains[2], gains[3]
    attn3c = swap(attn3, "c")
    attn_whole = plan.join_group([[attn0, attn1, attn2, attn3], [attn0c, attn1c, attn2c, attn3c]])

    raw = product(team_tokens, attn_whole)
    inverse = lax.rsqrt(plan.sum_rows(norm_columns(raw, columns)) / width + epsilon)
    turned, mixed_low = attend(lengths, raw, inverse, part_gains, cosine, sine)
    attn_terms = product(mixed_low, out_whole).astype(bf16)
    attn_terms, down1, team_tokens = sync(attn_terms, down1, team_tokens)
    down2, down0c, down1c = plan.shift(down1), swap(w_down, "c"), swap(down1, "c")
    token_parts = plan.core_halves(team_tokens)
    terms = plan.terms_first(attn_terms)
    terms = plan.terms_second(*terms)
    attn_proj = plan.terms_sum(*terms)
    attn_normed, attn_inverse = norm_forward(attn_proj, attn_gain_wide)
    hidden = tokens.astype(f32) + attn_normed

    rows = plan.rows_first(plan.grouped(hidden.astype(bf16)))
    rows = plan.rows_second(*rows)
    down2, *rows = sync(down2, *rows)
    down3, down2c = plan.shift(down2), swap(down2, "c")
    team_hidden = join(*rows)
    gate = product(team_hidden, gate_whole)
    hidden_parts = plan.core_halves(team_hidden)
    gate, down3, *hidden_parts = sync(gate, down3, *hidden_parts)
    down3c = swap(down3, "c")
    upward = product(team_hidden, up_whole)
    down_whole = plan.join_group([[w_down, down1, down2, down3], [down0c, down1c, down2c, down3c]])
    sigmoid_gate = jax.nn.sigmoid(gate)
    activated = gate * sigmoid_gate
    inner_low = (activated * upward).astype(bf16)
    terms = plan.terms_first(product(inner_low, down_whole).astype(bf16))
    inner_parts = plan.core_halves(inner_low)
    down = plan.terms_sum(*plan.terms_second(*terms))
    down_normed, down_inverse = norm_forward(down, mlp_gain_wide)
    block_out = (live_col * (hidden + down_normed)).astype(bf16)

    grad_out = live_col * cotangent.astype(f32)
    grad_down, term_mlp_gain = norm_back(down, down_inverse, mlp_gain_wide, grad_out)
    rows = plan.rows_second(*plan.rows_first(grad_down.astype(bf16)))
    *inner_parts, mixed_other, mixed_mine = sync(*inner_parts, *plan.core_halves(mixed_low))
    team_grad_down = join(*rows)

    def terms_of(left, right):
        return inner_rows(left, right).astype(bf16)

    def summed(mine, other):
        return (mine.astype(f32) + other.astype(f32)).astype(bf16)

    down_other = swap(terms_of(inner_parts[0], team_grad_down), "c")
    down_mine = terms_of(inner_parts[1], team_grad_down)
    team_grad_down, down_mine = sync(team_grad_down, down_mine)
    grad_inner = product_tt(team_grad_down, down_whole)
    grad_gate = grad_inner * upward * sigmoid_gate * (1.0 + gate * (1.0 - sigmoid_gate))
    grad_up = grad_inner * activated
    grad_gate, grad_up, down_other, down_mine = sync(
        grad_gate.astype(bf16), grad_up.astype(bf16), down_other, down_mine
    )
    down_terms = summed(down_mine, down_other)
    grad_gate, grad_up, down_terms = sync(grad_gate, grad_up, down_terms)
    grad_w_down = lax.psum_scatter(down_terms, plan.z_axes, scatter_dimension=0, tiled=True)
    grad_from_mlp = product_tt(grad_gate, gate_whole) + product_tt(grad_up, up_whole)
    grad_from_mlp, grad_gate, grad_up, *hidden_parts = sync(
        grad_from_mlp.astype(bf16), grad_gate, grad_up, *hidden_parts
    )
    terms = plan.terms_first(grad_from_mlp)
    gate_other = swap(terms_of(hidden_parts[0], grad_gate), "c")
    gate_other, grad_gate, *terms = sync(gate_other, grad_gate, *terms)
    terms = plan.terms_second(*terms)
    gate_terms = summed(terms_of(hidden_parts[1], grad_gate), gate_other)
    gate_terms, grad_up, *terms = sync(gate_terms, grad_up, *terms)
    grad_hidden = grad_out + plan.ungrouped(plan.terms_sum(*terms))

    grad_proj, term_attn_gain = norm_back(attn_proj, attn_inverse, attn_gain_wide, grad_hidden)
    gate_sum = plan.shift(plan.ring_part(gate_terms, 1))
    rows = plan.rows_first(grad_proj.astype(bf16))
    up_other = swap(terms_of(hidden_parts[0], grad_up), "c")
    up_other, grad_up, grad_w_down, *rows = sync(up_other, grad_up, grad_w_down, *rows)
    rows = plan.rows_second(*rows)
    up_terms = summed(terms_of(hidden_parts[1], grad_up), up_other)
    up_terms, gate_sum, *rows = sync(up_terms, gate_sum, *rows)
    up_block = lax.psum_scatter(up_terms, plan.z_axes, scatter_dimension=0, tiled=True)
    gate_sum = plan.shift(summed(plan.ring_part(gate_terms, 2), gate_sum))
    team_grad_proj = join(*rows)
    grad_mixed = product_tt(team_grad_proj, out_whole).astype(bf16)
    scaled, grad_value, means, part_terms = attend_back(
        lengths, raw, turned, inverse, part_gains, cosine, sine, grad_mixed
    )
    gain_terms = jnp.stack([term_attn_gain, term_mlp_gain]).reshape(2, 2, 2, 2, 2, 2, -1)
    means, part_terms, gain_terms, gate_sum, team_grad_proj = sync(
        means, part_terms, gain_terms, gate_sum, team_grad_proj
    )
    gate_sum = plan.shift(summed(plan.ring_part(gate_terms, 3), gate_sum))
    out_other = swap(terms_of(mixed_other, team_grad_proj), "c")
    means = plan.sum_rows(means) / width
    means, out_other = sync(means, out_other)
    out_terms = summed(terms_of(mixed_mine, team_grad_proj), out_other)
    grad_raw = raw_back(raw, scaled, inverse, means, grad_value)
    attn_other = swap(terms_of(token_parts[0], grad_raw), "c")
    attn_mine = terms_of(token_parts[1], grad_raw)
    attn_mine, attn_other, grad_raw, out_terms, part_terms, gain_terms = sync(
        attn_mine, attn_other, grad_raw, out_terms, part_terms, gain_terms
    )
    attn_terms = summed(attn_mine, attn_other)
    attn_sum = plan.shift(plan.ring_part(attn_terms, 1))
    grad_from_attn = product_tt(grad_raw, attn_whole).astype(bf16)
    grad_from_attn, up_block = sync(grad_from_attn, up_block)
    terms = plan.terms_first(grad_from_attn)
    up_block = plan.return_columns(up_block)
    gain_terms = plan.gain_step(gain_terms, "c", 3)
    part_terms = part_terms + swap(part_terms, "c")
    attn_sum, gate_sum, part_terms, gain_terms, up_block, *terms = sync(
        attn_sum, gate_sum, part_terms, gain_terms, up_block, *terms
    )
    attn_sum = plan.shift(summed(plan.ring_part(attn_terms, 2), attn_sum))
    out_sum = plan.shift(plan.ring_part(out_terms, 1))
    terms = plan.terms_second(*terms)
    gate_block = plan.return_columns(summed(plan.ring_part(gate_terms, 0), gate_sum))
    attn_sum, out_sum, gate_block, part_terms, gain_terms, *terms = sync(
        attn_sum, out_sum, gate_block, part_terms, gain_terms, *terms
    )
    attn_sum = plan.shift(summed(plan.ring_part(attn_terms, 3), attn_sum))
    out_sum = plan.shift(summed(plan.ring_part(out_terms, 2), out_sum))
    grad_tokens = grad_hidden + plan.ungrouped(plan.terms_sum(*terms))
    gain_terms = plan.gain_step(plan.gain_step(gain_terms, "x", 2), "y", 1)
    part_terms = part_terms + swap(part_terms, "zh")
    grad_w_gate, grad_w_up = plan.whole_columns(gate_block), plan.whole_columns(up_block)
    attn_sum, out_sum, gain_terms, part_terms, grad_tokens, grad_w_gate, grad_w_up = sync(
        attn_sum, out_sum, gain_terms, part_terms, grad_tokens, grad_w_gate, grad_w_up
    )
    attn_block = plan.return_columns(summed(plan.ring_part(attn_terms, 0), attn_sum))
    out_sum = plan.shift(summed(plan.ring_part(out_terms, 3), out_sum))
    part_grads = plan.own_gains(part_terms + swap(part_terms, "zl"))
    gain_terms = plan.gain_step(plan.gain_step(gain_terms, "zh", 1), "zl", 1)
    attn_block, out_sum, part_grads, gain_terms = sync(attn_block, out_sum, part_grads, gain_terms)
    grad_w_out = plan.ring_part(out_terms, 0).astype(f32) + out_sum.astype(f32)
    grad_w_query, grad_w_key, grad_w_value = (
        plan.whole_columns(attn_block[..., k * columns : (k + 1) * columns]) for k in range(3)
    )
    return (
        block_out,
        grad_tokens.astype(bf16),
        grad_w_query,
        grad_w_key,
        grad_w_value,
        grad_w_out,
        grad_w_gate,
        grad_w_up,
        grad_w_down.astype(f32),
        part_grads[0],
        part_grads[1],
        gain_terms[0],
        gain_terms[1],
    )


def solution(mesh):
    if tuple(mesh.shape.values()) == (8, 4):
        mesh = Mesh(mesh.devices.reshape(2, 2, 2, 2, 2), Cube.every)
        every, step = Cube.every, local_cube
    else:
        every = tuple(mesh.axis_names)

        def step(*arrays):
            return local_plain(Plain(*every), *arrays)

    rows, line = P(every, None), P(every)
    return jax.shard_map(
        step,
        mesh=mesh,
        in_specs=(rows, line) + (rows,) * 7 + (line,) * 4 + (rows,),
        out_specs=(rows,) * 9 + (line,) * 4,
        check_vma=False,
    )
```

```python
import functools

import jax
import jax.numpy as jnp
from jax import lax
from jax.experimental import pallas as pl
from jax.experimental.pallas import tpu as pltpu
from jax.sharding import Mesh, PartitionSpec as P

HEAD_DIM = 128
BLOCK = 128

epsilon = 1e-06
rope_base = 500000.0
f32 = jnp.float32
bf16 = jnp.bfloat16
NO_COST = pl.CostEstimate(flops=0, bytes_accessed=0, transcendentals=0)


def product(left, right):
    return jnp.dot(left, right, preferred_element_type=f32)


def product_tt(left, right):
    return lax.dot_general(left, right, (((1,), (1,)), ((), ())), preferred_element_type=f32)


def inner_rows(left, right):
    return lax.dot_general(left, right, (((0,), (0,)), ((), ())), preferred_element_type=f32)


def norm_forward(values, gain):
    inverse = lax.rsqrt(jnp.mean(values * values, axis=-1, keepdims=True) + epsilon)
    return (values * inverse * gain, inverse)


def norm_back(values, inverse, gain, incoming):
    normed = values * inverse
    scaled = incoming * gain
    gain_term = jnp.sum(incoming * normed, axis=0)
    back = inverse * (scaled - normed * jnp.mean(scaled * normed, axis=-1, keepdims=True))
    return (back, gain_term)


def angles(position):
    half = HEAD_DIM // 2
    freq = rope_base ** (-jnp.arange(half, dtype=f32) / half)
    angle = position.astype(f32).reshape(-1, 1) * freq
    cosine, sine = jnp.cos(angle), jnp.sin(angle)
    return jnp.concatenate([cosine, cosine], axis=1), jnp.concatenate([-sine, sine], axis=1)


def row_layout(lengths):
    nblock = lengths.shape[0]
    row_ids = jnp.arange(nblock * BLOCK, dtype=jnp.int32)
    begin = jnp.arange(nblock, dtype=jnp.int32) * BLOCK
    cover = (
        (lengths[None, :] > 0)
        & (row_ids[:, None] >= begin[None, :])
        & (row_ids[:, None] < begin[None, :] + lengths[None, :])
    )
    live = jnp.any(cover, axis=1)
    owner = jnp.sum(jnp.where(cover, begin[None, :], 0), axis=1)
    return (live, row_ids - owner)


def allowed_keys(lengths_ref, device, nrows):
    rows = lax.broadcasted_iota(jnp.int32, (nrows, nrows), 0)
    keys = lax.broadcasted_iota(jnp.int32, (nrows, nrows), 1)

    def number(ids):
        found = -1 - ids
        for block in range(nrows // BLOCK):
            begin, length = block * BLOCK, lengths_ref[device, block]
            found = jnp.where((ids >= begin) & (ids < begin + length), begin, found)
        return found

    return (number(rows) == number(keys)) & (keys <= rows)


def turn(values, cosine, sine):
    return values * cosine + pltpu.roll(values, HEAD_DIM // 2, 1) * sine


def probabilities(query, key, allowed):
    scores = product_tt(query, key) * HEAD_DIM ** (-0.5)
    scores = jnp.where(allowed, scores, -1e30)
    powers = jnp.exp(scores - jnp.max(scores, axis=-1, keepdims=True))
    return powers / jnp.sum(powers, axis=-1, keepdims=True)


def attend_kernel(
    lengths_ref, raw_ref, inverse_ref, gains_ref, cosine_ref, sine_ref, turned_ref, mixed_ref
):
    nrows, columns = mixed_ref.shape
    allowed = allowed_keys(lengths_ref, pl.program_id(0), nrows)
    cosine, sine = cosine_ref[...], sine_ref[...]
    for head in range(columns // HEAD_DIM):
        here = slice(head * HEAD_DIM, (head + 1) * HEAD_DIM)
        turned = []
        for which in range(2):
            there = slice(which * columns + here.start, which * columns + here.stop)
            normed = raw_ref[:, there] * inverse_ref[:, which : which + 1]
            rotated = turn(normed * gains_ref[which : which + 1, here], cosine, sine).astype(bf16)
            turned_ref[:, there] = rotated
            turned.append(rotated)
        there = slice(2 * columns + here.start, 2 * columns + here.stop)
        value = raw_ref[:, there].astype(bf16)
        turned_ref[:, there] = value
        probs = probabilities(turned[0], turned[1], allowed)
        mixed_ref[:, here] = product(probs.astype(bf16), value).astype(bf16)


def attend_back_kernel(
    lengths_ref, raw_ref, turned_ref, inverse_ref, gains_ref, cosine_ref, sine_ref, grad_ref,
    scaled_ref, grad_value_ref, means_ref, terms_ref,
):
    nrows, columns = grad_ref.shape
    device = pl.program_id(0)
    allowed = allowed_keys(lengths_ref, device, nrows)
    cosine, sine = cosine_ref[...], sine_ref[...]

    @pl.when(device == 0)
    def _():
        terms_ref[...] = jnp.zeros_like(terms_ref)

    sums = [0.0, 0.0]
    for head in range(columns // HEAD_DIM):
        here = slice(head * HEAD_DIM, (head + 1) * HEAD_DIM)
        spots = [slice(k * columns + here.start, k * columns + here.stop) for k in range(3)]
        query, key, value = (turned_ref[:, spot] for spot in spots)
        incoming = grad_ref[:, here]
        probs = probabilities(query, key, allowed)
        grad_probs = product_tt(incoming, value)
        inner = jnp.sum(probs * grad_probs, axis=-1, keepdims=True)
        grad_scores = (probs * (grad_probs - inner)).astype(bf16)
        grad_value_ref[:, here] = inner_rows(probs.astype(bf16), incoming).astype(bf16)
        back = (product(grad_scores, key), inner_rows(grad_scores, query))
        for which in range(2):
            turned = turn(back[which] * HEAD_DIM ** (-0.5), cosine, -sine)
            normed = raw_ref[:, spots[which]] * inverse_ref[:, which : which + 1]
            terms_ref[which : which + 1, here] += jnp.sum(turned * normed, axis=0, keepdims=True)
            scaled = turned * gains_ref[which : which + 1, here]
            scaled_ref[:, spots[which]] = scaled
            sums[which] = sums[which] + jnp.sum(scaled * normed, axis=-1, keepdims=True)
    means_ref[...] = jnp.concatenate(sums, axis=1)


def attend_specs(nrows, columns):
    def rows(wide):
        return pl.BlockSpec((nrows, wide), lambda b: (b, 0))

    lengths = pl.BlockSpec(memory_space=pltpu.SMEM)
    gains = pl.BlockSpec((2, columns), lambda b: (0, 0))
    return rows, lengths, gains


def attend(lengths, raw, inverse, gains, cosine, sine):
    size, nrows = lengths.shape[0], raw.shape[0] // lengths.shape[0]
    columns = raw.shape[1] // 3
    rows, whole, gain = attend_specs(nrows, columns)
    return pl.pallas_call(
        attend_kernel,
        grid=(size,),
        in_specs=[whole, rows(3 * columns), rows(2), gain, rows(HEAD_DIM), rows(HEAD_DIM)],
        out_specs=[rows(3 * columns), rows(columns)],
        out_shape=[
            jax.ShapeDtypeStruct(raw.shape, bf16),
            jax.ShapeDtypeStruct((raw.shape[0], columns), bf16),
        ],
        cost_estimate=NO_COST,
    )(lengths, raw, inverse, gains, cosine, sine)


def attend_back(lengths, raw, turned, inverse, gains, cosine, sine, grad):
    size, nrows = lengths.shape[0], raw.shape[0] // lengths.shape[0]
    columns = raw.shape[1] // 3
    rows, whole, gain = attend_specs(nrows, columns)
    return pl.pallas_call(
        attend_back_kernel,
        grid=(size,),
        in_specs=[
            whole, rows(3 * columns), rows(3 * columns), rows(2), gain,
            rows(HEAD_DIM), rows(HEAD_DIM), rows(columns),
        ],
        out_specs=[rows(2 * columns), rows(columns), rows(2), gain],
        out_shape=[
            jax.ShapeDtypeStruct((raw.shape[0], 2 * columns), f32),
            jax.ShapeDtypeStruct((raw.shape[0], columns), bf16),
            jax.ShapeDtypeStruct((raw.shape[0], 2), f32),
            jax.ShapeDtypeStruct((2, columns), f32),
        ],
        cost_estimate=NO_COST,
    )(lengths, raw, turned, inverse, gains, cosine, sine, grad)


def swap(value, axis):
    return lax.ppermute(value, axis, ((0, 1), (1, 0)))


def sync(*values):
    return lax.optimization_barrier(values)


def pick(value, index, axis):
    return lax.dynamic_index_in_dim(value, index, axis, keepdims=False)


def join_kernel(table_ref, *refs):
    pieces, out, held, sems = refs[:-3], refs[-3], refs[-2], refs[-1]
    loads, stores = [], []
    for k, piece in enumerate(pieces):
        here = pl.ds(pl.multiple_of(table_ref[k] * 64, 64), piece.shape[0])
        loads.append(pltpu.make_async_copy(piece, held.at[here], sems.at[0, k]))
        stores.append(pltpu.make_async_copy(held.at[here], out.at[here], sems.at[1, k]))
        loads[-1].start()
    for load, store in zip(loads, stores):
        load.wait()
        store.start()
    for store in stores:
        store.wait()


def join(*pieces, table=None):
    if table is None:
        begins = [sum(piece.shape[0] for piece in pieces[:k]) // 64 for k in range(len(pieces))]
        table = jnp.array(begins, jnp.int32)
    shape = (sum(piece.shape[0] for piece in pieces), pieces[0].shape[1])
    return pl.pallas_call(
        join_kernel,
        in_specs=[pl.BlockSpec(memory_space=pltpu.SMEM)]
        + [pl.BlockSpec(memory_space=pl.ANY)] * len(pieces),
        out_specs=pl.BlockSpec(memory_space=pl.ANY),
        out_shape=jax.ShapeDtypeStruct(shape, pieces[0].dtype),
        scratch_shapes=[
            pltpu.VMEM(shape, pieces[0].dtype),
            pltpu.SemaphoreType.DMA((2, len(pieces))),
        ],
        compiler_params=pltpu.CompilerParams(vmem_limit_bytes=32 * 2**20),
        cost_estimate=NO_COST,
    )(table, *pieces)


def regroup_kernel(halves, in_ref, out_ref):
    for tile in range(len(halves) // 2):
        parts = [in_ref[:, half * 64 : (half + 1) * 64] for half in halves[2 * tile : 2 * tile + 2]]
        out_ref[:, tile * 128 : (tile + 1) * 128] = jnp.concatenate(parts, axis=1)


def regroup(value, halves):
    rows, width = value.shape
    block = pl.BlockSpec((rows // 2, width), lambda k: (k, 0))
    return pl.pallas_call(
        functools.partial(regroup_kernel, halves),
        grid=(2,),
        in_specs=[block],
        out_specs=block,
        out_shape=jax.ShapeDtypeStruct(value.shape, value.dtype),
        cost_estimate=NO_COST,
    )(value)


def spread_kernel(order, parts_ref, out_ref):
    wide = out_ref.shape[1] // len(order)
    for block, (part, column) in enumerate(order):
        here = slice(block * wide, (block + 1) * wide)
        out_ref[:, here] = parts_ref[part, :, column * wide : (column + 1) * wide].astype(f32)


def spread(parts, order):
    shape = (parts.shape[1], parts.shape[0] * parts.shape[2])
    return pl.pallas_call(
        functools.partial(spread_kernel, order),
        in_specs=[pl.BlockSpec(memory_space=pltpu.VMEM)],
        out_specs=pl.BlockSpec(memory_space=pltpu.VMEM),
        out_shape=jax.ShapeDtypeStruct(shape, f32),
        cost_estimate=NO_COST,
    )(parts)


class Cube:
    every = ("y", "x", "c", "zh", "zl")
    team = ("y", "x")
    z_axes = ("zh", "zl")
    group = ("c", "zh", "zl")

    def __init__(self):
        self.place = [lax.axis_index(axis) for axis in self.every]
        self.core = self.place[2]
        self.z = lax.axis_index(self.z_axes)
        self.size = 4
        self.index = lax.axis_index(self.team)

    def shift(self, value):
        return lax.ppermute(value, self.z_axes, ((0, 1), (1, 2), (2, 3), (3, 0)))

    def rows_first(self, rows):
        half = rows.shape[0] // 2
        top, low = rows[:half], rows[half:]
        return top, low, swap(top, "x"), swap(low, "y")

    def rows_second(self, top, low, top_x, low_y):
        top_y, low_x = swap(top, "y"), swap(low, "x")
        return top, low, top_x, low_x, top_y, low_y, swap(top_x, "y"), swap(low_y, "x")

    def terms_first(self, terms):
        terms = terms.reshape(2, 2, 2, -1, terms.shape[1])
        top, low = swap(terms[1, :, 0], "y"), swap(terms[:, 1, 1], "x")
        return terms[0, :, 0], terms[:, 0, 1], top, low

    def terms_second(self, top, low, top_y, low_x):
        top = top.astype(f32) + top_y.astype(f32)
        low = low.astype(f32) + low_x.astype(f32)
        return top[0], low[0], swap(top[1].astype(bf16), "x"), swap(low[1].astype(bf16), "y")

    def terms_sum(self, top, low, top_x, low_y):
        return jnp.concatenate([top + top_x.astype(f32), low + low_y.astype(f32)])

    def sum_along(self, rows, axis):
        shape = rows.shape
        rows = rows.reshape((2, 2, -1) + shape[1:])
        rows = rows + jnp.flip(swap(rows, axis), self.team.index(axis))
        return rows.reshape(shape)

    def sum_rows(self, rows):
        return self.sum_along(self.sum_along(rows, "y"), "x")

    def order(self, mine, other, index, axis):
        first = index == 0
        return jnp.stack([jnp.where(first, mine, other), jnp.where(first, other, mine)], axis)

    def team_columns(self, weight):
        rows = weight.shape[0]
        return weight.reshape(rows, 4, -1).transpose(1, 0, 2)

    def whole_columns(self, parts):
        return spread(parts, [(part, 0) for part in range(4)])

    def send_columns(self, parts):
        return lax.all_to_all(parts, self.team, 0, 0).reshape(-1, parts.shape[2])

    def return_columns(self, block):
        return lax.all_to_all(block.reshape(4, -1, block.shape[1]), self.team, 0, 0)

    def grouped(self, rows):
        return regroup(rows, [spot * 8 + place for place in range(8) for spot in range(4)])

    def ungrouped(self, rows):
        return regroup(rows, [place * 4 + spot for spot in range(4) for place in range(8)])

    def join_group(self, blocks):
        table, pieces = [], []
        for core in range(2):
            for k in range(4):
                unit = blocks[core][k].shape[0] // 64
                table.append(((self.core ^ core) * 4 + (self.z - k) % 4) * unit)
                pieces.append(blocks[core][k])
        return join(*pieces, table=jnp.stack(table).astype(jnp.int32))

    def core_halves(self, values):
        half = values.shape[1] // 2
        return [
            lax.dynamic_slice_in_dim(values, index * half, half, 1)
            for index in (1 - self.core, self.core)
        ]

    def ring_sum(self, k, terms, so_far=None):
        rows = terms[0].shape[0] // 4
        part = (self.z - k) % 4

        def pick_rows(term):
            if isinstance(term, tuple):
                begin = part % 2 * rows
                low, high = (lax.dynamic_slice_in_dim(half, begin, rows, 0) for half in term)
                return jnp.where(part < 2, low, high)
            return lax.dynamic_slice_in_dim(term, part * rows, rows, 0)

        parts = [pick_rows(term).astype(f32) for term in terms]
        return sum(parts if so_far is None else parts + [so_far.astype(f32)])

    def ring_step(self, k, terms, so_far=None):
        return self.shift(self.ring_sum(k, terms, so_far).astype(bf16))

    def small_rows(self, gains, lengths, width):
        small = [jnp.pad(row.astype(bf16), (0, width - row.shape[0])) for row in (*gains, lengths)]
        return jnp.pad(jnp.stack(small), ((0, 16 - len(small)), (0, 0)))

    def small_step(self, small, axis):
        index = self.place[self.every.index(axis)]
        small = self.order(small, swap(small, axis), index, 1)
        return small.reshape(small.shape[0], -1, small.shape[-1])

    def small_end(self, small, count):
        gains = small[:4].reshape(4, -1).astype(f32)
        y, x, c, _, _ = self.place
        ids = [
            (((y ^ dy) * 2 + (x ^ dx)) * 2 + c) * 4 + self.z for dy in range(2) for dx in range(2)
        ]
        lengths = jnp.stack([pick(small[4], i, 0) for i in ids])[:, :count]
        return gains, lengths.astype(jnp.int32)

    def gain_step(self, terms, axis, dim):
        index = self.place[self.every.index(axis)]
        return pick(terms, index, dim) + swap(pick(terms, 1 - index, dim), axis)

    def own_gains(self, terms):
        terms = terms.reshape(terms.shape[0], 2, 2, 2, -1)
        for index in self.place[2:]:
            terms = pick(terms, index, 1)
        return terms


class Plain:
    def __init__(self, team, group):
        self.team, self.group = team, group
        self.every = (team, group)
        self.size = lax.axis_size(team)
        self.index = lax.axis_index(team)

    def gather_rows(self, rows):
        return lax.all_gather(rows, self.team, axis=0, tiled=True)

    def scatter_rows(self, terms):
        return lax.psum_scatter(terms, self.team, scatter_dimension=0, tiled=True).astype(f32)

    def sum_rows(self, rows):
        return lax.psum(rows, self.team)

    def gather_columns(self, weight):
        rows = weight.shape[0]
        parts = weight.reshape(rows, self.size, -1).transpose(1, 0, 2)
        block = lax.all_to_all(parts, self.team, 0, 0)
        whole = lax.all_gather(block, self.group, axis=1, tiled=True)
        return whole.reshape(-1, block.shape[2])

    def scatter_columns(self, terms):
        terms = terms.reshape(self.size, -1, terms.shape[1])
        block = lax.psum_scatter(terms, self.group, scatter_dimension=1, tiled=True)
        parts = lax.all_to_all(block, self.team, 0, 0)
        return parts.transpose(1, 0, 2).reshape(parts.shape[1], -1).astype(f32)

    def gather_group(self, weight):
        return lax.all_gather(weight, self.group, axis=0, tiled=True)

    def scatter_group(self, terms, axis=0):
        block = lax.psum_scatter(terms, self.group, scatter_dimension=axis, tiled=True)
        return block.astype(f32)


def norm_columns(raw, columns):
    parts = [raw[:, k * columns : (k + 1) * columns] for k in (0, 1)]
    return jnp.stack([jnp.sum(part * part, axis=-1) for part in parts], axis=-1)


def raw_back(raw, scaled, inverse, means, grad_value):
    columns = grad_value.shape[1]
    grads = []
    for which in (0, 1):
        here = slice(which * columns, (which + 1) * columns)
        scale = inverse[:, which : which + 1]
        normed = raw[:, here] * scale
        grad = scale * (scaled[:, here] - normed * means[:, which : which + 1])
        grads.append(grad.astype(bf16))
    return jnp.concatenate(grads + [grad_value], axis=1)


def local_plain(
    plan,
    tokens,
    block_lengths,
    w_query,
    w_key,
    w_value,
    w_out,
    w_gate,
    w_up,
    w_down,
    query_gain,
    key_gain,
    attn_gain,
    mlp_gain,
    cotangent,
):
    width = tokens.shape[1]
    columns = width // plan.size
    live, _ = row_layout(block_lengths)
    live_col = live.astype(f32)[:, None]
    lengths = lax.all_gather(block_lengths, plan.team)
    _, position = jax.vmap(row_layout)(lengths)
    cosine, sine = angles(position)
    gains = jnp.stack([query_gain, key_gain, attn_gain, mlp_gain])
    gains = lax.all_gather(gains, plan.every, axis=1, tiled=True).astype(f32)
    part_gains = lax.dynamic_slice_in_dim(gains[:2], plan.index * columns, columns, axis=1)
    attn_gain_wide, mlp_gain_wide = gains[2], gains[3]
    attn_whole = jnp.concatenate(
        [plan.gather_columns(w) for w in (w_query, w_key, w_value)], axis=1
    )
    out_whole = plan.gather_group(w_out)
    gate_whole = plan.gather_columns(w_gate)
    up_whole = plan.gather_columns(w_up)
    down_whole = plan.gather_group(w_down)

    team_tokens = plan.gather_rows(tokens)
    raw = product(team_tokens, attn_whole)
    inverse = lax.rsqrt(plan.sum_rows(norm_columns(raw, columns)) / width + epsilon)
    turned, mixed_low = attend(lengths, raw, inverse, part_gains, cosine, sine)
    attn_proj = plan.scatter_rows(product(mixed_low, out_whole).astype(bf16))
    attn_normed, attn_inverse = norm_forward(attn_proj, attn_gain_wide)
    hidden = tokens.astype(f32) + attn_normed
    team_hidden = plan.gather_rows(hidden.astype(bf16))
    gate = product(team_hidden, gate_whole)
    upward = product(team_hidden, up_whole)
    sigmoid_gate = jax.nn.sigmoid(gate)
    activated = gate * sigmoid_gate
    inner_low = (activated * upward).astype(bf16)
    down = plan.scatter_rows(product(inner_low, down_whole).astype(bf16))
    down_normed, down_inverse = norm_forward(down, mlp_gain_wide)
    block_out = (live_col * (hidden + down_normed)).astype(bf16)

    grad_out = live_col * cotangent.astype(f32)
    grad_down, term_mlp_gain = norm_back(down, down_inverse, mlp_gain_wide, grad_out)
    team_grad_down = plan.gather_rows(grad_down.astype(bf16))
    grad_w_down = plan.scatter_group(inner_rows(inner_low, team_grad_down).astype(bf16))
    grad_inner = product_tt(team_grad_down, down_whole)
    grad_gate = grad_inner * upward * sigmoid_gate * (1.0 + gate * (1.0 - sigmoid_gate))
    grad_up = grad_inner * activated
    grad_gate, grad_up = grad_gate.astype(bf16), grad_up.astype(bf16)
    grad_w_gate = plan.scatter_columns(inner_rows(team_hidden, grad_gate).astype(bf16))
    grad_w_up = plan.scatter_columns(inner_rows(team_hidden, grad_up).astype(bf16))
    grad_from_mlp = product_tt(grad_gate, gate_whole) + product_tt(grad_up, up_whole)
    grad_hidden = grad_out + plan.scatter_rows(grad_from_mlp.astype(bf16))

    grad_proj, term_attn_gain = norm_back(attn_proj, attn_inverse, attn_gain_wide, grad_hidden)
    team_grad_proj = plan.gather_rows(grad_proj.astype(bf16))
    grad_mixed = product_tt(team_grad_proj, out_whole).astype(bf16)
    grad_w_out = plan.scatter_group(inner_rows(mixed_low, team_grad_proj).astype(bf16))
    scaled, grad_value, means, part_terms = attend_back(
        lengths, raw, turned, inverse, part_gains, cosine, sine, grad_mixed
    )
    means = plan.sum_rows(means) / width
    grad_raw = raw_back(raw, scaled, inverse, means, grad_value)
    grad_w_query, grad_w_key, grad_w_value = (
        plan.scatter_columns(
            inner_rows(team_tokens, grad_raw[:, k * columns : (k + 1) * columns]).astype(bf16)
        )
        for k in range(3)
    )
    grad_from_attn = plan.scatter_rows(product_tt(grad_raw, attn_whole).astype(bf16))
    part_grads = plan.scatter_group(part_terms, 1)
    gain_grads = lax.psum_scatter(
        jnp.stack([term_attn_gain, term_mlp_gain]), plan.every, scatter_dimension=1, tiled=True
    )
    return (
        block_out,
        (grad_hidden + grad_from_attn).astype(bf16),
        grad_w_query,
        grad_w_key,
        grad_w_value,
        grad_w_out,
        grad_w_gate,
        grad_w_up,
        grad_w_down,
        part_grads[0],
        part_grads[1],
        gain_grads[0],
        gain_grads[1],
    )


def local_cube(
    tokens,
    block_lengths,
    w_query,
    w_key,
    w_value,
    w_out,
    w_gate,
    w_up,
    w_down,
    query_gain,
    key_gain,
    attn_gain,
    mlp_gain,
    cotangent,
):
    plan = Cube()
    width = tokens.shape[1]
    columns = width // plan.size
    live, _ = row_layout(block_lengths)
    live_col = live.astype(f32)[:, None]

    def group_whole(block):
        return lax.all_gather(block, plan.group, axis=0, tiled=True)

    shard = query_gain.shape[0]
    small = plan.small_rows((query_gain, key_gain, attn_gain, mlp_gain), block_lengths, width)
    attn_parts = jnp.concatenate([plan.team_columns(w) for w in (w_query, w_key, w_value)], axis=2)
    attn_parts, own, out_rows, down0 = sync(attn_parts, tokens, w_out, w_down)
    packed = group_whole(jnp.concatenate([out_rows, small])).reshape(8, -1, width)
    down1 = plan.shift(down0)
    rows = plan.rows_first(plan.grouped(own))
    attn0 = plan.send_columns(attn_parts)
    attn0, w_gate, *rows = sync(attn0, w_gate, *rows)
    attn1, attn0c = plan.shift(attn0), swap(attn0, "c")
    rows = plan.rows_second(*rows)
    attn1, attn0c, down1, w_gate, *rows = sync(attn1, attn0c, down1, w_gate, *rows)
    gate = plan.send_columns(plan.team_columns(w_gate))
    attn2, attn1c = plan.shift(attn1), swap(attn1, "c")
    team_tokens = join(*rows)
    attn2, attn1c, gate, w_up, team_tokens, packed = sync(
        attn2, attn1c, gate, w_up, team_tokens, packed
    )
    gate_whole = group_whole(gate)
    up = plan.send_columns(plan.team_columns(w_up))
    attn3, attn2c = plan.shift(attn2), swap(attn2, "c")
    out_whole = packed[:, : w_out.shape[0]].reshape(-1, width)
    small = packed[:, w_out.shape[0] : w_out.shape[0] + 5, :shard].transpose(1, 0, 2)
    small = plan.small_step(plan.small_step(small, "x"), "y")
    attn3, attn2c, small, out_whole, up = sync(attn3, attn2c, small, out_whole, up)
    up_whole = group_whole(up)
    gains, lengths = plan.small_end(small, block_lengths.shape[0])
    _, position = jax.vmap(row_layout)(lengths)
    cosine, sine = angles(position)
    part_gains = lax.dynamic_slice_in_dim(gains[:2], plan.index * columns, columns, axis=1)
    attn_gain_wide, mlp_gain_wide = gains[2], gains[3]
    attn3c = swap(attn3, "c")
    attn_whole = plan.join_group([[attn0, attn1, attn2, attn3], [attn0c, attn1c, attn2c, attn3c]])

    raw = product(team_tokens, attn_whole)
    inverse = lax.rsqrt(plan.sum_rows(norm_columns(raw, columns)) / width + epsilon)
    turned, mixed_low = attend(lengths, raw, inverse, part_gains, cosine, sine)
    attn_terms = product(mixed_low, out_whole).astype(bf16)
    attn_terms, down1, team_tokens = sync(attn_terms, down1, team_tokens)
    down2, down0c, down1c = plan.shift(down1), swap(w_down, "c"), swap(down1, "c")
    terms = plan.terms_first(attn_terms)
    terms = plan.terms_second(*terms)
    attn_proj = plan.terms_sum(*terms)
    attn_normed, attn_inverse = norm_forward(attn_proj, attn_gain_wide)
    hidden = tokens.astype(f32) + attn_normed

    rows = plan.rows_first(plan.grouped(hidden.astype(bf16)))
    rows = plan.rows_second(*rows)
    team_hidden = join(*rows)
    gate = product(team_hidden, gate_whole)
    hidden_parts = plan.core_halves(team_hidden)
    gate, down2, *hidden_parts = sync(gate, down2, *hidden_parts)
    down3, down2c = plan.shift(down2), swap(down2, "c")
    upward = product(team_hidden, up_whole)
    upward, down3 = sync(upward, down3)
    down3c = swap(down3, "c")
    down_whole = plan.join_group([[w_down, down1, down2, down3], [down0c, down1c, down2c, down3c]])
    sigmoid_gate = jax.nn.sigmoid(gate)
    activated = gate * sigmoid_gate
    inner_low = (activated * upward).astype(bf16)
    terms = plan.terms_first(product(inner_low, down_whole).astype(bf16))
    *inner_parts, top, low, top_y, low_x = sync(*plan.core_halves(inner_low), *terms)
    down = plan.terms_sum(*plan.terms_second(top, low, top_y, low_x))
    down_normed, down_inverse = norm_forward(down, mlp_gain_wide)
    block_out = (live_col * (hidden + down_normed)).astype(bf16)

    grad_out = live_col * cotangent.astype(f32)
    grad_down, term_mlp_gain = norm_back(down, down_inverse, mlp_gain_wide, grad_out)
    rows = plan.rows_second(*plan.rows_first(grad_down.astype(bf16)))
    team_grad_down = join(*rows)

    def terms_of(left, right):
        return inner_rows(left, right).astype(bf16)

    def summed(mine, other):
        return (mine.astype(f32) + other.astype(f32)).astype(bf16)

    down_other = swap(terms_of(inner_parts[0], team_grad_down), "c")
    down_mine = terms_of(inner_parts[1], team_grad_down)
    team_grad_down, down_mine, down_other = sync(team_grad_down, down_mine, down_other)
    down_terms = summed(down_mine, down_other)
    gain_shape = (2, 2, 2, 2, 2, -1)
    team_grad_down, down_terms, mlp_terms = sync(team_grad_down, down_terms, term_mlp_gain)
    mlp_terms = plan.gain_step(mlp_terms.reshape(gain_shape), "c", 2)
    team_grad_down, mlp_terms = sync(team_grad_down, mlp_terms)
    grad_w_down = lax.psum_scatter(down_terms, plan.z_axes, scatter_dimension=0, tiled=True)
    grad_inner = product_tt(team_grad_down, down_whole)
    grad_gate = grad_inner * upward * sigmoid_gate * (1.0 + gate * (1.0 - sigmoid_gate))
    grad_up = grad_inner * activated
    grad_gate, grad_up, *hidden_parts = sync(
        grad_gate.astype(bf16), grad_up.astype(bf16), *hidden_parts
    )
    gate_away = terms_of(hidden_parts[0], grad_gate)
    gate_away, grad_up, other_part = sync(gate_away, grad_up, hidden_parts[0])
    gate_other = swap(gate_away, "c")
    up_away = terms_of(other_part, grad_up)
    up_away, grad_gate, grad_up = sync(up_away, grad_gate, grad_up)
    up_other = swap(up_away, "c")
    grad_from_mlp = product_tt(grad_gate, gate_whole) + product_tt(grad_up, up_whole)
    grad_from_mlp, grad_gate, grad_up, hidden_part = sync(
        grad_from_mlp.astype(bf16), grad_gate, grad_up, hidden_parts[1]
    )
    terms = plan.terms_first(grad_from_mlp)
    gate_terms = summed(terms_of(hidden_part, grad_gate), gate_other)
    gate_terms, grad_up, *terms = sync(gate_terms, grad_up, *terms)
    gate_block = lax.psum_scatter(gate_terms, plan.z_axes, scatter_dimension=0, tiled=True)
    terms = plan.terms_second(*terms)
    late_parts = (*plan.core_halves(team_tokens), *plan.core_halves(mixed_low))
    token_other, token_mine, mixed_other, mixed_mine, grad_up, *terms = sync(
        *late_parts, grad_up, *terms
    )
    grad_hidden = grad_out + plan.ungrouped(plan.terms_sum(*terms))

    grad_proj, term_attn_gain = norm_back(attn_proj, attn_inverse, attn_gain_wide, grad_hidden)
    rows = plan.rows_first(grad_proj.astype(bf16))
    up_mine = terms_of(hidden_part, grad_up)
    up_mine, up_other, grad_w_down, *rows = sync(up_mine, up_other, grad_w_down, *rows)
    rows = plan.rows_second(*rows)
    up_terms = summed(up_mine, up_other)
    up_terms, gate_block, *rows = sync(up_terms, gate_block, *rows)
    up_block = lax.psum_scatter(up_terms, plan.z_axes, scatter_dimension=0, tiled=True)
    team_grad_proj = join(*rows)
    grad_mixed = product_tt(team_grad_proj, out_whole).astype(bf16)
    scaled, grad_value, means, part_terms = attend_back(
        lengths, raw, turned, inverse, part_gains, cosine, sine, grad_mixed
    )
    attn_gain_terms = plan.gain_step(term_attn_gain.reshape(gain_shape), "c", 2)
    gain_terms = jnp.stack([attn_gain_terms, mlp_terms])
    gate_block = plan.return_columns(gate_block)
    means, part_terms, gain_terms, team_grad_proj, gate_block = sync(
        means, part_terms, gain_terms, team_grad_proj, gate_block
    )
    out_away = terms_of(mixed_other, team_grad_proj)
    means = plan.sum_along(means, "y")
    means, out_away, team_grad_proj = sync(means, out_away, team_grad_proj)
    out_mine = terms_of(mixed_mine, team_grad_proj)
    means = plan.sum_along(means, "x") / width
    means, out_mine = sync(means, out_mine)
    grad_raw = raw_back(raw, scaled, inverse, means, grad_value)
    half = token_other.shape[1] // 2
    attn_other = [swap(terms_of(token_other[:, :half], grad_raw), "c")]
    attn_other += [swap(terms_of(token_other[:, half:], grad_raw), "c")]
    out_other = swap(out_away, "c")
    attn_mine = terms_of(token_mine, grad_raw)
    grad_from_attn = product_tt(grad_raw, attn_whole).astype(bf16)
    grad_from_attn, attn_mine, part_terms, gain_terms, *attn_other = sync(
        grad_from_attn, attn_mine, part_terms, gain_terms, *attn_other
    )
    attn_terms = (attn_mine, tuple(attn_other))
    attn_sum = plan.ring_step(1, attn_terms)
    terms = plan.terms_first(grad_from_attn)
    part_terms = part_terms + swap(part_terms, "c")
    attn_sum, out_other, part_terms, *terms = sync(attn_sum, out_other, part_terms, *terms)
    out_terms = (out_mine, out_other)
    attn_sum = plan.ring_step(2, attn_terms, attn_sum)
    out_sum = plan.ring_step(1, out_terms)
    gain_terms = plan.gain_step(gain_terms, "zh", 3)
    part_terms = part_terms + swap(part_terms, "zh")
    terms = plan.terms_second(*terms)
    grad_w_gate = plan.whole_columns(gate_block)
    attn_sum, out_sum, gain_terms, part_terms, up_block, grad_w_gate, *terms = sync(
        attn_sum, out_sum, gain_terms, part_terms, up_block, grad_w_gate, *terms
    )
    attn_sum = plan.ring_step(3, attn_terms, attn_sum)
    out_sum = plan.ring_step(2, out_terms, out_sum)
    up_block = plan.return_columns(up_block)
    grad_tokens = grad_hidden + plan.ungrouped(plan.terms_sum(*terms))
    gain_terms = plan.gain_step(gain_terms, "zl", 3)
    part_grads = plan.own_gains(part_terms + swap(part_terms, "zl"))
    attn_sum, out_sum, up_block, gain_terms, part_grads, grad_tokens = sync(
        attn_sum, out_sum, up_block, gain_terms, part_grads, grad_tokens
    )
    attn_block = plan.return_columns(plan.ring_sum(0, attn_terms, attn_sum).astype(bf16))
    out_sum = plan.ring_step(3, out_terms, out_sum)
    gain_terms = plan.gain_step(plan.gain_step(gain_terms, "x", 2), "y", 1)
    grad_w_up = plan.whole_columns(up_block)
    attn_block, grad_w_up, out_sum, gain_terms = sync(attn_block, grad_w_up, out_sum, gain_terms)
    grad_w_out = plan.ring_sum(0, out_terms, out_sum)
    grad_w_query, grad_w_key, grad_w_value = (
        plan.whole_columns(attn_block[..., k * columns : (k + 1) * columns]) for k in range(3)
    )
    return (
        block_out,
        grad_tokens.astype(bf16),
        grad_w_query,
        grad_w_key,
        grad_w_value,
        grad_w_out,
        grad_w_gate,
        grad_w_up,
        grad_w_down.astype(f32),
        part_grads[0],
        part_grads[1],
        gain_terms[0],
        gain_terms[1],
    )


def solution(mesh):
    if tuple(mesh.shape.values()) == (8, 4):
        mesh = Mesh(mesh.devices.reshape(2, 2, 2, 2, 2), Cube.every)
        every, step = Cube.every, local_cube
    else:
        every = tuple(mesh.axis_names)

        def step(*arrays):
            return local_plain(Plain(*every), *arrays)

    rows, line = P(every, None), P(every)
    return jax.shard_map(
        step,
        mesh=mesh,
        in_specs=(rows, line) + (rows,) * 7 + (line,) * 4 + (rows,),
        out_specs=(rows,) * 9 + (line,) * 4,
        check_vma=False,
    )
```

```python
import functools

import jax
import jax.numpy as jnp
from jax import lax
from jax.experimental import pallas as pl
from jax.experimental.pallas import tpu as pltpu
from jax.sharding import Mesh, PartitionSpec as P

HEAD_DIM = 128
BLOCK = 128

epsilon = 1e-06
rope_base = 500000.0
f32 = jnp.float32
bf16 = jnp.bfloat16
NO_COST = pl.CostEstimate(flops=0, bytes_accessed=0, transcendentals=0)


def product(left, right):
    return jnp.dot(left, right, preferred_element_type=f32)


def product_tt(left, right):
    return lax.dot_general(left, right, (((1,), (1,)), ((), ())), preferred_element_type=f32)


def inner_rows(left, right):
    return lax.dot_general(left, right, (((0,), (0,)), ((), ())), preferred_element_type=f32)


def norm_forward(values, gain):
    inverse = lax.rsqrt(jnp.mean(values * values, axis=-1, keepdims=True) + epsilon)
    return (values * inverse * gain, inverse)


def norm_back(values, inverse, gain, incoming):
    normed = values * inverse
    scaled = incoming * gain
    gain_term = jnp.sum(incoming * normed, axis=0)
    back = inverse * (scaled - normed * jnp.mean(scaled * normed, axis=-1, keepdims=True))
    return (back, gain_term)


def angles(position):
    half = HEAD_DIM // 2
    freq = rope_base ** (-jnp.arange(half, dtype=f32) / half)
    angle = position.astype(f32).reshape(-1, 1) * freq
    cosine, sine = jnp.cos(angle), jnp.sin(angle)
    return jnp.concatenate([cosine, cosine], axis=1), jnp.concatenate([-sine, sine], axis=1)


def row_layout(lengths):
    nblock = lengths.shape[0]
    row_ids = jnp.arange(nblock * BLOCK, dtype=jnp.int32)
    begin = jnp.arange(nblock, dtype=jnp.int32) * BLOCK
    cover = (
        (lengths[None, :] > 0)
        & (row_ids[:, None] >= begin[None, :])
        & (row_ids[:, None] < begin[None, :] + lengths[None, :])
    )
    live = jnp.any(cover, axis=1)
    owner = jnp.sum(jnp.where(cover, begin[None, :], 0), axis=1)
    return (live, row_ids - owner)


def allowed_keys(lengths_ref, device, nrows):
    rows = lax.broadcasted_iota(jnp.int32, (nrows, nrows), 0)
    keys = lax.broadcasted_iota(jnp.int32, (nrows, nrows), 1)

    def number(ids):
        found = -1 - ids
        for block in range(nrows // BLOCK):
            begin, length = block * BLOCK, lengths_ref[device, block]
            found = jnp.where((ids >= begin) & (ids < begin + length), begin, found)
        return found

    return (number(rows) == number(keys)) & (keys <= rows)


def turn(values, cosine, sine):
    return values * cosine + pltpu.roll(values, HEAD_DIM // 2, 1) * sine


def probabilities(query, key, allowed):
    scores = product_tt(query, key) * HEAD_DIM ** (-0.5)
    scores = jnp.where(allowed, scores, -1e30)
    powers = jnp.exp(scores - jnp.max(scores, axis=-1, keepdims=True))
    return powers * (1.0 / jnp.sum(powers, axis=-1, keepdims=True))


def attend_kernel(
    lengths_ref, raw_ref, inverse_ref, gains_ref, cosine_ref, sine_ref, turned_ref, mixed_ref
):
    nrows, columns = mixed_ref.shape
    allowed = allowed_keys(lengths_ref, pl.program_id(0), nrows)
    cosine, sine = cosine_ref[...], sine_ref[...]
    for head in range(columns // HEAD_DIM):
        here = slice(head * HEAD_DIM, (head + 1) * HEAD_DIM)
        turned = []
        for which in range(2):
            there = slice(which * columns + here.start, which * columns + here.stop)
            normed = raw_ref[:, there] * inverse_ref[:, which : which + 1]
            rotated = turn(normed * gains_ref[which : which + 1, here], cosine, sine).astype(bf16)
            turned_ref[:, there] = rotated
            turned.append(rotated)
        there = slice(2 * columns + here.start, 2 * columns + here.stop)
        value = raw_ref[:, there].astype(bf16)
        turned_ref[:, there] = value
        probs = probabilities(turned[0], turned[1], allowed)
        mixed_ref[:, here] = product(probs.astype(bf16), value).astype(bf16)


def attend_back_kernel(
    lengths_ref, raw_ref, turned_ref, inverse_ref, gains_ref, cosine_ref, sine_ref, grad_ref,
    scaled_ref, grad_value_ref, means_ref, terms_ref,
):
    nrows, columns = grad_ref.shape
    device = pl.program_id(0)
    allowed = allowed_keys(lengths_ref, device, nrows)
    cosine, sine = cosine_ref[...], sine_ref[...]

    @pl.when(device == 0)
    def _():
        terms_ref[...] = jnp.zeros_like(terms_ref)

    sums = [0.0, 0.0]
    for head in range(columns // HEAD_DIM):
        here = slice(head * HEAD_DIM, (head + 1) * HEAD_DIM)
        spots = [slice(k * columns + here.start, k * columns + here.stop) for k in range(3)]
        query, key, value = (turned_ref[:, spot] for spot in spots)
        incoming = grad_ref[:, here]
        probs = probabilities(query, key, allowed)
        grad_probs = product_tt(incoming, value)
        inner = jnp.sum(probs * grad_probs, axis=-1, keepdims=True)
        grad_scores = (probs * (grad_probs - inner)).astype(bf16)
        grad_value_ref[:, here] = inner_rows(probs.astype(bf16), incoming).astype(bf16)
        back = (product(grad_scores, key), inner_rows(grad_scores, query))
        for which in range(2):
            turned = turn(back[which] * HEAD_DIM ** (-0.5), cosine, -sine)
            normed = raw_ref[:, spots[which]] * inverse_ref[:, which : which + 1]
            terms_ref[which : which + 1, here] += jnp.sum(turned * normed, axis=0, keepdims=True)
            scaled = turned * gains_ref[which : which + 1, here]
            scaled_ref[:, spots[which]] = scaled
            sums[which] = sums[which] + jnp.sum(scaled * normed, axis=-1, keepdims=True)
    means_ref[...] = jnp.concatenate(sums, axis=1)


def attend_specs(nrows, columns):
    def rows(wide):
        return pl.BlockSpec((nrows, wide), lambda b: (b, 0))

    lengths = pl.BlockSpec(memory_space=pltpu.SMEM)
    gains = pl.BlockSpec((2, columns), lambda b: (0, 0))
    return rows, lengths, gains


def attend(lengths, raw, inverse, gains, cosine, sine):
    size, nrows = lengths.shape[0], raw.shape[0] // lengths.shape[0]
    columns = raw.shape[1] // 3
    rows, whole, gain = attend_specs(nrows, columns)
    return pl.pallas_call(
        attend_kernel,
        grid=(size,),
        in_specs=[whole, rows(3 * columns), rows(2), gain, rows(HEAD_DIM), rows(HEAD_DIM)],
        out_specs=[rows(3 * columns), rows(columns)],
        out_shape=[
            jax.ShapeDtypeStruct(raw.shape, bf16),
            jax.ShapeDtypeStruct((raw.shape[0], columns), bf16),
        ],
        cost_estimate=NO_COST,
    )(lengths, raw, inverse, gains, cosine, sine)


def attend_back(lengths, raw, turned, inverse, gains, cosine, sine, grad):
    size, nrows = lengths.shape[0], raw.shape[0] // lengths.shape[0]
    columns = raw.shape[1] // 3
    rows, whole, gain = attend_specs(nrows, columns)
    return pl.pallas_call(
        attend_back_kernel,
        grid=(size,),
        in_specs=[
            whole, rows(3 * columns), rows(3 * columns), rows(2), gain,
            rows(HEAD_DIM), rows(HEAD_DIM), rows(columns),
        ],
        out_specs=[rows(2 * columns), rows(columns), rows(2), gain],
        out_shape=[
            jax.ShapeDtypeStruct((raw.shape[0], 2 * columns), f32),
            jax.ShapeDtypeStruct((raw.shape[0], columns), bf16),
            jax.ShapeDtypeStruct((raw.shape[0], 2), f32),
            jax.ShapeDtypeStruct((2, columns), f32),
        ],
        cost_estimate=NO_COST,
    )(lengths, raw, turned, inverse, gains, cosine, sine, grad)


def swap(value, axis):
    return lax.ppermute(value, axis, ((0, 1), (1, 0)))


def sync(*values):
    return lax.optimization_barrier(values)


def pick(value, index, axis):
    return lax.dynamic_index_in_dim(value, index, axis, keepdims=False)


def join_kernel(table_ref, *refs):
    pieces, out, held, sems = refs[:-3], refs[-3], refs[-2], refs[-1]
    loads, stores = [], []
    for k, piece in enumerate(pieces):
        here = pl.ds(pl.multiple_of(table_ref[k] * 64, 64), piece.shape[0])
        loads.append(pltpu.make_async_copy(piece, held.at[here], sems.at[0, k]))
        stores.append(pltpu.make_async_copy(held.at[here], out.at[here], sems.at[1, k]))
        loads[-1].start()
    for load, store in zip(loads, stores):
        load.wait()
        store.start()
    for store in stores:
        store.wait()


def join(*pieces, table=None):
    if table is None:
        begins = [sum(piece.shape[0] for piece in pieces[:k]) // 64 for k in range(len(pieces))]
        table = jnp.array(begins, jnp.int32)
    shape = (sum(piece.shape[0] for piece in pieces), pieces[0].shape[1])
    return pl.pallas_call(
        join_kernel,
        in_specs=[pl.BlockSpec(memory_space=pltpu.SMEM)]
        + [pl.BlockSpec(memory_space=pl.ANY)] * len(pieces),
        out_specs=pl.BlockSpec(memory_space=pl.ANY),
        out_shape=jax.ShapeDtypeStruct(shape, pieces[0].dtype),
        scratch_shapes=[
            pltpu.VMEM(shape, pieces[0].dtype),
            pltpu.SemaphoreType.DMA((2, len(pieces))),
        ],
        compiler_params=pltpu.CompilerParams(vmem_limit_bytes=32 * 2**20),
        cost_estimate=NO_COST,
    )(table, *pieces)


def regroup_kernel(halves, in_ref, out_ref):
    for tile in range(len(halves) // 2):
        parts = [in_ref[:, half * 64 : (half + 1) * 64] for half in halves[2 * tile : 2 * tile + 2]]
        out_ref[:, tile * 128 : (tile + 1) * 128] = jnp.concatenate(parts, axis=1)


def regroup(value, halves):
    rows, width = value.shape
    block = pl.BlockSpec((rows // 2, width), lambda k: (k, 0))
    return pl.pallas_call(
        functools.partial(regroup_kernel, halves),
        grid=(2,),
        in_specs=[block],
        out_specs=block,
        out_shape=jax.ShapeDtypeStruct(value.shape, value.dtype),
        cost_estimate=NO_COST,
    )(value)


def spread_kernel(order, parts_ref, out_ref):
    wide = out_ref.shape[1] // len(order)
    for block, (part, column) in enumerate(order):
        here = slice(block * wide, (block + 1) * wide)
        out_ref[:, here] = parts_ref[part, :, column * wide : (column + 1) * wide].astype(f32)


def spread(parts, order):
    shape = (parts.shape[1], parts.shape[0] * parts.shape[2])
    return pl.pallas_call(
        functools.partial(spread_kernel, order),
        in_specs=[pl.BlockSpec(memory_space=pltpu.VMEM)],
        out_specs=pl.BlockSpec(memory_space=pltpu.VMEM),
        out_shape=jax.ShapeDtypeStruct(shape, f32),
        cost_estimate=NO_COST,
    )(parts)


def proj_back_kernel(
    halves, top_ref, low_ref, top_x_ref, low_y_ref, live_ref, cotangent_ref, proj_ref, inverse_ref,
    gain_ref, hidden_ref, grad_top_ref, grad_low_ref, term_ref,
):
    parts = ((top_ref, top_x_ref, grad_top_ref), (low_ref, low_y_ref, grad_low_ref))
    gain = gain_ref[...]
    term = 0.0
    for half, (mine_ref, other_ref, grad_ref) in enumerate(parts):
        total = mine_ref[...] + other_ref[...].astype(f32)
        blocks = [total[:, k * 64 : (k + 1) * 64] for k in halves]
        total = jnp.concatenate(blocks, axis=1)
        total += live_ref[half] * cotangent_ref[half].astype(f32)
        hidden_ref[half] = total
        normed = proj_ref[half] * inverse_ref[half]
        term += jnp.sum(total * normed, axis=0, keepdims=True)
        scaled = total * gain
        mean = jnp.mean(scaled * normed, axis=-1, keepdims=True)
        grad_ref[...] = (inverse_ref[half] * (scaled - normed * mean)).astype(bf16)
    first = pl.program_id(0) == 0
    term_ref[...] = jnp.where(first, term, term_ref[...] + term)


def ordered(blocks, left_ref, right_ref, left_x_ref, right_y_ref):
    left = left_ref[...] + left_x_ref[...].astype(f32)
    right = right_ref[...] + right_y_ref[...].astype(f32)
    half = left.shape[1] // 64
    parts = [(left, k) if k < half else (right, k - half) for k in blocks]
    return jnp.concatenate([part[:, k * 64 : (k + 1) * 64] for part, k in parts], axis=1)


def tokens_kernel(blocks, left_ref, right_ref, left_x_ref, right_y_ref, hidden_ref, out_ref):
    total = ordered(blocks, left_ref, right_ref, left_x_ref, right_y_ref)
    out_ref[...] = (total + hidden_ref[...]).astype(bf16)


def tokens_end(blocks, left, right, left_x, right_y, hidden):
    rows, width = hidden.shape
    side = pl.BlockSpec((rows // 4, width // 2), lambda k: (k, 0))
    whole = pl.BlockSpec((rows // 4, width), lambda k: (k, 0))
    return pl.pallas_call(
        functools.partial(tokens_kernel, blocks),
        grid=(4,),
        in_specs=[side, side, side, side, whole],
        out_specs=whole,
        out_shape=jax.ShapeDtypeStruct((rows, width), bf16),
        cost_estimate=NO_COST,
    )(left, right, left_x, right_y, hidden)


def proj_back_kernel(
    blocks, left_ref, right_ref, left_x_ref, right_y_ref, live_ref, cotangent_ref, proj_ref,
    inverse_ref, gain_ref, hidden_ref, grad_ref, term_ref,
):
    total = ordered(blocks, left_ref, right_ref, left_x_ref, right_y_ref)
    total += live_ref[...] * cotangent_ref[...].astype(f32)
    hidden_ref[...] = total
    normed = proj_ref[...] * inverse_ref[...]
    term = jnp.sum(total * normed, axis=0, keepdims=True)
    scaled = total * gain_ref[...]
    mean = jnp.mean(scaled * normed, axis=-1, keepdims=True)
    grad_ref[...] = (inverse_ref[...] * (scaled - normed * mean)).astype(bf16)
    first = pl.program_id(0) == 0
    term_ref[...] = jnp.where(first, term, term_ref[...] + term)


def proj_back(blocks, left, right, left_x, right_y, live, cotangent, proj, inverse, gain):
    rows, width = proj.shape
    side = pl.BlockSpec((rows // 4, width // 2), lambda k: (k, 0))
    whole = pl.BlockSpec((rows // 4, width), lambda k: (k, 0))
    column = pl.BlockSpec((rows // 4, 1), lambda k: (k, 0))
    line = pl.BlockSpec((1, width), lambda k: (0, 0))
    hidden, grad, term = pl.pallas_call(
        functools.partial(proj_back_kernel, blocks),
        grid=(4,),
        in_specs=[side, side, side, side, column, whole, whole, column, line],
        out_specs=[whole, whole, line],
        out_shape=[
            jax.ShapeDtypeStruct((rows, width), f32),
            jax.ShapeDtypeStruct((rows, width), bf16),
            jax.ShapeDtypeStruct((1, width), f32),
        ],
        cost_estimate=NO_COST,
    )(left, right, left_x, right_y, live, cotangent, proj, inverse, gain.reshape(1, width))
    return hidden, grad, term[0]


def spread_three_kernel(parts_ref, *out_refs):
    columns = parts_ref.shape[2] // 3
    for which, out_ref in enumerate(out_refs):
        there = slice(which * columns, (which + 1) * columns)
        for part in range(parts_ref.shape[0]):
            here = slice(part * columns, (part + 1) * columns)
            out_ref[:, here] = parts_ref[part, :, there].astype(f32)


def spread_three(parts):
    shape = (parts.shape[1], parts.shape[0] * parts.shape[2] // 3)
    return pl.pallas_call(
        spread_three_kernel,
        in_specs=[pl.BlockSpec(memory_space=pltpu.VMEM)],
        out_specs=[pl.BlockSpec(memory_space=pltpu.VMEM)] * 3,
        out_shape=[jax.ShapeDtypeStruct(shape, f32)] * 3,
        cost_estimate=NO_COST,
    )(parts)


class Cube:
    every = ("y", "x", "c", "zh", "zl")
    team = ("y", "x")
    z_axes = ("zh", "zl")
    group = ("c", "zh", "zl")

    def __init__(self):
        self.place = [lax.axis_index(axis) for axis in self.every]
        self.core = self.place[2]
        self.z = lax.axis_index(self.z_axes)
        self.size = 4
        self.index = lax.axis_index(self.team)

    def shift(self, value):
        return lax.ppermute(value, self.z_axes, ((0, 1), (1, 2), (2, 3), (3, 0)))

    def rows_first(self, rows):
        half = rows.shape[0] // 2
        top, low = rows[:half], rows[half:]
        return top, low, swap(top, "x"), swap(low, "y")

    def rows_second(self, top, low, top_x, low_y):
        top_y, low_x = swap(top, "y"), swap(low, "x")
        return top, low, top_x, low_x, top_y, low_y, swap(top_x, "y"), swap(low_y, "x")

    def terms_first(self, make, *values):
        left, right = 0, 1

        def along_x(place):
            return lambda rows: rows.reshape(2, 2, -1, rows.shape[1])[:, place].reshape(
                -1, rows.shape[1]
            )

        def along_y(place):
            return lambda rows: rows[place * rows.shape[0] // 2 : (place + 1) * rows.shape[0] // 2]

        left_away = make(along_y(1), left, *values).astype(bf16)
        right_away = make(along_x(1), right, *values).astype(bf16)
        left_away, right_away, *values = sync(left_away, right_away, *values)
        left_other, right_other = swap(left_away, "y"), swap(right_away, "x")
        left_mine = make(along_y(0), left, *values).astype(bf16)
        right_mine = make(along_x(0), right, *values).astype(bf16)
        return left_mine, right_mine, left_other, right_other

    def terms_added(self, left_mine, right_mine, left_other, right_other):
        left = left_mine.astype(f32) + left_other.astype(f32)
        right = right_mine.astype(f32) + right_other.astype(f32)
        half = left.shape[0] // 2
        return left[:half], right[:half], left[half:].astype(bf16), right[half:].astype(bf16)

    def terms_second(self, *terms):
        left, right, left_away, right_away = self.terms_added(*terms)
        return left, right, swap(left_away, "x"), swap(right_away, "y")

    def terms_sum(self, left, right, left_x, right_y):
        return jnp.concatenate([left + left_x.astype(f32), right + right_y.astype(f32)], axis=1)

    def sum_along(self, rows, axis):
        shape = rows.shape
        rows = rows.reshape((2, 2, -1) + shape[1:])
        rows = rows + jnp.flip(swap(rows, axis), self.team.index(axis))
        return rows.reshape(shape)

    def sum_rows(self, rows):
        return self.sum_along(self.sum_along(rows, "y"), "x")

    def order(self, mine, other, index, axis):
        first = index == 0
        return jnp.stack([jnp.where(first, mine, other), jnp.where(first, other, mine)], axis)

    def team_columns(self, weight):
        rows = weight.shape[0]
        return weight.reshape(rows, 4, -1).transpose(1, 0, 2)

    def whole_columns(self, parts):
        return spread(parts, [(part, 0) for part in range(4)])

    def send_columns(self, parts):
        return lax.all_to_all(parts, self.team, 0, 0).reshape(-1, parts.shape[2])

    def return_columns(self, block):
        return lax.all_to_all(block.reshape(4, -1, block.shape[1]), self.team, 0, 0)

    def grouped(self, rows):
        return regroup(rows, [spot * 8 + place for place in range(8) for spot in range(4)])

    own_order = [place * 4 + spot for spot in range(4) for place in range(8)]

    def ungrouped(self, rows):
        return regroup(rows, self.own_order)

    def join_group(self, blocks):
        table, pieces = [], []
        for core in range(2):
            for k in range(4):
                unit = blocks[core][k].shape[0] // 64
                table.append(((self.core ^ core) * 4 + (self.z - k) % 4) * unit)
                pieces.append(blocks[core][k])
        return join(*pieces, table=jnp.stack(table).astype(jnp.int32))

    def core_halves(self, values):
        half = values.shape[1] // 2
        return [
            lax.dynamic_slice_in_dim(values, index * half, half, 1)
            for index in (1 - self.core, self.core)
        ]

    def ring_sum(self, k, terms, so_far=None):
        rows = terms[0].shape[0] // 4
        part = (self.z - k) % 4

        def pick_rows(term):
            if isinstance(term, tuple):
                begin = part % 2 * rows
                low, high = (lax.dynamic_slice_in_dim(half, begin, rows, 0) for half in term)
                return jnp.where(part < 2, low, high)
            return lax.dynamic_slice_in_dim(term, part * rows, rows, 0)

        parts = [pick_rows(term).astype(f32) for term in terms]
        return sum(parts if so_far is None else parts + [so_far.astype(f32)])

    def ring_step(self, k, terms, so_far=None):
        return self.shift(self.ring_sum(k, terms, so_far).astype(bf16))

    def small_rows(self, gains, lengths, width):
        small = [jnp.pad(row.astype(bf16), (0, width - row.shape[0])) for row in (*gains, lengths)]
        return jnp.pad(jnp.stack(small), ((0, 16 - len(small)), (0, 0)))

    def small_step(self, small, axis):
        index = self.place[self.every.index(axis)]
        small = self.order(small, swap(small, axis), index, 1)
        return small.reshape(small.shape[0], -1, small.shape[-1])

    def small_end(self, small, count):
        gains = small[:4].reshape(4, -1).astype(f32)
        y, x, c, _, _ = self.place
        ids = [
            (((y ^ dy) * 2 + (x ^ dx)) * 2 + c) * 4 + self.z for dy in range(2) for dx in range(2)
        ]
        lengths = jnp.stack([pick(small[4], i, 0) for i in ids])[:, :count]
        return gains, lengths.astype(jnp.int32)

    def gain_step(self, terms, axis, dim):
        index = self.place[self.every.index(axis)]
        return pick(terms, index, dim) + swap(pick(terms, 1 - index, dim), axis)

    def both_step(self, terms, parts, axis, dim):
        index = self.place[self.every.index(axis)]
        away = pick(terms, 1 - index, dim)
        other = swap(jnp.concatenate([away.reshape(-1), parts.reshape(-1)]), axis)
        terms = pick(terms, index, dim) + other[: away.size].reshape(away.shape)
        return terms, parts + other[away.size :].reshape(parts.shape)

    def own_gains(self, terms):
        terms = terms.reshape(terms.shape[0], 2, 2, 2, -1)
        for index in self.place[2:]:
            terms = pick(terms, index, 1)
        return terms


class Plain:
    def __init__(self, team, group):
        self.team, self.group = team, group
        self.every = (team, group)
        self.size = lax.axis_size(team)
        self.index = lax.axis_index(team)

    def gather_rows(self, rows):
        return lax.all_gather(rows, self.team, axis=0, tiled=True)

    def scatter_rows(self, terms):
        return lax.psum_scatter(terms, self.team, scatter_dimension=0, tiled=True).astype(f32)

    def sum_rows(self, rows):
        return lax.psum(rows, self.team)

    def gather_columns(self, weight):
        rows = weight.shape[0]
        parts = weight.reshape(rows, self.size, -1).transpose(1, 0, 2)
        block = lax.all_to_all(parts, self.team, 0, 0)
        whole = lax.all_gather(block, self.group, axis=1, tiled=True)
        return whole.reshape(-1, block.shape[2])

    def scatter_columns(self, terms):
        terms = terms.reshape(self.size, -1, terms.shape[1])
        block = lax.psum_scatter(terms, self.group, scatter_dimension=1, tiled=True)
        parts = lax.all_to_all(block, self.team, 0, 0)
        return parts.transpose(1, 0, 2).reshape(parts.shape[1], -1).astype(f32)

    def gather_group(self, weight):
        return lax.all_gather(weight, self.group, axis=0, tiled=True)

    def scatter_group(self, terms, axis=0):
        block = lax.psum_scatter(terms, self.group, scatter_dimension=axis, tiled=True)
        return block.astype(f32)


def norm_columns(raw, columns):
    parts = [raw[:, k * columns : (k + 1) * columns] for k in (0, 1)]
    return jnp.stack([jnp.sum(part * part, axis=-1) for part in parts], axis=-1)


def raw_back(raw, scaled, inverse, means, grad_value):
    columns = grad_value.shape[1]
    grads = []
    for which in (0, 1):
        here = slice(which * columns, (which + 1) * columns)
        scale = inverse[:, which : which + 1]
        normed = raw[:, here] * scale
        grad = scale * (scaled[:, here] - normed * means[:, which : which + 1])
        grads.append(grad.astype(bf16))
    return jnp.concatenate(grads + [grad_value], axis=1)


def local_plain(
    plan,
    tokens,
    block_lengths,
    w_query,
    w_key,
    w_value,
    w_out,
    w_gate,
    w_up,
    w_down,
    query_gain,
    key_gain,
    attn_gain,
    mlp_gain,
    cotangent,
):
    width = tokens.shape[1]
    columns = width // plan.size
    live, _ = row_layout(block_lengths)
    live_col = live.astype(f32)[:, None]
    lengths = lax.all_gather(block_lengths, plan.team)
    _, position = jax.vmap(row_layout)(lengths)
    cosine, sine = angles(position)
    gains = jnp.stack([query_gain, key_gain, attn_gain, mlp_gain])
    gains = lax.all_gather(gains, plan.every, axis=1, tiled=True).astype(f32)
    part_gains = lax.dynamic_slice_in_dim(gains[:2], plan.index * columns, columns, axis=1)
    attn_gain_wide, mlp_gain_wide = gains[2], gains[3]
    attn_whole = jnp.concatenate(
        [plan.gather_columns(w) for w in (w_query, w_key, w_value)], axis=1
    )
    out_whole = plan.gather_group(w_out)
    gate_whole = plan.gather_columns(w_gate)
    up_whole = plan.gather_columns(w_up)
    down_whole = plan.gather_group(w_down)

    team_tokens = plan.gather_rows(tokens)
    raw = product(team_tokens, attn_whole)
    inverse = lax.rsqrt(plan.sum_rows(norm_columns(raw, columns)) / width + epsilon)
    turned, mixed_low = attend(lengths, raw, inverse, part_gains, cosine, sine)
    attn_proj = plan.scatter_rows(product(mixed_low, out_whole).astype(bf16))
    attn_normed, attn_inverse = norm_forward(attn_proj, attn_gain_wide)
    hidden = tokens.astype(f32) + attn_normed
    team_hidden = plan.gather_rows(hidden.astype(bf16))
    gate = product(team_hidden, gate_whole)
    upward = product(team_hidden, up_whole)
    sigmoid_gate = jax.nn.sigmoid(gate)
    activated = gate * sigmoid_gate
    inner_low = (activated * upward).astype(bf16)
    down = plan.scatter_rows(product(inner_low, down_whole).astype(bf16))
    down_normed, down_inverse = norm_forward(down, mlp_gain_wide)
    block_out = (live_col * (hidden + down_normed)).astype(bf16)

    grad_out = live_col * cotangent.astype(f32)
    grad_down, term_mlp_gain = norm_back(down, down_inverse, mlp_gain_wide, grad_out)
    team_grad_down = plan.gather_rows(grad_down.astype(bf16))
    grad_w_down = plan.scatter_group(inner_rows(inner_low, team_grad_down).astype(bf16))
    grad_inner = product_tt(team_grad_down, down_whole)
    grad_gate = grad_inner * upward * sigmoid_gate * (1.0 + gate * (1.0 - sigmoid_gate))
    grad_up = grad_inner * activated
    grad_gate, grad_up = grad_gate.astype(bf16), grad_up.astype(bf16)
    grad_w_gate = plan.scatter_columns(inner_rows(team_hidden, grad_gate).astype(bf16))
    grad_w_up = plan.scatter_columns(inner_rows(team_hidden, grad_up).astype(bf16))
    grad_from_mlp = product_tt(grad_gate, gate_whole) + product_tt(grad_up, up_whole)
    grad_hidden = grad_out + plan.scatter_rows(grad_from_mlp.astype(bf16))

    grad_proj, term_attn_gain = norm_back(attn_proj, attn_inverse, attn_gain_wide, grad_hidden)
    team_grad_proj = plan.gather_rows(grad_proj.astype(bf16))
    grad_mixed = product_tt(team_grad_proj, out_whole).astype(bf16)
    grad_w_out = plan.scatter_group(inner_rows(mixed_low, team_grad_proj).astype(bf16))
    scaled, grad_value, means, part_terms = attend_back(
        lengths, raw, turned, inverse, part_gains, cosine, sine, grad_mixed
    )
    means = plan.sum_rows(means) / width
    grad_raw = raw_back(raw, scaled, inverse, means, grad_value)
    grad_w_query, grad_w_key, grad_w_value = (
        plan.scatter_columns(
            inner_rows(team_tokens, grad_raw[:, k * columns : (k + 1) * columns]).astype(bf16)
        )
        for k in range(3)
    )
    grad_from_attn = plan.scatter_rows(product_tt(grad_raw, attn_whole).astype(bf16))
    part_grads = plan.scatter_group(part_terms, 1)
    gain_grads = lax.psum_scatter(
        jnp.stack([term_attn_gain, term_mlp_gain]), plan.every, scatter_dimension=1, tiled=True
    )
    return (
        block_out,
        (grad_hidden + grad_from_attn).astype(bf16),
        grad_w_query,
        grad_w_key,
        grad_w_value,
        grad_w_out,
        grad_w_gate,
        grad_w_up,
        grad_w_down,
        part_grads[0],
        part_grads[1],
        gain_grads[0],
        gain_grads[1],
    )


def local_cube(
    tokens,
    block_lengths,
    w_query,
    w_key,
    w_value,
    w_out,
    w_gate,
    w_up,
    w_down,
    query_gain,
    key_gain,
    attn_gain,
    mlp_gain,
    cotangent,
):
    plan = Cube()
    width = tokens.shape[1]
    columns = width // plan.size
    live, _ = row_layout(block_lengths)
    live_col = live.astype(f32)[:, None]

    def group_whole(block):
        return lax.all_gather(block, plan.group, axis=0, tiled=True)

    shard = query_gain.shape[0]
    small = plan.small_rows((query_gain, key_gain, attn_gain, mlp_gain), block_lengths, width)
    attn_parts = jnp.concatenate([plan.team_columns(w) for w in (w_query, w_key, w_value)], axis=2)
    attn_parts, own, out_rows, down0 = sync(attn_parts, tokens, w_out, w_down)
    packed = group_whole(jnp.concatenate([out_rows, small])).reshape(8, -1, width)
    down1 = plan.shift(down0)
    rows = plan.rows_first(plan.grouped(own))
    attn0 = plan.send_columns(attn_parts)
    attn0, w_gate, *rows = sync(attn0, w_gate, *rows)
    attn1, attn0c = plan.shift(attn0), swap(attn0, "c")
    rows = plan.rows_second(*rows)
    attn1, attn0c, down1, w_gate, *rows = sync(attn1, attn0c, down1, w_gate, *rows)
    gate = plan.send_columns(plan.team_columns(w_gate))
    attn2, attn1c = plan.shift(attn1), swap(attn1, "c")
    team_tokens = join(*rows)
    attn2, attn1c, gate, w_up, team_tokens, packed = sync(
        attn2, attn1c, gate, w_up, team_tokens, packed
    )
    gate_whole = group_whole(gate)
    up = plan.send_columns(plan.team_columns(w_up))
    attn3, attn2c = plan.shift(attn2), swap(attn2, "c")
    out_whole = packed[:, : w_out.shape[0]].reshape(-1, width)
    small = packed[:, w_out.shape[0] : w_out.shape[0] + 5, :shard].transpose(1, 0, 2)
    small = plan.small_step(plan.small_step(small, "x"), "y")
    attn3, attn2c, small, out_whole, up = sync(attn3, attn2c, small, out_whole, up)
    up_whole = group_whole(up)
    gains, lengths = plan.small_end(small, block_lengths.shape[0])
    _, position = jax.vmap(row_layout)(lengths)
    cosine, sine = angles(position)
    part_gains = lax.dynamic_slice_in_dim(gains[:2], plan.index * columns, columns, axis=1)
    attn_gain_wide, mlp_gain_wide = gains[2], gains[3]
    attn3c = swap(attn3, "c")
    attn_whole = plan.join_group([[attn0, attn1, attn2, attn3], [attn0c, attn1c, attn2c, attn3c]])

    raw = product(team_tokens, attn_whole)
    inverse = lax.rsqrt(plan.sum_rows(norm_columns(raw, columns)) / width + epsilon)
    turned, mixed_low = attend(lengths, raw, inverse, part_gains, cosine, sine)
    mixed_low, down1, team_tokens = sync(mixed_low, down1, team_tokens)
    down2, down0c, down1c = plan.shift(down1), swap(w_down, "c"), swap(down1, "c")
    half = width // 2

    def by_columns(rows, side, left, right):
        return product(rows(left), right[:, side * half : (side + 1) * half])

    def by_rows(rows, side, left, right):
        return product_tt(rows(left), right[side * half : (side + 1) * half])

    terms = plan.terms_first(by_columns, mixed_low, out_whole)
    terms = plan.terms_second(*terms)
    attn_proj = plan.terms_sum(*terms)
    attn_normed, attn_inverse = norm_forward(attn_proj, attn_gain_wide)
    hidden = tokens.astype(f32) + attn_normed

    rows = plan.rows_first(plan.grouped(hidden.astype(bf16)))
    rows = plan.rows_second(*rows)
    team_hidden = join(*rows)
    gate = product(team_hidden, gate_whole).astype(bf16)
    hidden_parts = plan.core_halves(team_hidden)
    gate, down2, *hidden_parts = sync(gate, down2, *hidden_parts)
    down3, down2c = plan.shift(down2), swap(down2, "c")
    upward = product(team_hidden, up_whole).astype(bf16)
    inner_low = (jax.nn.silu(gate.astype(f32)) * upward.astype(f32)).astype(bf16)
    inner_low, down3 = sync(inner_low, down3)
    down3c = swap(down3, "c")
    down_whole = plan.join_group([[w_down, down1, down2, down3], [down0c, down1c, down2c, down3c]])
    terms = plan.terms_first(by_columns, inner_low, down_whole)
    *inner_parts, left, right, left_y, right_x = sync(*plan.core_halves(inner_low), *terms)
    down = plan.terms_sum(*plan.terms_second(left, right, left_y, right_x))
    down_normed, down_inverse = norm_forward(down, mlp_gain_wide)
    block_out = (live_col * (hidden + down_normed)).astype(bf16)

    grad_out = live_col * cotangent.astype(f32)
    grad_down, term_mlp_gain = norm_back(down, down_inverse, mlp_gain_wide, grad_out)
    rows = plan.rows_second(*plan.rows_first(grad_down.astype(bf16)))
    team_grad_down = join(*rows)

    def terms_of(left, right):
        return inner_rows(left, right).astype(bf16)

    def summed(mine, other):
        return (mine.astype(f32) + other.astype(f32)).astype(bf16)

    down_other = swap(terms_of(inner_parts[0], team_grad_down), "c")
    down_mine = terms_of(inner_parts[1], team_grad_down)
    team_grad_down, down_mine, down_other = sync(team_grad_down, down_mine, down_other)
    down_terms = summed(down_mine, down_other)
    gain_shape = (2, 2, 2, 2, 2, -1)
    team_grad_down, down_terms, mlp_terms = sync(team_grad_down, down_terms, term_mlp_gain)
    mlp_terms = plan.gain_step(mlp_terms.reshape(gain_shape), "c", 2)
    team_grad_down, mlp_terms = sync(team_grad_down, mlp_terms)
    grad_w_down = lax.psum_scatter(down_terms, plan.z_axes, scatter_dimension=0, tiled=True)
    grad_inner = product_tt(team_grad_down, down_whole)
    gate_wide = gate.astype(f32)
    sigmoid_gate = jax.nn.sigmoid(gate_wide)
    slope = sigmoid_gate * (1.0 + gate_wide * (1.0 - sigmoid_gate))
    grad_gate = grad_inner * upward.astype(f32) * slope
    grad_up = grad_inner * (gate_wide * sigmoid_gate)
    grad_gate, grad_up, *hidden_parts = sync(
        grad_gate.astype(bf16), grad_up.astype(bf16), *hidden_parts
    )
    gate_away = terms_of(hidden_parts[0], grad_gate)
    gate_away, grad_up, other_part = sync(gate_away, grad_up, hidden_parts[0])
    gate_other = swap(gate_away, "c")
    up_away = terms_of(other_part, grad_up)
    up_away, grad_gate, grad_up = sync(up_away, grad_gate, grad_up)
    up_other = swap(up_away, "c")
    hidden_part = hidden_parts[1]

    def from_mlp(rows, side, gate_grad, up_grad):
        return by_rows(rows, side, gate_grad, gate_whole) + by_rows(rows, side, up_grad, up_whole)

    terms = plan.terms_first(from_mlp, grad_gate, grad_up)
    left, right, left_y, right_x = terms
    left, right, grad_gate, grad_up, hidden_part, own_tokens, own_mixed = sync(
        left, right, grad_gate, grad_up, hidden_part, team_tokens, mixed_low
    )
    terms = left, right, left_y, right_x
    gate_terms = summed(terms_of(hidden_part, grad_gate), gate_other)
    late_parts = (*plan.core_halves(own_tokens), *plan.core_halves(own_mixed))
    gate_terms, grad_up, token_other, token_mine, mixed_other, mixed_mine, *terms = sync(
        gate_terms, grad_up, *late_parts, *terms
    )
    gate_block = lax.psum_scatter(gate_terms, plan.z_axes, scatter_dimension=0, tiled=True)
    terms = plan.terms_second(*terms)
    grad_up, *terms = sync(grad_up, *terms)

    grad_hidden, grad_proj, term_attn_gain = proj_back(
        plan.own_order, *terms, live_col, cotangent, attn_proj, attn_inverse, attn_gain_wide
    )
    rows = plan.rows_first(grad_proj)
    up_mine = terms_of(hidden_part, grad_up)
    up_mine, up_other, grad_w_down, *rows = sync(up_mine, up_other, grad_w_down, *rows)
    rows = plan.rows_second(*rows)
    up_terms = summed(up_mine, up_other)
    up_terms, gate_block, *rows = sync(up_terms, gate_block, *rows)
    up_block = lax.psum_scatter(up_terms, plan.z_axes, scatter_dimension=0, tiled=True)
    team_grad_proj = join(*rows)
    grad_mixed = product_tt(team_grad_proj, out_whole).astype(bf16)
    scaled, grad_value, means, part_terms = attend_back(
        lengths, raw, turned, inverse, part_gains, cosine, sine, grad_mixed
    )
    attn_gain_terms = plan.gain_step(term_attn_gain.reshape(gain_shape), "c", 2)
    gain_terms = jnp.stack([attn_gain_terms, mlp_terms])
    gate_block = plan.return_columns(gate_block)
    means, part_terms, gain_terms, team_grad_proj, gate_block = sync(
        means, part_terms, gain_terms, team_grad_proj, gate_block
    )
    out_away = terms_of(mixed_other, team_grad_proj)
    means = plan.sum_along(means, "y")
    means, out_away, team_grad_proj = sync(means, out_away, team_grad_proj)
    out_mine = terms_of(mixed_mine, team_grad_proj)
    means = plan.sum_along(means, "x") / width
    means, out_mine = sync(means, out_mine)
    grad_raw = raw_back(raw, scaled, inverse, means, grad_value)
    part = token_other.shape[1] // 2
    attn_other = [swap(terms_of(token_other[:, :part], grad_raw), "c")]
    attn_other += [swap(terms_of(token_other[:, part:], grad_raw), "c")]
    out_other = swap(out_away, "c")
    attn_mine = terms_of(token_mine, grad_raw)
    part_terms = part_terms + swap(part_terms, "c")
    grad_raw, attn_mine, out_mine, out_other, part_terms, gain_terms, *attn_other = sync(
        grad_raw, attn_mine, out_mine, out_other, part_terms, gain_terms, *attn_other
    )
    attn_terms, out_terms = (attn_mine, tuple(attn_other)), (out_mine, out_other)
    attn_sum, out_sum = plan.ring_step(1, attn_terms), plan.ring_step(1, out_terms)
    terms = plan.terms_first(by_rows, grad_raw, attn_whole)
    gain_terms, part_terms = plan.both_step(gain_terms, part_terms, "zh", 3)
    attn_sum, out_sum, part_terms, gain_terms, *terms = sync(
        attn_sum, out_sum, part_terms, gain_terms, *terms
    )
    attn_sum = plan.ring_sum(2, attn_terms, attn_sum).astype(bf16)
    out_sum = plan.ring_sum(2, out_terms, out_sum).astype(bf16)
    attn_sum, out_sum, part_terms, gain_terms, *terms = sync(
        attn_sum, out_sum, part_terms, gain_terms, *terms
    )
    attn_sum, out_sum = plan.shift(attn_sum), plan.shift(out_sum)
    gain_terms, part_terms = plan.both_step(gain_terms, part_terms, "zl", 3)
    up_block = plan.return_columns(up_block)
    terms = plan.terms_added(*terms)
    attn_sum, out_sum, gain_terms, part_terms, up_block, *terms = sync(
        attn_sum, out_sum, gain_terms, part_terms, up_block, *terms
    )
    attn_sum = plan.ring_sum(3, attn_terms, attn_sum).astype(bf16)
    out_sum = plan.ring_sum(3, out_terms, out_sum).astype(bf16)
    attn_sum, out_sum, gate_block, up_block, left, right, left_away, right_away = sync(
        attn_sum, out_sum, gate_block, up_block, *terms
    )
    attn_sum, out_sum = plan.shift(attn_sum), plan.shift(out_sum)
    left_x, right_y = swap(left_away, "x"), swap(right_away, "y")
    grad_w_gate, grad_w_up = plan.whole_columns(gate_block), plan.whole_columns(up_block)
    gain_terms = plan.gain_step(gain_terms, "x", 2)
    part_grads = plan.own_gains(part_terms)
    attn_sum, out_sum, gain_terms, part_grads, grad_w_gate, grad_w_up, left_x, right_y = sync(
        attn_sum, out_sum, gain_terms, part_grads, grad_w_gate, grad_w_up, left_x, right_y
    )
    attn_sum = plan.ring_sum(0, attn_terms, attn_sum).astype(bf16)
    attn_sum, out_sum, gain_terms, left_x, right_y = sync(
        attn_sum, out_sum, gain_terms, left_x, right_y
    )
    grad_tokens = tokens_end(plan.own_order, left, right, left_x, right_y, grad_hidden)
    attn_block = plan.return_columns(attn_sum)
    gain_terms = plan.gain_step(gain_terms, "y", 1)
    grad_w_out = plan.ring_sum(0, out_terms, out_sum)
    attn_block, grad_w_out, gain_terms, grad_tokens = sync(
        attn_block, grad_w_out, gain_terms, grad_tokens
    )
    grad_w_query, grad_w_key, grad_w_value = spread_three(attn_block)
    return (
        block_out,
        grad_tokens,
        grad_w_query,
        grad_w_key,
        grad_w_value,
        grad_w_out,
        grad_w_gate,
        grad_w_up,
        grad_w_down.astype(f32),
        part_grads[0],
        part_grads[1],
        gain_terms[0],
        gain_terms[1],
    )


def solution(mesh):
    if tuple(mesh.shape.values()) == (8, 4):
        mesh = Mesh(mesh.devices.reshape(2, 2, 2, 2, 2), Cube.every)
        every, step = Cube.every, local_cube
    else:
        every = tuple(mesh.axis_names)

        def step(*arrays):
            return local_plain(Plain(*every), *arrays)

    rows, line = P(every, None), P(every)
    return jax.shard_map(
        step,
        mesh=mesh,
        in_specs=(rows, line) + (rows,) * 7 + (line,) * 4 + (rows,),
        out_specs=(rows,) * 9 + (line,) * 4,
        check_vma=False,
    )
```

```python
import functools

import jax
import jax.numpy as jnp
from jax import lax
from jax.experimental import pallas as pl
from jax.experimental.pallas import tpu as pltpu
from jax.sharding import Mesh, PartitionSpec as P

HEAD_DIM = 128
BLOCK = 128

epsilon = 1e-06
rope_base = 500000.0
f32 = jnp.float32
bf16 = jnp.bfloat16
NO_COST = pl.CostEstimate(flops=0, bytes_accessed=0, transcendentals=0)


def product(left, right):
    return jnp.dot(left, right, preferred_element_type=f32)


def product_tt(left, right):
    return lax.dot_general(left, right, (((1,), (1,)), ((), ())), preferred_element_type=f32)


def inner_rows(left, right):
    return lax.dot_general(left, right, (((0,), (0,)), ((), ())), preferred_element_type=f32)


def norm_forward(values, gain):
    inverse = lax.rsqrt(jnp.mean(values * values, axis=-1, keepdims=True) + epsilon)
    return (values * inverse * gain, inverse)


def norm_back(values, inverse, gain, incoming):
    normed = values * inverse
    scaled = incoming * gain
    gain_term = jnp.sum(incoming * normed, axis=0)
    back = inverse * (scaled - normed * jnp.mean(scaled * normed, axis=-1, keepdims=True))
    return (back, gain_term)


def angles(position):
    half = HEAD_DIM // 2
    freq = rope_base ** (-jnp.arange(half, dtype=f32) / half)
    angle = position.astype(f32).reshape(-1, 1) * freq
    cosine, sine = jnp.cos(angle), jnp.sin(angle)
    return jnp.concatenate([cosine, cosine], axis=1), jnp.concatenate([-sine, sine], axis=1)


def row_layout(lengths):
    nblock = lengths.shape[0]
    row_ids = jnp.arange(nblock * BLOCK, dtype=jnp.int32)
    begin = jnp.arange(nblock, dtype=jnp.int32) * BLOCK
    cover = (
        (lengths[None, :] > 0)
        & (row_ids[:, None] >= begin[None, :])
        & (row_ids[:, None] < begin[None, :] + lengths[None, :])
    )
    live = jnp.any(cover, axis=1)
    owner = jnp.sum(jnp.where(cover, begin[None, :], 0), axis=1)
    return (live, row_ids - owner)


def allowed_keys(lengths_ref, device, nrows):
    rows = lax.broadcasted_iota(jnp.int32, (nrows, nrows), 0)
    keys = lax.broadcasted_iota(jnp.int32, (nrows, nrows), 1)

    def number(ids):
        found = -1 - ids
        for block in range(nrows // BLOCK):
            begin, length = block * BLOCK, lengths_ref[device, block]
            found = jnp.where((ids >= begin) & (ids < begin + length), begin, found)
        return found

    return (number(rows) == number(keys)) & (keys <= rows)


def turn(values, cosine, sine):
    return values * cosine + pltpu.roll(values, HEAD_DIM // 2, 1) * sine


def probabilities(query, key, allowed):
    scores = product_tt(query, key) * HEAD_DIM ** (-0.5)
    scores = jnp.where(allowed, scores, -1e30)
    powers = jnp.exp(scores - jnp.max(scores, axis=-1, keepdims=True))
    return powers * (1.0 / jnp.sum(powers, axis=-1, keepdims=True))


def attend_kernel(
    lengths_ref, raw_ref, inverse_ref, gains_ref, cosine_ref, sine_ref, turned_ref, mixed_ref
):
    nrows, columns = mixed_ref.shape
    allowed = allowed_keys(lengths_ref, pl.program_id(0), nrows)
    cosine, sine = cosine_ref[...], sine_ref[...]
    for head in range(columns // HEAD_DIM):
        here = slice(head * HEAD_DIM, (head + 1) * HEAD_DIM)
        turned = []
        for which in range(2):
            there = slice(which * columns + here.start, which * columns + here.stop)
            normed = raw_ref[:, there] * inverse_ref[:, which : which + 1]
            rotated = turn(normed * gains_ref[which : which + 1, here], cosine, sine).astype(bf16)
            turned_ref[:, there] = rotated
            turned.append(rotated)
        there = slice(2 * columns + here.start, 2 * columns + here.stop)
        value = raw_ref[:, there].astype(bf16)
        turned_ref[:, there] = value
        probs = probabilities(turned[0], turned[1], allowed)
        mixed_ref[:, here] = product(probs.astype(bf16), value).astype(bf16)


def attend_back_kernel(
    lengths_ref, raw_ref, turned_ref, inverse_ref, gains_ref, cosine_ref, sine_ref, grad_ref,
    scaled_ref, grad_value_ref, means_ref, terms_ref,
):
    nrows, columns = grad_ref.shape
    device = pl.program_id(0)
    allowed = allowed_keys(lengths_ref, device, nrows)
    cosine, sine = cosine_ref[...], sine_ref[...]

    @pl.when(device == 0)
    def _():
        terms_ref[...] = jnp.zeros_like(terms_ref)

    sums = [0.0, 0.0]
    for head in range(columns // HEAD_DIM):
        here = slice(head * HEAD_DIM, (head + 1) * HEAD_DIM)
        spots = [slice(k * columns + here.start, k * columns + here.stop) for k in range(3)]
        query, key, value = (turned_ref[:, spot] for spot in spots)
        incoming = grad_ref[:, here]
        probs = probabilities(query, key, allowed)
        grad_probs = product_tt(incoming, value)
        inner = jnp.sum(probs * grad_probs, axis=-1, keepdims=True)
        grad_scores = (probs * (grad_probs - inner)).astype(bf16)
        grad_value_ref[:, here] = inner_rows(probs.astype(bf16), incoming).astype(bf16)
        back = (product(grad_scores, key), inner_rows(grad_scores, query))
        for which in range(2):
            turned = turn(back[which] * HEAD_DIM ** (-0.5), cosine, -sine)
            normed = raw_ref[:, spots[which]] * inverse_ref[:, which : which + 1]
            terms_ref[which : which + 1, here] += jnp.sum(turned * normed, axis=0, keepdims=True)
            scaled = turned * gains_ref[which : which + 1, here]
            scaled_ref[:, spots[which]] = scaled
            sums[which] = sums[which] + jnp.sum(scaled * normed, axis=-1, keepdims=True)
    means_ref[...] = jnp.concatenate(sums, axis=1)


def attend_specs(nrows, columns):
    def rows(wide):
        return pl.BlockSpec((nrows, wide), lambda b: (b, 0))

    lengths = pl.BlockSpec(memory_space=pltpu.SMEM)
    gains = pl.BlockSpec((2, columns), lambda b: (0, 0))
    return rows, lengths, gains


def attend(lengths, raw, inverse, gains, cosine, sine):
    size, nrows = lengths.shape[0], raw.shape[0] // lengths.shape[0]
    columns = raw.shape[1] // 3
    rows, whole, gain = attend_specs(nrows, columns)
    return pl.pallas_call(
        attend_kernel,
        grid=(size,),
        in_specs=[whole, rows(3 * columns), rows(2), gain, rows(HEAD_DIM), rows(HEAD_DIM)],
        out_specs=[rows(3 * columns), rows(columns)],
        out_shape=[
            jax.ShapeDtypeStruct(raw.shape, bf16),
            jax.ShapeDtypeStruct((raw.shape[0], columns), bf16),
        ],
        cost_estimate=NO_COST,
    )(lengths, raw, inverse, gains, cosine, sine)


def attend_back(lengths, raw, turned, inverse, gains, cosine, sine, grad):
    size, nrows = lengths.shape[0], raw.shape[0] // lengths.shape[0]
    columns = raw.shape[1] // 3
    rows, whole, gain = attend_specs(nrows, columns)
    return pl.pallas_call(
        attend_back_kernel,
        grid=(size,),
        in_specs=[
            whole, rows(3 * columns), rows(3 * columns), rows(2), gain,
            rows(HEAD_DIM), rows(HEAD_DIM), rows(columns),
        ],
        out_specs=[rows(2 * columns), rows(columns), rows(2), gain],
        out_shape=[
            jax.ShapeDtypeStruct((raw.shape[0], 2 * columns), f32),
            jax.ShapeDtypeStruct((raw.shape[0], columns), bf16),
            jax.ShapeDtypeStruct((raw.shape[0], 2), f32),
            jax.ShapeDtypeStruct((2, columns), f32),
        ],
        cost_estimate=NO_COST,
    )(lengths, raw, turned, inverse, gains, cosine, sine, grad)


def swap(value, axis):
    return lax.ppermute(value, axis, ((0, 1), (1, 0)))


def sync(*values):
    return lax.optimization_barrier(values)


def pick(value, index, axis):
    return lax.dynamic_index_in_dim(value, index, axis, keepdims=False)


def join_kernel(table_ref, *refs):
    pieces, out, held, sems = refs[:-3], refs[-3], refs[-2], refs[-1]
    loads, stores = [], []
    for k, piece in enumerate(pieces):
        here = pl.ds(pl.multiple_of(table_ref[k] * 64, 64), piece.shape[0])
        loads.append(pltpu.make_async_copy(piece, held.at[here], sems.at[0, k]))
        stores.append(pltpu.make_async_copy(held.at[here], out.at[here], sems.at[1, k]))
        loads[-1].start()
    for load, store in zip(loads, stores):
        load.wait()
        store.start()
    for store in stores:
        store.wait()


def join(*pieces, table=None):
    if table is None:
        begins = [sum(piece.shape[0] for piece in pieces[:k]) // 64 for k in range(len(pieces))]
        table = jnp.array(begins, jnp.int32)
    shape = (sum(piece.shape[0] for piece in pieces), pieces[0].shape[1])
    return pl.pallas_call(
        join_kernel,
        in_specs=[pl.BlockSpec(memory_space=pltpu.SMEM)]
        + [pl.BlockSpec(memory_space=pl.ANY)] * len(pieces),
        out_specs=pl.BlockSpec(memory_space=pl.ANY),
        out_shape=jax.ShapeDtypeStruct(shape, pieces[0].dtype),
        scratch_shapes=[
            pltpu.VMEM(shape, pieces[0].dtype),
            pltpu.SemaphoreType.DMA((2, len(pieces))),
        ],
        compiler_params=pltpu.CompilerParams(vmem_limit_bytes=32 * 2**20),
        cost_estimate=NO_COST,
    )(table, *pieces)


def regroup_kernel(halves, in_ref, out_ref):
    for tile in range(len(halves) // 2):
        parts = [in_ref[:, half * 64 : (half + 1) * 64] for half in halves[2 * tile : 2 * tile + 2]]
        out_ref[:, tile * 128 : (tile + 1) * 128] = jnp.concatenate(parts, axis=1)


def regroup(value, halves):
    rows, width = value.shape
    block = pl.BlockSpec((rows // 2, width), lambda k: (k, 0))
    return pl.pallas_call(
        functools.partial(regroup_kernel, halves),
        grid=(2,),
        in_specs=[block],
        out_specs=block,
        out_shape=jax.ShapeDtypeStruct(value.shape, value.dtype),
        cost_estimate=NO_COST,
    )(value)


def spread_kernel(order, parts_ref, out_ref):
    wide = out_ref.shape[1] // len(order)
    for block, (part, column) in enumerate(order):
        here = slice(block * wide, (block + 1) * wide)
        out_ref[:, here] = parts_ref[part, :, column * wide : (column + 1) * wide].astype(f32)


def spread(parts, order):
    shape = (parts.shape[1], parts.shape[0] * parts.shape[2])
    return pl.pallas_call(
        functools.partial(spread_kernel, order),
        in_specs=[pl.BlockSpec(memory_space=pltpu.VMEM)],
        out_specs=pl.BlockSpec(memory_space=pltpu.VMEM),
        out_shape=jax.ShapeDtypeStruct(shape, f32),
        cost_estimate=NO_COST,
    )(parts)


def ordered(blocks, *refs):
    left = sum(ref[...].astype(f32) for ref in refs[0::2])
    right = sum(ref[...].astype(f32) for ref in refs[1::2])
    half = left.shape[1] // 64
    parts = [(left, k) if k < half else (right, k - half) for k in blocks]
    return jnp.concatenate([part[:, k * 64 : (k + 1) * 64] for part, k in parts], axis=1)


def tokens_kernel(blocks, *refs):
    *sides, hidden_ref, out_ref = refs
    out_ref[...] = (ordered(blocks, *sides) + hidden_ref[...]).astype(bf16)


def tokens_end(blocks, sides, hidden):
    rows, width = hidden.shape
    side = pl.BlockSpec((rows // 4, width // 2), lambda k: (k, 0))
    whole = pl.BlockSpec((rows // 4, width), lambda k: (k, 0))
    return pl.pallas_call(
        functools.partial(tokens_kernel, blocks),
        grid=(4,),
        in_specs=[side] * len(sides) + [whole],
        out_specs=whole,
        out_shape=jax.ShapeDtypeStruct((rows, width), bf16),
        cost_estimate=NO_COST,
    )(*sides, hidden)


def proj_back_kernel(blocks, *refs):
    *sides, live_ref, cotangent_ref, proj_ref, inverse_ref, gain_ref = refs[:-3]
    hidden_ref, grad_ref, term_ref = refs[-3:]
    total = ordered(blocks, *sides)
    total += live_ref[...] * cotangent_ref[...].astype(f32)
    hidden_ref[...] = total
    normed = proj_ref[...] * inverse_ref[...]
    term = jnp.sum(total * normed, axis=0, keepdims=True)
    scaled = total * gain_ref[...]
    mean = jnp.mean(scaled * normed, axis=-1, keepdims=True)
    grad_ref[...] = (inverse_ref[...] * (scaled - normed * mean)).astype(bf16)
    first = pl.program_id(0) == 0
    term_ref[...] = jnp.where(first, term, term_ref[...] + term)


def proj_back(blocks, sides, live, cotangent, proj, inverse, gain):
    rows, width = proj.shape
    side = pl.BlockSpec((rows // 4, width // 2), lambda k: (k, 0))
    whole = pl.BlockSpec((rows // 4, width), lambda k: (k, 0))
    column = pl.BlockSpec((rows // 4, 1), lambda k: (k, 0))
    line = pl.BlockSpec((1, width), lambda k: (0, 0))
    hidden, grad, term = pl.pallas_call(
        functools.partial(proj_back_kernel, blocks),
        grid=(4,),
        in_specs=[side] * len(sides) + [column, whole, whole, column, line],
        out_specs=[whole, whole, line],
        out_shape=[
            jax.ShapeDtypeStruct((rows, width), f32),
            jax.ShapeDtypeStruct((rows, width), bf16),
            jax.ShapeDtypeStruct((1, width), f32),
        ],
        cost_estimate=NO_COST,
    )(*sides, live, cotangent, proj, inverse, gain.reshape(1, width))
    return hidden, grad, term[0]


def spread_three_kernel(parts_ref, *out_refs):
    columns = parts_ref.shape[2] // 3
    for which, out_ref in enumerate(out_refs):
        there = slice(which * columns, (which + 1) * columns)
        for part in range(parts_ref.shape[0]):
            here = slice(part * columns, (part + 1) * columns)
            out_ref[:, here] = parts_ref[part, :, there].astype(f32)


def spread_three(parts):
    shape = (parts.shape[1], parts.shape[0] * parts.shape[2] // 3)
    return pl.pallas_call(
        spread_three_kernel,
        in_specs=[pl.BlockSpec(memory_space=pltpu.VMEM)],
        out_specs=[pl.BlockSpec(memory_space=pltpu.VMEM)] * 3,
        out_shape=[jax.ShapeDtypeStruct(shape, f32)] * 3,
        cost_estimate=NO_COST,
    )(parts)


class Cube:
    every = ("y", "x", "c", "zh", "zl")
    team = ("y", "x")
    z_axes = ("zh", "zl")
    group = ("c", "zh", "zl")

    def __init__(self):
        self.place = [lax.axis_index(axis) for axis in self.every]
        self.core = self.place[2]
        self.z = lax.axis_index(self.z_axes)
        self.size = 4
        self.index = lax.axis_index(self.team)

    def shift(self, value):
        return lax.ppermute(value, self.z_axes, ((0, 1), (1, 2), (2, 3), (3, 0)))

    def rows_first(self, rows):
        half = rows.shape[0] // 2
        top, low = rows[:half], rows[half:]
        return top, low, swap(top, "x"), swap(low, "y")

    def rows_second(self, top, low, top_x, low_y):
        top_y, low_x = swap(top, "y"), swap(low, "x")
        return top, low, top_x, low_x, top_y, low_y, swap(top_x, "y"), swap(low_y, "x")

    def terms_first(self, make, *values):
        left, right = 0, 1

        def along_x(place):
            return lambda rows: rows.reshape(2, 2, -1, rows.shape[1])[:, place].reshape(
                -1, rows.shape[1]
            )

        def along_y(place):
            return lambda rows: rows[place * rows.shape[0] // 2 : (place + 1) * rows.shape[0] // 2]

        left_away = make(along_y(1), left, *values).astype(bf16)
        right_away = make(along_x(1), right, *values).astype(bf16)
        left_away, right_away, *values = sync(left_away, right_away, *values)
        left_other, right_other = swap(left_away, "y"), swap(right_away, "x")
        left_mine = make(along_y(0), left, *values).astype(bf16)
        right_mine = make(along_x(0), right, *values).astype(bf16)
        return left_mine, right_mine, left_other, right_other

    def terms_added(self, left_mine, right_mine, left_other, right_other):
        half = left_mine.shape[0] // 2
        left_away = left_mine[half:].astype(f32) + left_other[half:].astype(f32)
        right_away = right_mine[half:].astype(f32) + right_other[half:].astype(f32)
        stay = (left_mine, right_mine, left_other, right_other)
        return (*stay, left_away.astype(bf16), right_away.astype(bf16))

    def terms_second(self, *terms):
        *stay, left_away, right_away = self.terms_added(*terms)
        return (*stay, swap(left_away, "x"), swap(right_away, "y"))

    def terms_sum(self, left_mine, right_mine, left_other, right_other, left_x, right_y):
        half = left_x.shape[0]
        left = (left_mine[:half], left_other[:half], left_x)
        right = (right_mine[:half], right_other[:half], right_y)
        sums = [sum(part.astype(f32) for part in parts) for parts in (left, right)]
        return jnp.concatenate(sums, axis=1)

    def sum_along(self, rows, axis):
        shape = rows.shape
        rows = rows.reshape((2, 2, -1) + shape[1:])
        rows = rows + jnp.flip(swap(rows, axis), self.team.index(axis))
        return rows.reshape(shape)

    def sum_rows(self, rows):
        return self.sum_along(self.sum_along(rows, "y"), "x")

    def order(self, mine, other, index, axis):
        first = index == 0
        return jnp.stack([jnp.where(first, mine, other), jnp.where(first, other, mine)], axis)

    def team_columns(self, weight):
        rows = weight.shape[0]
        return weight.reshape(rows, 4, -1).transpose(1, 0, 2)

    def whole_columns(self, parts):
        return spread(parts, [(part, 0) for part in range(4)])

    def send_columns(self, parts):
        return lax.all_to_all(parts, self.team, 0, 0).reshape(-1, parts.shape[2])

    def return_columns(self, block):
        return lax.all_to_all(block.reshape(4, -1, block.shape[1]), self.team, 0, 0)

    def grouped(self, rows):
        return regroup(rows, [spot * 8 + place for place in range(8) for spot in range(4)])

    own_order = [place * 4 + spot for spot in range(4) for place in range(8)]

    def ungrouped(self, rows):
        return regroup(rows, self.own_order)

    def join_group(self, blocks):
        table, pieces = [], []
        for core in range(2):
            for k in range(4):
                unit = blocks[core][k].shape[0] // 64
                table.append(((self.core ^ core) * 4 + (self.z - k) % 4) * unit)
                pieces.append(blocks[core][k])
        return join(*pieces, table=jnp.stack(table).astype(jnp.int32))

    def core_halves(self, values):
        half = values.shape[1] // 2
        return [
            lax.dynamic_slice_in_dim(values, index * half, half, 1)
            for index in (1 - self.core, self.core)
        ]

    def ring_sum(self, k, terms, so_far=None):
        rows = terms[0].shape[0] // 4
        part = (self.z - k) % 4

        def pick_rows(term):
            if isinstance(term, tuple):
                begin = part % 2 * rows
                low, high = (lax.dynamic_slice_in_dim(half, begin, rows, 0) for half in term)
                return jnp.where(part < 2, low, high)
            return lax.dynamic_slice_in_dim(term, part * rows, rows, 0)

        parts = [pick_rows(term).astype(f32) for term in terms]
        return sum(parts if so_far is None else parts + [so_far.astype(f32)])

    def ring_step(self, k, terms, so_far=None):
        return self.shift(self.ring_sum(k, terms, so_far).astype(bf16))

    def small_rows(self, gains, lengths, width):
        small = [jnp.pad(row.astype(bf16), (0, width - row.shape[0])) for row in (*gains, lengths)]
        return jnp.pad(jnp.stack(small), ((0, 16 - len(small)), (0, 0)))

    def small_step(self, small, axis):
        index = self.place[self.every.index(axis)]
        small = self.order(small, swap(small, axis), index, 1)
        return small.reshape(small.shape[0], -1, small.shape[-1])

    def small_end(self, small, count):
        gains = small[:4].reshape(4, -1).astype(f32)
        y, x, c, _, _ = self.place
        ids = [
            (((y ^ dy) * 2 + (x ^ dx)) * 2 + c) * 4 + self.z for dy in range(2) for dx in range(2)
        ]
        lengths = jnp.stack([pick(small[4], i, 0) for i in ids])[:, :count]
        return gains, lengths.astype(jnp.int32)

    def gain_step(self, terms, axis, dim):
        index = self.place[self.every.index(axis)]
        return pick(terms, index, dim) + swap(pick(terms, 1 - index, dim), axis)

    def both_step(self, terms, parts, axis, dim):
        index = self.place[self.every.index(axis)]
        away = pick(terms, 1 - index, dim)
        other = swap(jnp.concatenate([away.reshape(-1), parts.reshape(-1)]), axis)
        terms = pick(terms, index, dim) + other[: away.size].reshape(away.shape)
        return terms, parts + other[away.size :].reshape(parts.shape)

    def own_gains(self, terms):
        terms = terms.reshape(terms.shape[0], 2, 2, 2, -1)
        for index in self.place[2:]:
            terms = pick(terms, index, 1)
        return terms


class Plain:
    def __init__(self, team, group):
        self.team, self.group = team, group
        self.every = (team, group)
        self.size = lax.axis_size(team)
        self.index = lax.axis_index(team)

    def gather_rows(self, rows):
        return lax.all_gather(rows, self.team, axis=0, tiled=True)

    def scatter_rows(self, terms):
        return lax.psum_scatter(terms, self.team, scatter_dimension=0, tiled=True).astype(f32)

    def sum_rows(self, rows):
        return lax.psum(rows, self.team)

    def gather_columns(self, weight):
        rows = weight.shape[0]
        parts = weight.reshape(rows, self.size, -1).transpose(1, 0, 2)
        block = lax.all_to_all(parts, self.team, 0, 0)
        whole = lax.all_gather(block, self.group, axis=1, tiled=True)
        return whole.reshape(-1, block.shape[2])

    def scatter_columns(self, terms):
        terms = terms.reshape(self.size, -1, terms.shape[1])
        block = lax.psum_scatter(terms, self.group, scatter_dimension=1, tiled=True)
        parts = lax.all_to_all(block, self.team, 0, 0)
        return parts.transpose(1, 0, 2).reshape(parts.shape[1], -1).astype(f32)

    def gather_group(self, weight):
        return lax.all_gather(weight, self.group, axis=0, tiled=True)

    def scatter_group(self, terms, axis=0):
        block = lax.psum_scatter(terms, self.group, scatter_dimension=axis, tiled=True)
        return block.astype(f32)


def norm_columns(raw, columns):
    parts = [raw[:, k * columns : (k + 1) * columns] for k in (0, 1)]
    return jnp.stack([jnp.sum(part * part, axis=-1) for part in parts], axis=-1)


def raw_back(raw, scaled, inverse, means, grad_value):
    columns = grad_value.shape[1]
    grads = []
    for which in (0, 1):
        here = slice(which * columns, (which + 1) * columns)
        scale = inverse[:, which : which + 1]
        normed = raw[:, here] * scale
        grad = scale * (scaled[:, here] - normed * means[:, which : which + 1])
        grads.append(grad.astype(bf16))
    return jnp.concatenate(grads + [grad_value], axis=1)


def pair_kernel(first_y, second_y, first_x, second_x, first_w, second_w, left_ref, right_ref):
    def terms(first, second):
        first, second = (ref[...].reshape(-1, ref.shape[-1]) for ref in (first, second))
        total = product_tt(first, first_w[...]) + product_tt(second, second_w[...])
        return total.astype(bf16)

    step = pl.program_id(0)

    @pl.when(step < pl.num_programs(0) // 2)
    def _():
        left_ref[...] = terms(first_y, second_y)

    @pl.when(step >= pl.num_programs(0) // 2)
    def _():
        right_ref[...] = terms(first_x, second_x)


def pair_terms(place, first, second, first_whole, second_whole):
    rows, inner = first.shape
    width = first_whole.shape[0]
    quarter, tile = rows // 4, 256
    steps = width // tile
    along_y = pl.BlockSpec((1, 2, quarter, inner), lambda k: (place, 0, 0, 0))
    along_x = pl.BlockSpec((2, 1, quarter, inner), lambda k: (0, place, 0, 0))
    weight = pl.BlockSpec((tile, inner), lambda k: (k, 0))
    left = pl.BlockSpec((rows // 2, tile), lambda k: (0, jnp.minimum(k, steps // 2 - 1)))
    right = pl.BlockSpec((rows // 2, tile), lambda k: (0, jnp.maximum(k - steps // 2, 0)))
    first, second = (value.reshape(2, 2, quarter, inner) for value in (first, second))
    return pl.pallas_call(
        pair_kernel,
        grid=(steps,),
        in_specs=[along_y, along_y, along_x, along_x, weight, weight],
        out_specs=[left, right],
        out_shape=[jax.ShapeDtypeStruct((rows // 2, width // 2), bf16)] * 2,
        compiler_params=pltpu.CompilerParams(vmem_limit_bytes=40 * 2**20),
        cost_estimate=NO_COST,
    )(first, second, first, second, first_whole, second_whole)


def local_plain(
    plan,
    tokens,
    block_lengths,
    w_query,
    w_key,
    w_value,
    w_out,
    w_gate,
    w_up,
    w_down,
    query_gain,
    key_gain,
    attn_gain,
    mlp_gain,
    cotangent,
):
    width = tokens.shape[1]
    columns = width // plan.size
    live, _ = row_layout(block_lengths)
    live_col = live.astype(f32)[:, None]
    lengths = lax.all_gather(block_lengths, plan.team)
    _, position = jax.vmap(row_layout)(lengths)
    cosine, sine = angles(position)
    gains = jnp.stack([query_gain, key_gain, attn_gain, mlp_gain])
    gains = lax.all_gather(gains, plan.every, axis=1, tiled=True).astype(f32)
    part_gains = lax.dynamic_slice_in_dim(gains[:2], plan.index * columns, columns, axis=1)
    attn_gain_wide, mlp_gain_wide = gains[2], gains[3]
    attn_whole = jnp.concatenate(
        [plan.gather_columns(w) for w in (w_query, w_key, w_value)], axis=1
    )
    out_whole = plan.gather_group(w_out)
    gate_whole = plan.gather_columns(w_gate)
    up_whole = plan.gather_columns(w_up)
    down_whole = plan.gather_group(w_down)

    team_tokens = plan.gather_rows(tokens)
    raw = product(team_tokens, attn_whole)
    inverse = lax.rsqrt(plan.sum_rows(norm_columns(raw, columns)) / width + epsilon)
    turned, mixed_low = attend(lengths, raw, inverse, part_gains, cosine, sine)
    attn_proj = plan.scatter_rows(product(mixed_low, out_whole).astype(bf16))
    attn_normed, attn_inverse = norm_forward(attn_proj, attn_gain_wide)
    hidden = tokens.astype(f32) + attn_normed
    team_hidden = plan.gather_rows(hidden.astype(bf16))
    gate = product(team_hidden, gate_whole)
    upward = product(team_hidden, up_whole)
    sigmoid_gate = jax.nn.sigmoid(gate)
    activated = gate * sigmoid_gate
    inner_low = (activated * upward).astype(bf16)
    down = plan.scatter_rows(product(inner_low, down_whole).astype(bf16))
    down_normed, down_inverse = norm_forward(down, mlp_gain_wide)
    block_out = (live_col * (hidden + down_normed)).astype(bf16)

    grad_out = live_col * cotangent.astype(f32)
    grad_down, term_mlp_gain = norm_back(down, down_inverse, mlp_gain_wide, grad_out)
    team_grad_down = plan.gather_rows(grad_down.astype(bf16))
    grad_w_down = plan.scatter_group(inner_rows(inner_low, team_grad_down).astype(bf16))
    grad_inner = product_tt(team_grad_down, down_whole)
    grad_gate = grad_inner * upward * sigmoid_gate * (1.0 + gate * (1.0 - sigmoid_gate))
    grad_up = grad_inner * activated
    grad_gate, grad_up = grad_gate.astype(bf16), grad_up.astype(bf16)
    grad_w_gate = plan.scatter_columns(inner_rows(team_hidden, grad_gate).astype(bf16))
    grad_w_up = plan.scatter_columns(inner_rows(team_hidden, grad_up).astype(bf16))
    grad_from_mlp = product_tt(grad_gate, gate_whole) + product_tt(grad_up, up_whole)
    grad_hidden = grad_out + plan.scatter_rows(grad_from_mlp.astype(bf16))

    grad_proj, term_attn_gain = norm_back(attn_proj, attn_inverse, attn_gain_wide, grad_hidden)
    team_grad_proj = plan.gather_rows(grad_proj.astype(bf16))
    grad_mixed = product_tt(team_grad_proj, out_whole).astype(bf16)
    grad_w_out = plan.scatter_group(inner_rows(mixed_low, team_grad_proj).astype(bf16))
    scaled, grad_value, means, part_terms = attend_back(
        lengths, raw, turned, inverse, part_gains, cosine, sine, grad_mixed
    )
    means = plan.sum_rows(means) / width
    grad_raw = raw_back(raw, scaled, inverse, means, grad_value)
    grad_w_query, grad_w_key, grad_w_value = (
        plan.scatter_columns(
            inner_rows(team_tokens, grad_raw[:, k * columns : (k + 1) * columns]).astype(bf16)
        )
        for k in range(3)
    )
    grad_from_attn = plan.scatter_rows(product_tt(grad_raw, attn_whole).astype(bf16))
    part_grads = plan.scatter_group(part_terms, 1)
    gain_grads = lax.psum_scatter(
        jnp.stack([term_attn_gain, term_mlp_gain]), plan.every, scatter_dimension=1, tiled=True
    )
    return (
        block_out,
        (grad_hidden + grad_from_attn).astype(bf16),
        grad_w_query,
        grad_w_key,
        grad_w_value,
        grad_w_out,
        grad_w_gate,
        grad_w_up,
        grad_w_down,
        part_grads[0],
        part_grads[1],
        gain_grads[0],
        gain_grads[1],
    )


def local_cube(
    tokens,
    block_lengths,
    w_query,
    w_key,
    w_value,
    w_out,
    w_gate,
    w_up,
    w_down,
    query_gain,
    key_gain,
    attn_gain,
    mlp_gain,
    cotangent,
):
    plan = Cube()
    width = tokens.shape[1]
    columns = width // plan.size
    live, _ = row_layout(block_lengths)
    live_col = live.astype(f32)[:, None]

    def group_whole(block):
        return lax.all_gather(block, plan.group, axis=0, tiled=True)

    shard = query_gain.shape[0]
    small = plan.small_rows((query_gain, key_gain, attn_gain, mlp_gain), block_lengths, width)
    attn_parts = jnp.concatenate([plan.team_columns(w) for w in (w_query, w_key, w_value)], axis=2)
    attn_parts, own, out_rows, down0 = sync(attn_parts, tokens, w_out, w_down)
    packed = group_whole(jnp.concatenate([out_rows, small])).reshape(8, -1, width)
    down1 = plan.shift(down0)
    rows = plan.rows_first(plan.grouped(own))
    attn0 = plan.send_columns(attn_parts)
    attn0, w_gate, *rows = sync(attn0, w_gate, *rows)
    attn1, attn0c = plan.shift(attn0), swap(attn0, "c")
    rows = plan.rows_second(*rows)
    attn1, attn0c, down1, w_gate, *rows = sync(attn1, attn0c, down1, w_gate, *rows)
    gate = plan.send_columns(plan.team_columns(w_gate))
    attn2, attn1c = plan.shift(attn1), swap(attn1, "c")
    team_tokens = join(*rows)
    attn2, attn1c, gate, w_up, team_tokens, packed = sync(
        attn2, attn1c, gate, w_up, team_tokens, packed
    )
    gate_whole = group_whole(gate)
    up = plan.send_columns(plan.team_columns(w_up))
    attn3, attn2c = plan.shift(attn2), swap(attn2, "c")
    out_whole = packed[:, : w_out.shape[0]].reshape(-1, width)
    small = packed[:, w_out.shape[0] : w_out.shape[0] + 5, :shard].transpose(1, 0, 2)
    small = plan.small_step(plan.small_step(small, "x"), "y")
    attn3, attn2c, small, out_whole, up = sync(attn3, attn2c, small, out_whole, up)
    up_whole = group_whole(up)
    gains, lengths = plan.small_end(small, block_lengths.shape[0])
    _, position = jax.vmap(row_layout)(lengths)
    cosine, sine = angles(position)
    part_gains = lax.dynamic_slice_in_dim(gains[:2], plan.index * columns, columns, axis=1)
    attn_gain_wide, mlp_gain_wide = gains[2], gains[3]
    attn3c = swap(attn3, "c")
    attn_whole = plan.join_group([[attn0, attn1, attn2, attn3], [attn0c, attn1c, attn2c, attn3c]])

    raw = product(team_tokens, attn_whole)
    inverse = lax.rsqrt(plan.sum_rows(norm_columns(raw, columns)) / width + epsilon)
    turned, mixed_low = attend(lengths, raw, inverse, part_gains, cosine, sine)
    mixed_low, down1, team_tokens = sync(mixed_low, down1, team_tokens)
    down2, down0c, down1c = plan.shift(down1), swap(w_down, "c"), swap(down1, "c")
    half = width // 2

    def by_columns(rows, side, left, right):
        return product(rows(left), right[:, side * half : (side + 1) * half])

    def by_rows(rows, side, left, right):
        return product_tt(rows(left), right[side * half : (side + 1) * half])

    terms = plan.terms_first(by_columns, mixed_low, out_whole)
    terms = plan.terms_second(*terms)
    attn_proj = plan.terms_sum(*terms)
    attn_normed, attn_inverse = norm_forward(attn_proj, attn_gain_wide)
    hidden = tokens.astype(f32) + attn_normed

    rows = plan.rows_first(plan.grouped(hidden.astype(bf16)))
    rows = plan.rows_second(*rows)
    team_hidden = join(*rows)
    gate = product(team_hidden, gate_whole).astype(bf16)
    hidden_parts = plan.core_halves(team_hidden)
    gate, down2, *hidden_parts = sync(gate, down2, *hidden_parts)
    down3, down2c = plan.shift(down2), swap(down2, "c")
    upward = product(team_hidden, up_whole).astype(bf16)
    inner_low = (jax.nn.silu(gate.astype(f32)) * upward.astype(f32)).astype(bf16)
    inner_low, down3 = sync(inner_low, down3)
    down3c = swap(down3, "c")
    down_whole = plan.join_group([[w_down, down1, down2, down3], [down0c, down1c, down2c, down3c]])
    terms = plan.terms_first(by_columns, inner_low, down_whole)
    *inner_parts, left, right, left_y, right_x = sync(*plan.core_halves(inner_low), *terms)
    down = plan.terms_sum(*plan.terms_second(left, right, left_y, right_x))
    down_normed, down_inverse = norm_forward(down, mlp_gain_wide)
    block_out = (live_col * (hidden + down_normed)).astype(bf16)

    grad_out = live_col * cotangent.astype(f32)
    grad_down, term_mlp_gain = norm_back(down, down_inverse, mlp_gain_wide, grad_out)
    rows = plan.rows_second(*plan.rows_first(grad_down.astype(bf16)))
    team_grad_down = join(*rows)

    def terms_of(left, right):
        return inner_rows(left, right).astype(bf16)

    def summed(mine, other):
        return (mine.astype(f32) + other.astype(f32)).astype(bf16)

    down_other = swap(terms_of(inner_parts[0], team_grad_down), "c")
    down_mine = terms_of(inner_parts[1], team_grad_down)
    team_grad_down, down_mine, down_other = sync(team_grad_down, down_mine, down_other)
    down_terms = summed(down_mine, down_other)
    gain_shape = (2, 2, 2, 2, 2, -1)
    team_grad_down, down_terms, mlp_terms = sync(team_grad_down, down_terms, term_mlp_gain)
    mlp_terms = plan.gain_step(mlp_terms.reshape(gain_shape), "c", 2)
    team_grad_down, mlp_terms = sync(team_grad_down, mlp_terms)
    grad_w_down = lax.psum_scatter(down_terms, plan.z_axes, scatter_dimension=0, tiled=True)
    grad_inner = product_tt(team_grad_down, down_whole)
    gate_wide = gate.astype(f32)
    sigmoid_gate = jax.nn.sigmoid(gate_wide)
    slope = sigmoid_gate * (1.0 + gate_wide * (1.0 - sigmoid_gate))
    grad_gate = grad_inner * upward.astype(f32) * slope
    grad_up = grad_inner * (gate_wide * sigmoid_gate)
    grad_gate, grad_up, *hidden_parts = sync(
        grad_gate.astype(bf16), grad_up.astype(bf16), *hidden_parts
    )
    gate_away = terms_of(hidden_parts[0], grad_gate)
    gate_away, grad_up, other_part = sync(gate_away, grad_up, hidden_parts[0])
    gate_other = swap(gate_away, "c")
    up_away = terms_of(other_part, grad_up)
    up_away, grad_gate, grad_up = sync(up_away, grad_gate, grad_up)
    up_other = swap(up_away, "c")
    hidden_part = hidden_parts[1]

    left_away, right_away = pair_terms(1, grad_gate, grad_up, gate_whole, up_whole)
    left_away, right_away, grad_gate, grad_up, hidden_part, own_tokens, own_mixed = sync(
        left_away, right_away, grad_gate, grad_up, hidden_part, team_tokens, mixed_low
    )
    left_y, right_x = swap(left_away, "y"), swap(right_away, "x")
    left, right = pair_terms(0, grad_gate, grad_up, gate_whole, up_whole)
    terms = left, right, left_y, right_x
    gate_terms = summed(terms_of(hidden_part, grad_gate), gate_other)
    late_parts = (*plan.core_halves(own_tokens), *plan.core_halves(own_mixed))
    gate_terms, grad_up, token_other, token_mine, mixed_other, mixed_mine, *terms = sync(
        gate_terms, grad_up, *late_parts, *terms
    )
    gate_block = lax.psum_scatter(gate_terms, plan.z_axes, scatter_dimension=0, tiled=True)
    terms = plan.terms_second(*terms)
    grad_up, *terms = sync(grad_up, *terms)

    grad_hidden, grad_proj, term_attn_gain = proj_back(
        plan.own_order, terms, live_col, cotangent, attn_proj, attn_inverse, attn_gain_wide
    )
    rows = plan.rows_first(grad_proj)
    up_mine = terms_of(hidden_part, grad_up)
    up_mine, up_other, grad_w_down, *rows = sync(up_mine, up_other, grad_w_down, *rows)
    rows = plan.rows_second(*rows)
    up_terms = summed(up_mine, up_other)
    up_terms, gate_block, *rows = sync(up_terms, gate_block, *rows)
    up_block = lax.psum_scatter(up_terms, plan.z_axes, scatter_dimension=0, tiled=True)
    team_grad_proj = join(*rows)
    grad_mixed = product_tt(team_grad_proj, out_whole).astype(bf16)
    scaled, grad_value, means, part_terms = attend_back(
        lengths, raw, turned, inverse, part_gains, cosine, sine, grad_mixed
    )
    attn_gain_terms = plan.gain_step(term_attn_gain.reshape(gain_shape), "c", 2)
    gain_terms = jnp.stack([attn_gain_terms, mlp_terms])
    gate_block = plan.return_columns(gate_block)
    means, part_terms, gain_terms, team_grad_proj, gate_block = sync(
        means, part_terms, gain_terms, team_grad_proj, gate_block
    )
    out_away = terms_of(mixed_other, team_grad_proj)
    means = plan.sum_along(means, "y")
    means, out_away, team_grad_proj = sync(means, out_away, team_grad_proj)
    out_mine = terms_of(mixed_mine, team_grad_proj)
    means = plan.sum_along(means, "x") / width
    means, out_mine = sync(means, out_mine)
    grad_raw = raw_back(raw, scaled, inverse, means, grad_value)
    part = token_other.shape[1] // 2
    attn_other = [swap(terms_of(token_other[:, :part], grad_raw), "c")]
    attn_other += [swap(terms_of(token_other[:, part:], grad_raw), "c")]
    out_other = swap(out_away, "c")
    attn_mine = terms_of(token_mine, grad_raw)
    part_terms = part_terms + swap(part_terms, "c")
    grad_raw, attn_mine, out_mine, out_other, part_terms, gain_terms, *attn_other = sync(
        grad_raw, attn_mine, out_mine, out_other, part_terms, gain_terms, *attn_other
    )
    attn_terms, out_terms = (attn_mine, tuple(attn_other)), (out_mine, out_other)
    attn_sum, out_sum = plan.ring_step(1, attn_terms), plan.ring_step(1, out_terms)
    terms = plan.terms_first(by_rows, grad_raw, attn_whole)
    gain_terms, part_terms = plan.both_step(gain_terms, part_terms, "zh", 3)
    attn_sum, out_sum, part_terms, gain_terms, *terms = sync(
        attn_sum, out_sum, part_terms, gain_terms, *terms
    )
    attn_sum = plan.ring_sum(2, attn_terms, attn_sum).astype(bf16)
    out_sum = plan.ring_sum(2, out_terms, out_sum).astype(bf16)
    attn_sum, out_sum, part_terms, gain_terms, *terms = sync(
        attn_sum, out_sum, part_terms, gain_terms, *terms
    )
    attn_sum, out_sum = plan.shift(attn_sum), plan.shift(out_sum)
    gain_terms, part_terms = plan.both_step(gain_terms, part_terms, "zl", 3)
    up_block = plan.return_columns(up_block)
    terms = plan.terms_added(*terms)
    attn_sum, out_sum, gain_terms, part_terms, up_block, *terms = sync(
        attn_sum, out_sum, gain_terms, part_terms, up_block, *terms
    )
    attn_sum = plan.ring_sum(3, attn_terms, attn_sum).astype(bf16)
    out_sum = plan.ring_sum(3, out_terms, out_sum).astype(bf16)
    attn_sum, out_sum, gate_block, up_block, *sides, left_away, right_away = sync(
        attn_sum, out_sum, gate_block, up_block, *terms
    )
    attn_sum, out_sum = plan.shift(attn_sum), plan.shift(out_sum)
    left_x, right_y = swap(left_away, "x"), swap(right_away, "y")
    grad_w_gate, grad_w_up = plan.whole_columns(gate_block), plan.whole_columns(up_block)
    gain_terms = plan.gain_step(gain_terms, "x", 2)
    part_grads = plan.own_gains(part_terms)
    attn_sum, out_sum, gain_terms, part_grads, grad_w_gate, grad_w_up, left_x, right_y = sync(
        attn_sum, out_sum, gain_terms, part_grads, grad_w_gate, grad_w_up, left_x, right_y
    )
    attn_sum = plan.ring_sum(0, attn_terms, attn_sum).astype(bf16)
    attn_sum, out_sum, gain_terms, left_x, right_y = sync(
        attn_sum, out_sum, gain_terms, left_x, right_y
    )
    grad_tokens = tokens_end(plan.own_order, (*sides, left_x, right_y), grad_hidden)
    attn_block = plan.return_columns(attn_sum)
    gain_terms = plan.gain_step(gain_terms, "y", 1)
    grad_w_out = plan.ring_sum(0, out_terms, out_sum)
    attn_block, grad_w_out, gain_terms, grad_tokens = sync(
        attn_block, grad_w_out, gain_terms, grad_tokens
    )
    grad_w_query, grad_w_key, grad_w_value = spread_three(attn_block)
    return (
        block_out,
        grad_tokens,
        grad_w_query,
        grad_w_key,
        grad_w_value,
        grad_w_out,
        grad_w_gate,
        grad_w_up,
        grad_w_down.astype(f32),
        part_grads[0],
        part_grads[1],
        gain_terms[0],
        gain_terms[1],
    )


def solution(mesh):
    if tuple(mesh.shape.values()) == (8, 4):
        mesh = Mesh(mesh.devices.reshape(2, 2, 2, 2, 2), Cube.every)
        every, step = Cube.every, local_cube
    else:
        every = tuple(mesh.axis_names)

        def step(*arrays):
            return local_plain(Plain(*every), *arrays)

    rows, line = P(every, None), P(every)
    return jax.shard_map(
        step,
        mesh=mesh,
        in_specs=(rows, line) + (rows,) * 7 + (line,) * 4 + (rows,),
        out_specs=(rows,) * 9 + (line,) * 4,
        check_vma=False,
    )
```

```python
import functools

import jax
import jax.numpy as jnp
from jax import lax
from jax.experimental import pallas as pl
from jax.experimental.pallas import tpu as pltpu
from jax.sharding import Mesh, PartitionSpec as P

HEAD_DIM = 128
BLOCK = 128

epsilon = 1e-06
rope_base = 500000.0
f32 = jnp.float32
bf16 = jnp.bfloat16
NO_COST = pl.CostEstimate(flops=0, bytes_accessed=0, transcendentals=0)


def product(left, right):
    return jnp.dot(left, right, preferred_element_type=f32)


def product_tt(left, right):
    return lax.dot_general(left, right, (((1,), (1,)), ((), ())), preferred_element_type=f32)


def inner_rows(left, right):
    return lax.dot_general(left, right, (((0,), (0,)), ((), ())), preferred_element_type=f32)


def norm_forward(values, gain):
    inverse = lax.rsqrt(jnp.mean(values * values, axis=-1, keepdims=True) + epsilon)
    return (values * inverse * gain, inverse)


def norm_back(values, inverse, gain, incoming):
    normed = values * inverse
    scaled = incoming * gain
    gain_term = jnp.sum(incoming * normed, axis=0)
    back = inverse * (scaled - normed * jnp.mean(scaled * normed, axis=-1, keepdims=True))
    return (back, gain_term)


def angles(position):
    half = HEAD_DIM // 2
    freq = rope_base ** (-jnp.arange(half, dtype=f32) / half)
    angle = position.astype(f32).reshape(-1, 1) * freq
    cosine, sine = jnp.cos(angle), jnp.sin(angle)
    return jnp.concatenate([cosine, cosine], axis=1), jnp.concatenate([-sine, sine], axis=1)


def row_layout(lengths):
    nblock = lengths.shape[0]
    row_ids = jnp.arange(nblock * BLOCK, dtype=jnp.int32)
    begin = jnp.arange(nblock, dtype=jnp.int32) * BLOCK
    cover = (
        (lengths[None, :] > 0)
        & (row_ids[:, None] >= begin[None, :])
        & (row_ids[:, None] < begin[None, :] + lengths[None, :])
    )
    live = jnp.any(cover, axis=1)
    owner = jnp.sum(jnp.where(cover, begin[None, :], 0), axis=1)
    return (live, row_ids - owner)


def allowed_keys(lengths_ref, device, nrows):
    rows = lax.broadcasted_iota(jnp.int32, (nrows, nrows), 0)
    keys = lax.broadcasted_iota(jnp.int32, (nrows, nrows), 1)

    def number(ids):
        found = -1 - ids
        for block in range(nrows // BLOCK):
            begin, length = block * BLOCK, lengths_ref[device, block]
            found = jnp.where((ids >= begin) & (ids < begin + length), begin, found)
        return found

    return (number(rows) == number(keys)) & (keys <= rows)


def turn(values, cosine, sine):
    return values * cosine + pltpu.roll(values, HEAD_DIM // 2, 1) * sine


def probabilities(query, key, allowed):
    scores = product_tt(query, key) * HEAD_DIM ** (-0.5)
    scores = jnp.where(allowed, scores, -1e30)
    powers = jnp.exp(scores - jnp.max(scores, axis=-1, keepdims=True))
    return powers * (1.0 / jnp.sum(powers, axis=-1, keepdims=True))


def attend_kernel(
    lengths_ref, raw_ref, inverse_ref, gains_ref, cosine_ref, sine_ref, turned_ref, mixed_ref
):
    nrows, columns = mixed_ref.shape
    allowed = allowed_keys(lengths_ref, pl.program_id(0), nrows)
    cosine, sine = cosine_ref[...], sine_ref[...]
    for head in range(columns // HEAD_DIM):
        here = slice(head * HEAD_DIM, (head + 1) * HEAD_DIM)
        turned = []
        for which in range(2):
            there = slice(which * columns + here.start, which * columns + here.stop)
            normed = raw_ref[:, there] * inverse_ref[:, which : which + 1]
            rotated = turn(normed * gains_ref[which : which + 1, here], cosine, sine).astype(bf16)
            turned_ref[:, there] = rotated
            turned.append(rotated)
        there = slice(2 * columns + here.start, 2 * columns + here.stop)
        value = raw_ref[:, there].astype(bf16)
        turned_ref[:, there] = value
        probs = probabilities(turned[0], turned[1], allowed)
        mixed_ref[:, here] = product(probs.astype(bf16), value).astype(bf16)


def attend_back_kernel(
    lengths_ref, raw_ref, turned_ref, inverse_ref, gains_ref, cosine_ref, sine_ref, grad_ref,
    scaled_ref, grad_value_ref, means_ref, terms_ref,
):
    nrows, columns = grad_ref.shape
    device = pl.program_id(0)
    allowed = allowed_keys(lengths_ref, device, nrows)
    cosine, sine = cosine_ref[...], sine_ref[...]

    @pl.when(device == 0)
    def _():
        terms_ref[...] = jnp.zeros_like(terms_ref)

    sums = [0.0, 0.0]
    for head in range(columns // HEAD_DIM):
        here = slice(head * HEAD_DIM, (head + 1) * HEAD_DIM)
        spots = [slice(k * columns + here.start, k * columns + here.stop) for k in range(3)]
        query, key, value = (turned_ref[:, spot] for spot in spots)
        incoming = grad_ref[:, here]
        probs = probabilities(query, key, allowed)
        grad_probs = product_tt(incoming, value)
        inner = jnp.sum(probs * grad_probs, axis=-1, keepdims=True)
        grad_scores = (probs * (grad_probs - inner)).astype(bf16)
        grad_value_ref[:, here] = inner_rows(probs.astype(bf16), incoming).astype(bf16)
        back = (product(grad_scores, key), inner_rows(grad_scores, query))
        for which in range(2):
            turned = turn(back[which] * HEAD_DIM ** (-0.5), cosine, -sine)
            normed = raw_ref[:, spots[which]] * inverse_ref[:, which : which + 1]
            terms_ref[which : which + 1, here] += jnp.sum(turned * normed, axis=0, keepdims=True)
            scaled = turned * gains_ref[which : which + 1, here]
            scaled_ref[:, spots[which]] = scaled
            sums[which] = sums[which] + jnp.sum(scaled * normed, axis=-1, keepdims=True)
    means_ref[...] = jnp.concatenate(sums, axis=1)


def attend_specs(nrows, columns):
    def rows(wide):
        return pl.BlockSpec((nrows, wide), lambda b: (b, 0))

    lengths = pl.BlockSpec(memory_space=pltpu.SMEM)
    gains = pl.BlockSpec((2, columns), lambda b: (0, 0))
    return rows, lengths, gains


def attend(lengths, raw, inverse, gains, cosine, sine):
    size, nrows = lengths.shape[0], raw.shape[0] // lengths.shape[0]
    columns = raw.shape[1] // 3
    rows, whole, gain = attend_specs(nrows, columns)
    return pl.pallas_call(
        attend_kernel,
        grid=(size,),
        in_specs=[whole, rows(3 * columns), rows(2), gain, rows(HEAD_DIM), rows(HEAD_DIM)],
        out_specs=[rows(3 * columns), rows(columns)],
        out_shape=[
            jax.ShapeDtypeStruct(raw.shape, bf16),
            jax.ShapeDtypeStruct((raw.shape[0], columns), bf16),
        ],
        cost_estimate=NO_COST,
    )(lengths, raw, inverse, gains, cosine, sine)


def attend_back(lengths, raw, turned, inverse, gains, cosine, sine, grad):
    size, nrows = lengths.shape[0], raw.shape[0] // lengths.shape[0]
    columns = raw.shape[1] // 3
    rows, whole, gain = attend_specs(nrows, columns)
    return pl.pallas_call(
        attend_back_kernel,
        grid=(size,),
        in_specs=[
            whole, rows(3 * columns), rows(3 * columns), rows(2), gain,
            rows(HEAD_DIM), rows(HEAD_DIM), rows(columns),
        ],
        out_specs=[rows(2 * columns), rows(columns), rows(2), gain],
        out_shape=[
            jax.ShapeDtypeStruct((raw.shape[0], 2 * columns), f32),
            jax.ShapeDtypeStruct((raw.shape[0], columns), bf16),
            jax.ShapeDtypeStruct((raw.shape[0], 2), f32),
            jax.ShapeDtypeStruct((2, columns), f32),
        ],
        cost_estimate=NO_COST,
    )(lengths, raw, turned, inverse, gains, cosine, sine, grad)


def swap(value, axis):
    return lax.ppermute(value, axis, ((0, 1), (1, 0)))


def sync(*values):
    return lax.optimization_barrier(values)


def pick(value, index, axis):
    return lax.dynamic_index_in_dim(value, index, axis, keepdims=False)


def join_kernel(table_ref, *refs):
    pieces, out, held, sems = refs[:-3], refs[-3], refs[-2], refs[-1]
    loads, stores = [], []
    for k, piece in enumerate(pieces):
        here = pl.ds(pl.multiple_of(table_ref[k] * 64, 64), piece.shape[0])
        loads.append(pltpu.make_async_copy(piece, held.at[here], sems.at[0, k]))
        stores.append(pltpu.make_async_copy(held.at[here], out.at[here], sems.at[1, k]))
        loads[-1].start()
    for load, store in zip(loads, stores):
        load.wait()
        store.start()
    for store in stores:
        store.wait()


def join(*pieces, table=None):
    if table is None:
        begins = [sum(piece.shape[0] for piece in pieces[:k]) // 64 for k in range(len(pieces))]
        table = jnp.array(begins, jnp.int32)
    shape = (sum(piece.shape[0] for piece in pieces), pieces[0].shape[1])
    return pl.pallas_call(
        join_kernel,
        in_specs=[pl.BlockSpec(memory_space=pltpu.SMEM)]
        + [pl.BlockSpec(memory_space=pl.ANY)] * len(pieces),
        out_specs=pl.BlockSpec(memory_space=pl.ANY),
        out_shape=jax.ShapeDtypeStruct(shape, pieces[0].dtype),
        scratch_shapes=[
            pltpu.VMEM(shape, pieces[0].dtype),
            pltpu.SemaphoreType.DMA((2, len(pieces))),
        ],
        compiler_params=pltpu.CompilerParams(vmem_limit_bytes=32 * 2**20),
        cost_estimate=NO_COST,
    )(table, *pieces)


def regroup_kernel(halves, in_ref, out_ref):
    for tile in range(len(halves) // 2):
        parts = [in_ref[:, half * 64 : (half + 1) * 64] for half in halves[2 * tile : 2 * tile + 2]]
        out_ref[:, tile * 128 : (tile + 1) * 128] = jnp.concatenate(parts, axis=1)


def regroup(value, halves):
    rows, width = value.shape
    block = pl.BlockSpec((rows // 2, width), lambda k: (k, 0))
    return pl.pallas_call(
        functools.partial(regroup_kernel, halves),
        grid=(2,),
        in_specs=[block],
        out_specs=block,
        out_shape=jax.ShapeDtypeStruct(value.shape, value.dtype),
        cost_estimate=NO_COST,
    )(value)


def spread_kernel(order, parts_ref, out_ref):
    wide = out_ref.shape[1] // len(order)
    for block, (part, column) in enumerate(order):
        here = slice(block * wide, (block + 1) * wide)
        out_ref[:, here] = parts_ref[part, :, column * wide : (column + 1) * wide].astype(f32)


def spread(parts, order):
    shape = (parts.shape[1], parts.shape[0] * parts.shape[2])
    return pl.pallas_call(
        functools.partial(spread_kernel, order),
        in_specs=[pl.BlockSpec(memory_space=pltpu.VMEM)],
        out_specs=pl.BlockSpec(memory_space=pltpu.VMEM),
        out_shape=jax.ShapeDtypeStruct(shape, f32),
        cost_estimate=NO_COST,
    )(parts)


def ordered(blocks, *refs):
    left = sum(ref[...].astype(f32) for ref in refs[0::2])
    right = sum(ref[...].astype(f32) for ref in refs[1::2])
    half = left.shape[1] // 64
    parts = [(left, k) if k < half else (right, k - half) for k in blocks]
    return jnp.concatenate([part[:, k * 64 : (k + 1) * 64] for part, k in parts], axis=1)


def tokens_kernel(blocks, *refs):
    *sides, hidden_ref, out_ref = refs
    out_ref[...] = (ordered(blocks, *sides) + hidden_ref[...]).astype(bf16)


def tokens_end(blocks, sides, hidden):
    rows, width = hidden.shape
    side = pl.BlockSpec((rows // 4, width // 2), lambda k: (k, 0))
    whole = pl.BlockSpec((rows // 4, width), lambda k: (k, 0))
    return pl.pallas_call(
        functools.partial(tokens_kernel, blocks),
        grid=(4,),
        in_specs=[side] * len(sides) + [whole],
        out_specs=whole,
        out_shape=jax.ShapeDtypeStruct((rows, width), bf16),
        cost_estimate=NO_COST,
    )(*sides, hidden)


def proj_back_kernel(blocks, *refs):
    *sides, live_ref, cotangent_ref, proj_ref, inverse_ref, gain_ref = refs[:-3]
    hidden_ref, grad_ref, term_ref = refs[-3:]
    total = ordered(blocks, *sides)
    total += live_ref[...] * cotangent_ref[...].astype(f32)
    hidden_ref[...] = total
    normed = proj_ref[...] * inverse_ref[...]
    term = jnp.sum(total * normed, axis=0, keepdims=True)
    scaled = total * gain_ref[...]
    mean = jnp.mean(scaled * normed, axis=-1, keepdims=True)
    grad_ref[...] = (inverse_ref[...] * (scaled - normed * mean)).astype(bf16)
    first = pl.program_id(0) == 0
    term_ref[...] = jnp.where(first, term, term_ref[...] + term)


def proj_back(blocks, sides, live, cotangent, proj, inverse, gain):
    rows, width = proj.shape
    side = pl.BlockSpec((rows // 4, width // 2), lambda k: (k, 0))
    whole = pl.BlockSpec((rows // 4, width), lambda k: (k, 0))
    column = pl.BlockSpec((rows // 4, 1), lambda k: (k, 0))
    line = pl.BlockSpec((1, width), lambda k: (0, 0))
    hidden, grad, term = pl.pallas_call(
        functools.partial(proj_back_kernel, blocks),
        grid=(4,),
        in_specs=[side] * len(sides) + [column, whole, whole, column, line],
        out_specs=[whole, whole, line],
        out_shape=[
            jax.ShapeDtypeStruct((rows, width), f32),
            jax.ShapeDtypeStruct((rows, width), bf16),
            jax.ShapeDtypeStruct((1, width), f32),
        ],
        cost_estimate=NO_COST,
    )(*sides, live, cotangent, proj, inverse, gain.reshape(1, width))
    return hidden, grad, term[0]


def spread_three_kernel(parts_ref, *out_refs):
    columns = parts_ref.shape[2] // 3
    for which, out_ref in enumerate(out_refs):
        there = slice(which * columns, (which + 1) * columns)
        for part in range(parts_ref.shape[0]):
            here = slice(part * columns, (part + 1) * columns)
            out_ref[:, here] = parts_ref[part, :, there].astype(f32)


def spread_three(parts):
    shape = (parts.shape[1], parts.shape[0] * parts.shape[2] // 3)
    return pl.pallas_call(
        spread_three_kernel,
        in_specs=[pl.BlockSpec(memory_space=pltpu.VMEM)],
        out_specs=[pl.BlockSpec(memory_space=pltpu.VMEM)] * 3,
        out_shape=[jax.ShapeDtypeStruct(shape, f32)] * 3,
        cost_estimate=NO_COST,
    )(parts)


class Cube:
    every = ("y", "x", "c", "zh", "zl")
    team = ("y", "x")
    z_axes = ("zh", "zl")
    group = ("c", "zh", "zl")

    def __init__(self):
        self.place = [lax.axis_index(axis) for axis in self.every]
        self.core = self.place[2]
        self.z = lax.axis_index(self.z_axes)
        self.size = 4
        self.index = lax.axis_index(self.team)

    def shift(self, value):
        return lax.ppermute(value, self.z_axes, ((0, 1), (1, 2), (2, 3), (3, 0)))

    def rows_first(self, rows):
        half = rows.shape[0] // 2
        top, low = rows[:half], rows[half:]
        return top, low, swap(top, "x"), swap(low, "y")

    def rows_second(self, top, low, top_x, low_y):
        top_y, low_x = swap(top, "y"), swap(low, "x")
        return top, low, top_x, low_x, top_y, low_y, swap(top_x, "y"), swap(low_y, "x")

    def terms_first(self, make, *values):
        left, right = 0, 1

        def along_x(place):
            return lambda rows: rows.reshape(2, 2, -1, rows.shape[1])[:, place].reshape(
                -1, rows.shape[1]
            )

        def along_y(place):
            return lambda rows: rows[place * rows.shape[0] // 2 : (place + 1) * rows.shape[0] // 2]

        left_away = make(along_y(1), left, *values).astype(bf16)
        right_away = make(along_x(1), right, *values).astype(bf16)
        left_away, right_away, *values = sync(left_away, right_away, *values)
        left_other, right_other = swap(left_away, "y"), swap(right_away, "x")
        left_mine = make(along_y(0), left, *values).astype(bf16)
        right_mine = make(along_x(0), right, *values).astype(bf16)
        return left_mine, right_mine, left_other, right_other

    def terms_added(self, left_mine, right_mine, left_other, right_other):
        half = left_mine.shape[0] // 2
        left_away = left_mine[half:].astype(f32) + left_other[half:].astype(f32)
        right_away = right_mine[half:].astype(f32) + right_other[half:].astype(f32)
        stay = (left_mine, right_mine, left_other, right_other)
        return (*stay, left_away.astype(bf16), right_away.astype(bf16))

    def terms_second(self, *terms):
        *stay, left_away, right_away = self.terms_added(*terms)
        return (*stay, swap(left_away, "x"), swap(right_away, "y"))

    def terms_sum(self, left_mine, right_mine, left_other, right_other, left_x, right_y):
        half = left_x.shape[0]
        left = (left_mine[:half], left_other[:half], left_x)
        right = (right_mine[:half], right_other[:half], right_y)
        sums = [sum(part.astype(f32) for part in parts) for parts in (left, right)]
        return jnp.concatenate(sums, axis=1)

    def sum_along(self, rows, axis):
        shape = rows.shape
        rows = rows.reshape((2, 2, -1) + shape[1:])
        rows = rows + jnp.flip(swap(rows, axis), self.team.index(axis))
        return rows.reshape(shape)

    def sum_rows(self, rows):
        return self.sum_along(self.sum_along(rows, "y"), "x")

    def order(self, mine, other, index, axis):
        first = index == 0
        return jnp.stack([jnp.where(first, mine, other), jnp.where(first, other, mine)], axis)

    def team_columns(self, weight):
        rows = weight.shape[0]
        return weight.reshape(rows, 4, -1).transpose(1, 0, 2)

    def whole_columns(self, parts):
        return spread(parts, [(part, 0) for part in range(4)])

    def send_columns(self, parts):
        return lax.all_to_all(parts, self.team, 0, 0).reshape(-1, parts.shape[2])

    def return_columns(self, block):
        return lax.all_to_all(block.reshape(4, -1, block.shape[1]), self.team, 0, 0)

    def grouped(self, rows):
        return regroup(rows, [spot * 8 + place for place in range(8) for spot in range(4)])

    own_order = [place * 4 + spot for spot in range(4) for place in range(8)]

    def ungrouped(self, rows):
        return regroup(rows, self.own_order)

    def join_group(self, blocks):
        table, pieces = [], []
        for core in range(2):
            for k in range(4):
                unit = blocks[core][k].shape[0] // 64
                table.append(((self.core ^ core) * 4 + (self.z - k) % 4) * unit)
                pieces.append(blocks[core][k])
        return join(*pieces, table=jnp.stack(table).astype(jnp.int32))

    def core_halves(self, values):
        half = values.shape[1] // 2
        return [
            lax.dynamic_slice_in_dim(values, index * half, half, 1)
            for index in (1 - self.core, self.core)
        ]

    def ring_sum(self, k, terms, so_far=None):
        rows = terms[0].shape[0] // 4
        part = (self.z - k) % 4

        def pick_rows(term):
            if isinstance(term, tuple):
                begin = part % 2 * rows
                low, high = (lax.dynamic_slice_in_dim(half, begin, rows, 0) for half in term)
                return jnp.where(part < 2, low, high)
            return lax.dynamic_slice_in_dim(term, part * rows, rows, 0)

        parts = [pick_rows(term).astype(f32) for term in terms]
        return sum(parts if so_far is None else parts + [so_far.astype(f32)])

    def ring_step(self, k, terms, so_far=None):
        return self.shift(self.ring_sum(k, terms, so_far).astype(bf16))

    def small_rows(self, gains, lengths, width):
        small = [jnp.pad(row.astype(bf16), (0, width - row.shape[0])) for row in (*gains, lengths)]
        return jnp.pad(jnp.stack(small), ((0, 16 - len(small)), (0, 0)))

    def small_step(self, small, axis):
        index = self.place[self.every.index(axis)]
        small = self.order(small, swap(small, axis), index, 1)
        return small.reshape(small.shape[0], -1, small.shape[-1])

    def small_end(self, small, count):
        gains = small[:4].reshape(4, -1).astype(f32)
        y, x, c, _, _ = self.place
        ids = [
            (((y ^ dy) * 2 + (x ^ dx)) * 2 + c) * 4 + self.z for dy in range(2) for dx in range(2)
        ]
        lengths = jnp.stack([pick(small[4], i, 0) for i in ids])[:, :count]
        return gains, lengths.astype(jnp.int32)

    def gain_step(self, terms, axis, dim):
        index = self.place[self.every.index(axis)]
        return pick(terms, index, dim) + swap(pick(terms, 1 - index, dim), axis)

    def both_step(self, terms, parts, axis, dim):
        index = self.place[self.every.index(axis)]
        away = pick(terms, 1 - index, dim)
        other = swap(jnp.concatenate([away.reshape(-1), parts.reshape(-1)]), axis)
        terms = pick(terms, index, dim) + other[: away.size].reshape(away.shape)
        return terms, parts + other[away.size :].reshape(parts.shape)

    def own_gains(self, terms):
        terms = terms.reshape(terms.shape[0], 2, 2, 2, -1)
        for index in self.place[2:]:
            terms = pick(terms, index, 1)
        return terms


class Plain:
    def __init__(self, team, group):
        self.team, self.group = team, group
        self.every = (team, group)
        self.size = lax.axis_size(team)
        self.index = lax.axis_index(team)

    def gather_rows(self, rows):
        return lax.all_gather(rows, self.team, axis=0, tiled=True)

    def scatter_rows(self, terms):
        return lax.psum_scatter(terms, self.team, scatter_dimension=0, tiled=True).astype(f32)

    def sum_rows(self, rows):
        return lax.psum(rows, self.team)

    def gather_columns(self, weight):
        rows = weight.shape[0]
        parts = weight.reshape(rows, self.size, -1).transpose(1, 0, 2)
        block = lax.all_to_all(parts, self.team, 0, 0)
        whole = lax.all_gather(block, self.group, axis=1, tiled=True)
        return whole.reshape(-1, block.shape[2])

    def scatter_columns(self, terms):
        terms = terms.reshape(self.size, -1, terms.shape[1])
        block = lax.psum_scatter(terms, self.group, scatter_dimension=1, tiled=True)
        parts = lax.all_to_all(block, self.team, 0, 0)
        return parts.transpose(1, 0, 2).reshape(parts.shape[1], -1).astype(f32)

    def gather_group(self, weight):
        return lax.all_gather(weight, self.group, axis=0, tiled=True)

    def scatter_group(self, terms, axis=0):
        block = lax.psum_scatter(terms, self.group, scatter_dimension=axis, tiled=True)
        return block.astype(f32)


def norm_columns(raw, columns):
    parts = [raw[:, k * columns : (k + 1) * columns] for k in (0, 1)]
    return jnp.stack([jnp.sum(part * part, axis=-1) for part in parts], axis=-1)


def raw_back(raw, scaled, inverse, means, grad_value):
    columns = grad_value.shape[1]
    grads = []
    for which in (0, 1):
        here = slice(which * columns, (which + 1) * columns)
        scale = inverse[:, which : which + 1]
        normed = raw[:, here] * scale
        grad = scale * (scaled[:, here] - normed * means[:, which : which + 1])
        grads.append(grad.astype(bf16))
    return jnp.concatenate(grads + [grad_value], axis=1)


def pair_kernel(first_y, second_y, first_x, second_x, first_w, second_w, left_ref, right_ref):
    def terms(first, second):
        first, second = (ref[...].reshape(-1, ref.shape[-1]) for ref in (first, second))
        total = product_tt(first, first_w[...]) + product_tt(second, second_w[...])
        return total.astype(bf16)

    step = pl.program_id(0)

    @pl.when(step < pl.num_programs(0) // 2)
    def _():
        left_ref[...] = terms(first_y, second_y)

    @pl.when(step >= pl.num_programs(0) // 2)
    def _():
        right_ref[...] = terms(first_x, second_x)


def pair_terms(place, first, second, first_whole, second_whole):
    rows, inner = first.shape
    width = first_whole.shape[0]
    quarter, tile = rows // 4, 256
    steps = width // tile
    along_y = pl.BlockSpec((1, 2, quarter, inner), lambda k: (place, 0, 0, 0))
    along_x = pl.BlockSpec((2, 1, quarter, inner), lambda k: (0, place, 0, 0))
    weight = pl.BlockSpec((tile, inner), lambda k: (k, 0))
    left = pl.BlockSpec((rows // 2, tile), lambda k: (0, jnp.minimum(k, steps // 2 - 1)))
    right = pl.BlockSpec((rows // 2, tile), lambda k: (0, jnp.maximum(k - steps // 2, 0)))
    first, second = (value.reshape(2, 2, quarter, inner) for value in (first, second))
    return pl.pallas_call(
        pair_kernel,
        grid=(steps,),
        in_specs=[along_y, along_y, along_x, along_x, weight, weight],
        out_specs=[left, right],
        out_shape=[jax.ShapeDtypeStruct((rows // 2, width // 2), bf16)] * 2,
        compiler_params=pltpu.CompilerParams(vmem_limit_bytes=40 * 2**20),
        cost_estimate=NO_COST,
    )(first, second, first, second, first_whole, second_whole)


def local_plain(
    plan,
    tokens,
    block_lengths,
    w_query,
    w_key,
    w_value,
    w_out,
    w_gate,
    w_up,
    w_down,
    query_gain,
    key_gain,
    attn_gain,
    mlp_gain,
    cotangent,
):
    width = tokens.shape[1]
    columns = width // plan.size
    live, _ = row_layout(block_lengths)
    live_col = live.astype(f32)[:, None]
    lengths = lax.all_gather(block_lengths, plan.team)
    _, position = jax.vmap(row_layout)(lengths)
    cosine, sine = angles(position)
    gains = jnp.stack([query_gain, key_gain, attn_gain, mlp_gain])
    gains = lax.all_gather(gains, plan.every, axis=1, tiled=True).astype(f32)
    part_gains = lax.dynamic_slice_in_dim(gains[:2], plan.index * columns, columns, axis=1)
    attn_gain_wide, mlp_gain_wide = gains[2], gains[3]
    attn_whole = jnp.concatenate(
        [plan.gather_columns(w) for w in (w_query, w_key, w_value)], axis=1
    )
    out_whole = plan.gather_group(w_out)
    gate_whole = plan.gather_columns(w_gate)
    up_whole = plan.gather_columns(w_up)
    down_whole = plan.gather_group(w_down)

    team_tokens = plan.gather_rows(tokens)
    raw = product(team_tokens, attn_whole)
    inverse = lax.rsqrt(plan.sum_rows(norm_columns(raw, columns)) / width + epsilon)
    turned, mixed_low = attend(lengths, raw, inverse, part_gains, cosine, sine)
    attn_proj = plan.scatter_rows(product(mixed_low, out_whole).astype(bf16))
    attn_normed, attn_inverse = norm_forward(attn_proj, attn_gain_wide)
    hidden = tokens.astype(f32) + attn_normed
    team_hidden = plan.gather_rows(hidden.astype(bf16))
    gate = product(team_hidden, gate_whole)
    upward = product(team_hidden, up_whole)
    sigmoid_gate = jax.nn.sigmoid(gate)
    activated = gate * sigmoid_gate
    inner_low = (activated * upward).astype(bf16)
    down = plan.scatter_rows(product(inner_low, down_whole).astype(bf16))
    down_normed, down_inverse = norm_forward(down, mlp_gain_wide)
    block_out = (live_col * (hidden + down_normed)).astype(bf16)

    grad_out = live_col * cotangent.astype(f32)
    grad_down, term_mlp_gain = norm_back(down, down_inverse, mlp_gain_wide, grad_out)
    team_grad_down = plan.gather_rows(grad_down.astype(bf16))
    grad_w_down = plan.scatter_group(inner_rows(inner_low, team_grad_down).astype(bf16))
    grad_inner = product_tt(team_grad_down, down_whole)
    grad_gate = grad_inner * upward * sigmoid_gate * (1.0 + gate * (1.0 - sigmoid_gate))
    grad_up = grad_inner * activated
    grad_gate, grad_up = grad_gate.astype(bf16), grad_up.astype(bf16)
    grad_w_gate = plan.scatter_columns(inner_rows(team_hidden, grad_gate).astype(bf16))
    grad_w_up = plan.scatter_columns(inner_rows(team_hidden, grad_up).astype(bf16))
    grad_from_mlp = product_tt(grad_gate, gate_whole) + product_tt(grad_up, up_whole)
    grad_hidden = grad_out + plan.scatter_rows(grad_from_mlp.astype(bf16))

    grad_proj, term_attn_gain = norm_back(attn_proj, attn_inverse, attn_gain_wide, grad_hidden)
    team_grad_proj = plan.gather_rows(grad_proj.astype(bf16))
    grad_mixed = product_tt(team_grad_proj, out_whole).astype(bf16)
    grad_w_out = plan.scatter_group(inner_rows(mixed_low, team_grad_proj).astype(bf16))
    scaled, grad_value, means, part_terms = attend_back(
        lengths, raw, turned, inverse, part_gains, cosine, sine, grad_mixed
    )
    means = plan.sum_rows(means) / width
    grad_raw = raw_back(raw, scaled, inverse, means, grad_value)
    grad_w_query, grad_w_key, grad_w_value = (
        plan.scatter_columns(
            inner_rows(team_tokens, grad_raw[:, k * columns : (k + 1) * columns]).astype(bf16)
        )
        for k in range(3)
    )
    grad_from_attn = plan.scatter_rows(product_tt(grad_raw, attn_whole).astype(bf16))
    part_grads = plan.scatter_group(part_terms, 1)
    gain_grads = lax.psum_scatter(
        jnp.stack([term_attn_gain, term_mlp_gain]), plan.every, scatter_dimension=1, tiled=True
    )
    return (
        block_out,
        (grad_hidden + grad_from_attn).astype(bf16),
        grad_w_query,
        grad_w_key,
        grad_w_value,
        grad_w_out,
        grad_w_gate,
        grad_w_up,
        grad_w_down,
        part_grads[0],
        part_grads[1],
        gain_grads[0],
        gain_grads[1],
    )


def local_cube(
    tokens,
    block_lengths,
    w_query,
    w_key,
    w_value,
    w_out,
    w_gate,
    w_up,
    w_down,
    query_gain,
    key_gain,
    attn_gain,
    mlp_gain,
    cotangent,
):
    plan = Cube()
    width = tokens.shape[1]
    columns = width // plan.size
    live, _ = row_layout(block_lengths)
    live_col = live.astype(f32)[:, None]

    def group_whole(block):
        return lax.all_gather(block, plan.group, axis=0, tiled=True)

    shard = query_gain.shape[0]
    small = plan.small_rows((query_gain, key_gain, attn_gain, mlp_gain), block_lengths, width)
    attn_parts = jnp.concatenate([plan.team_columns(w) for w in (w_query, w_key, w_value)], axis=2)
    attn_parts, own, out_rows, down0 = sync(attn_parts, tokens, w_out, w_down)
    packed = group_whole(jnp.concatenate([out_rows, small])).reshape(8, -1, width)
    down1 = plan.shift(down0)
    rows = plan.rows_first(plan.grouped(own))
    attn0 = plan.send_columns(attn_parts)
    attn0, w_gate, *rows = sync(attn0, w_gate, *rows)
    attn1, attn0c = plan.shift(attn0), swap(attn0, "c")
    rows = plan.rows_second(*rows)
    attn1, attn0c, down1, w_gate, *rows = sync(attn1, attn0c, down1, w_gate, *rows)
    gate = plan.send_columns(plan.team_columns(w_gate))
    attn2, attn1c = plan.shift(attn1), swap(attn1, "c")
    team_tokens = join(*rows)
    attn2, attn1c, gate, w_up, team_tokens, packed = sync(
        attn2, attn1c, gate, w_up, team_tokens, packed
    )
    gate_whole = group_whole(gate)
    up = plan.send_columns(plan.team_columns(w_up))
    attn3, attn2c = plan.shift(attn2), swap(attn2, "c")
    out_whole = packed[:, : w_out.shape[0]].reshape(-1, width)
    small = packed[:, w_out.shape[0] : w_out.shape[0] + 5, :shard].transpose(1, 0, 2)
    small = plan.small_step(plan.small_step(small, "x"), "y")
    attn3, attn2c, small, out_whole, up = sync(attn3, attn2c, small, out_whole, up)
    up_whole = group_whole(up)
    gains, lengths = plan.small_end(small, block_lengths.shape[0])
    _, position = jax.vmap(row_layout)(lengths)
    cosine, sine = angles(position)
    part_gains = lax.dynamic_slice_in_dim(gains[:2], plan.index * columns, columns, axis=1)
    attn_gain_wide, mlp_gain_wide = gains[2], gains[3]
    attn3c = swap(attn3, "c")
    attn_whole = plan.join_group([[attn0, attn1, attn2, attn3], [attn0c, attn1c, attn2c, attn3c]])

    raw = product(team_tokens, attn_whole)
    inverse = lax.rsqrt(plan.sum_rows(norm_columns(raw, columns)) / width + epsilon)
    turned, mixed_low = attend(lengths, raw, inverse, part_gains, cosine, sine)
    mixed_low, down1, team_tokens = sync(mixed_low, down1, team_tokens)
    down2, down0c, down1c = plan.shift(down1), swap(w_down, "c"), swap(down1, "c")
    half = width // 2

    def by_columns(rows, side, left, right):
        return product(rows(left), right[:, side * half : (side + 1) * half])

    def by_rows(rows, side, left, right):
        return product_tt(rows(left), right[side * half : (side + 1) * half])

    terms = plan.terms_first(by_columns, mixed_low, out_whole)
    terms = plan.terms_second(*terms)
    attn_proj = plan.terms_sum(*terms)
    attn_normed, attn_inverse = norm_forward(attn_proj, attn_gain_wide)
    hidden = tokens.astype(f32) + attn_normed

    rows = plan.rows_first(plan.grouped(hidden.astype(bf16)))
    rows = plan.rows_second(*rows)
    team_hidden = join(*rows)
    gate = product(team_hidden, gate_whole).astype(bf16)
    hidden_parts = plan.core_halves(team_hidden)
    gate, down2, *hidden_parts = sync(gate, down2, *hidden_parts)
    down3, down2c = plan.shift(down2), swap(down2, "c")
    upward = product(team_hidden, up_whole).astype(bf16)
    inner_low = (jax.nn.silu(gate.astype(f32)) * upward.astype(f32)).astype(bf16)
    inner_low, down3 = sync(inner_low, down3)
    down3c = swap(down3, "c")
    down_whole = plan.join_group([[w_down, down1, down2, down3], [down0c, down1c, down2c, down3c]])
    terms = plan.terms_first(by_columns, inner_low, down_whole)
    *inner_parts, left, right, left_y, right_x = sync(*plan.core_halves(inner_low), *terms)
    down = plan.terms_sum(*plan.terms_second(left, right, left_y, right_x))
    down_normed, down_inverse = norm_forward(down, mlp_gain_wide)
    block_out = (live_col * (hidden + down_normed)).astype(bf16)

    grad_out = live_col * cotangent.astype(f32)
    grad_down, term_mlp_gain = norm_back(down, down_inverse, mlp_gain_wide, grad_out)
    rows = plan.rows_second(*plan.rows_first(grad_down.astype(bf16)))
    team_grad_down = join(*rows)

    def terms_of(left, right):
        return inner_rows(left, right).astype(bf16)

    def summed(mine, other):
        return (mine.astype(f32) + other.astype(f32)).astype(bf16)

    down_other = swap(terms_of(inner_parts[0], team_grad_down), "c")
    down_mine = terms_of(inner_parts[1], team_grad_down)
    team_grad_down, down_mine, down_other = sync(team_grad_down, down_mine, down_other)
    down_terms = summed(down_mine, down_other)
    gain_shape = (2, 2, 2, 2, 2, -1)
    team_grad_down, down_terms, mlp_terms = sync(team_grad_down, down_terms, term_mlp_gain)
    mlp_terms = plan.gain_step(mlp_terms.reshape(gain_shape), "c", 2)
    team_grad_down, mlp_terms = sync(team_grad_down, mlp_terms)
    grad_w_down = lax.psum_scatter(down_terms, plan.z_axes, scatter_dimension=0, tiled=True)
    grad_inner = product_tt(team_grad_down, down_whole)
    gate_wide = gate.astype(f32)
    sigmoid_gate = jax.nn.sigmoid(gate_wide)
    slope = sigmoid_gate * (1.0 + gate_wide * (1.0 - sigmoid_gate))
    grad_gate = grad_inner * upward.astype(f32) * slope
    grad_up = grad_inner * (gate_wide * sigmoid_gate)
    grad_gate, grad_up, *hidden_parts = sync(
        grad_gate.astype(bf16), grad_up.astype(bf16), *hidden_parts
    )
    gate_away = terms_of(hidden_parts[0], grad_gate)
    gate_away, grad_up, other_part = sync(gate_away, grad_up, hidden_parts[0])
    gate_other = swap(gate_away, "c")
    up_away = terms_of(other_part, grad_up)
    up_away, grad_gate, grad_up = sync(up_away, grad_gate, grad_up)
    up_other = swap(up_away, "c")
    hidden_part = hidden_parts[1]

    left_away, right_away = pair_terms(1, grad_gate, grad_up, gate_whole, up_whole)
    left_away, right_away, grad_gate, grad_up, hidden_part, own_tokens, own_mixed = sync(
        left_away, right_away, grad_gate, grad_up, hidden_part, team_tokens, mixed_low
    )
    left_y, right_x = swap(left_away, "y"), swap(right_away, "x")
    left, right = pair_terms(0, grad_gate, grad_up, gate_whole, up_whole)
    terms = left, right, left_y, right_x
    gate_terms = summed(terms_of(hidden_part, grad_gate), gate_other)
    late_parts = (*plan.core_halves(own_tokens), *plan.core_halves(own_mixed))
    gate_terms, grad_up, token_other, token_mine, mixed_other, mixed_mine, *terms = sync(
        gate_terms, grad_up, *late_parts, *terms
    )
    gate_block = lax.psum_scatter(gate_terms, plan.z_axes, scatter_dimension=0, tiled=True)
    terms = plan.terms_second(*terms)
    grad_up, *terms = sync(grad_up, *terms)

    grad_hidden, grad_proj, term_attn_gain = proj_back(
        plan.own_order, terms, live_col, cotangent, attn_proj, attn_inverse, attn_gain_wide
    )
    rows = plan.rows_first(grad_proj)
    up_mine = terms_of(hidden_part, grad_up)
    up_mine, up_other, grad_w_down, *rows = sync(up_mine, up_other, grad_w_down, *rows)
    rows = plan.rows_second(*rows)
    up_terms = summed(up_mine, up_other)
    up_terms, *rows = sync(up_terms, *rows)
    up_block = lax.psum_scatter(up_terms, plan.z_axes, scatter_dimension=0, tiled=True)
    team_grad_proj = join(*rows)
    grad_mixed = product_tt(team_grad_proj, out_whole).astype(bf16)
    grad_mixed, gate_block = sync(grad_mixed, gate_block)
    scaled, grad_value, means, part_terms = attend_back(
        lengths, raw, turned, inverse, part_gains, cosine, sine, grad_mixed
    )
    attn_gain_terms = plan.gain_step(term_attn_gain.reshape(gain_shape), "c", 2)
    gain_terms = jnp.stack([attn_gain_terms, mlp_terms])
    gate_block = plan.return_columns(gate_block)
    means, part_terms, gain_terms, team_grad_proj, gate_block = sync(
        means, part_terms, gain_terms, team_grad_proj, gate_block
    )
    out_away = terms_of(mixed_other, team_grad_proj)
    means = plan.sum_along(means, "y")
    means, out_away, team_grad_proj = sync(means, out_away, team_grad_proj)
    out_mine = terms_of(mixed_mine, team_grad_proj)
    means = plan.sum_along(means, "x") / width
    means, out_mine = sync(means, out_mine)
    grad_raw = raw_back(raw, scaled, inverse, means, grad_value)
    part = token_other.shape[1] // 2
    attn_other = [swap(terms_of(token_other[:, :part], grad_raw), "c")]
    attn_other += [swap(terms_of(token_other[:, part:], grad_raw), "c")]
    out_other = swap(out_away, "c")
    attn_mine = terms_of(token_mine, grad_raw)
    part_terms = part_terms + swap(part_terms, "c")
    grad_raw, attn_mine, out_mine, out_other, part_terms, gain_terms, *attn_other = sync(
        grad_raw, attn_mine, out_mine, out_other, part_terms, gain_terms, *attn_other
    )
    attn_terms, out_terms = (attn_mine, tuple(attn_other)), (out_mine, out_other)
    attn_sum, out_sum = plan.ring_step(1, attn_terms), plan.ring_step(1, out_terms)
    terms = plan.terms_first(by_rows, grad_raw, attn_whole)
    gain_terms, part_terms = plan.both_step(gain_terms, part_terms, "zh", 3)
    attn_sum, out_sum, part_terms, gain_terms, *terms = sync(
        attn_sum, out_sum, part_terms, gain_terms, *terms
    )
    attn_sum = plan.ring_sum(2, attn_terms, attn_sum).astype(bf16)
    out_sum = plan.ring_sum(2, out_terms, out_sum).astype(bf16)
    attn_sum, out_sum, part_terms, gain_terms, *terms = sync(
        attn_sum, out_sum, part_terms, gain_terms, *terms
    )
    attn_sum, out_sum = plan.shift(attn_sum), plan.shift(out_sum)
    gain_terms, part_terms = plan.both_step(gain_terms, part_terms, "zl", 3)
    up_block = plan.return_columns(up_block)
    terms = plan.terms_added(*terms)
    attn_sum, out_sum, gain_terms, part_terms, up_block, *terms = sync(
        attn_sum, out_sum, gain_terms, part_terms, up_block, *terms
    )
    attn_sum = plan.ring_sum(3, attn_terms, attn_sum).astype(bf16)
    out_sum = plan.ring_sum(3, out_terms, out_sum).astype(bf16)
    attn_sum, out_sum, gate_block, up_block, *sides, left_away, right_away = sync(
        attn_sum, out_sum, gate_block, up_block, *terms
    )
    attn_sum, out_sum = plan.shift(attn_sum), plan.shift(out_sum)
    left_x, right_y = swap(left_away, "x"), swap(right_away, "y")
    grad_w_gate, grad_w_up = plan.whole_columns(gate_block), plan.whole_columns(up_block)
    gain_terms = plan.gain_step(gain_terms, "x", 2)
    part_grads = plan.own_gains(part_terms)
    attn_sum, out_sum, gain_terms, part_grads, grad_w_gate, grad_w_up, left_x, right_y = sync(
        attn_sum, out_sum, gain_terms, part_grads, grad_w_gate, grad_w_up, left_x, right_y
    )
    attn_sum = plan.ring_sum(0, attn_terms, attn_sum).astype(bf16)
    attn_sum, out_sum, gain_terms, left_x, right_y = sync(
        attn_sum, out_sum, gain_terms, left_x, right_y
    )
    grad_tokens = tokens_end(plan.own_order, (*sides, left_x, right_y), grad_hidden)
    attn_block = plan.return_columns(attn_sum)
    gain_terms = plan.gain_step(gain_terms, "y", 1)
    grad_w_out = plan.ring_sum(0, out_terms, out_sum)
    attn_block, grad_w_out, gain_terms, grad_tokens = sync(
        attn_block, grad_w_out, gain_terms, grad_tokens
    )
    grad_w_query, grad_w_key, grad_w_value = spread_three(attn_block)
    return (
        block_out,
        grad_tokens,
        grad_w_query,
        grad_w_key,
        grad_w_value,
        grad_w_out,
        grad_w_gate,
        grad_w_up,
        grad_w_down.astype(f32),
        part_grads[0],
        part_grads[1],
        gain_terms[0],
        gain_terms[1],
    )


def solution(mesh):
    if tuple(mesh.shape.values()) == (8, 4):
        mesh = Mesh(mesh.devices.reshape(2, 2, 2, 2, 2), Cube.every)
        every, step = Cube.every, local_cube
    else:
        every = tuple(mesh.axis_names)

        def step(*arrays):
            return local_plain(Plain(*every), *arrays)

    rows, line = P(every, None), P(every)
    return jax.shard_map(
        step,
        mesh=mesh,
        in_specs=(rows, line) + (rows,) * 7 + (line,) * 4 + (rows,),
        out_specs=(rows,) * 9 + (line,) * 4,
        check_vma=False,
    )
```
